32 devices in a mesh: row: 4 (over y, core), col: 8 (over z, x).
Axes of the slice: x: 2, y: 2, z: 4, core: 2. Of those that a mesh axis runs over, the one named last changes fastest.
Arguments:
- source: bfloat16 [8192, 512], P('row'), may hold values from -16 to 16
- target: bfloat16 [4096, 512], P('col'), may hold values from -6 to 6
- log_source_mass: float32 [8192], P('row'), may hold values from -1.5 to 1.5
- log_target_mass: float32 [4096], P('col'), may hold values from -1.5 to 1.5
Outputs:
- source_image: float32 [8192, 512], P(('row', 'col'))
- target_image: float32 [4096, 512], P('col')
The draws below stay inside these ranges and needn't reach their ends.
All inputs are finite; a program needn't handle non-finite values.
Results may differ from the reference program's by a relative error of at most 0.0055.
Values sent between devices are 32-bit elements; how exact they have to be, the bound alone decides.
No kernel may reach another device: no remote copies, remote signals or barrier semaphores. Data moves between devices by JAX's collectives and lax.ppermute only.
A program may use at most 64 MiB of HBM per device.

```python
import jax
import jax.numpy as jnp
from jax import lax

D = 512
S_DEV = 2048
ITERS = 2
NS = 8192
NT = 4096
N_ROW = 4


def draw_source(key, part):
    key = jax.random.fold_in(key, 11)
    first = jax.random.fold_in(key, 0)
    base = jax.random.normal(first, (NS, D), jnp.float32)
    return jnp.clip(base, -16.0, 16.0).astype(jnp.bfloat16)


def block_levels(stream_key, shape, shards, least, high):
    gain, own = 1.0, jax.random.fold_in(stream_key, 6)
    for dim, blocks in shards:
        heights = jnp.exp(jax.random.uniform(jax.random.fold_in(own, dim), (blocks,), jnp.float32, least / len(shards), high / len(shards)))
        gain = gain * jnp.repeat(heights, shape[dim] // blocks).reshape([-1 if axis == dim else 1 for axis in range(len(shape))])
    return gain


def bell_draw(key, dims, deviation, most, shards=(), held_as=jnp.bfloat16):
    entries = jax.random.normal(key, dims, jnp.float32) * deviation
    if len(shards) > 0:
        entries = block_levels(key, dims, shards, -0.22, 0.18) * entries
    return jnp.clip(entries, min=-most, max=most).astype(held_as)


def setup_inputs(seed: int = 0) -> dict:
    key_list = jax.random.split(jax.random.key(seed), 5)
    source = draw_source(jax.random.fold_in(key_list[4], 71), 0)
    target = bell_draw(key_list[1], (NT, D), 1.0, 6.0, ((0, 8),))
    log_source_mass = jnp.clip(jax.random.uniform(key_list[2], (NS,), jnp.float32, -1.5, 1.5) * block_levels(key_list[2], (NS,), ((0, 4),), -0.4, 0.0), -1.5, 1.5)
    log_target_mass = jnp.clip(jax.random.uniform(key_list[3], (NT,), jnp.float32, -1.5, 1.5) * block_levels(key_list[3], (NT,), ((0, 8),), -0.4, 0.0), -1.5, 1.5)
    return dict(source=source, target=target, log_source_mass=log_source_mass, log_target_mass=log_target_mass)


blur = 0.1


def block_cost(xb, sqx, yall, sqy):
    inner = jnp.dot(xb.astype(jnp.float32), yall.astype(jnp.float32).T, precision=lax.Precision.HIGHEST)
    return (sqx[:, None] + sqy[None, :] - 2.0 * inner) / D


def reference(source, target, log_source_mass, log_target_mass):
    sqx_all = jnp.sum(source.astype(jnp.float32) ** 2, axis=1)
    sqy = jnp.sum(target.astype(jnp.float32) ** 2, axis=1)
    xs = source.reshape(N_ROW, S_DEV, D)
    sqxs = sqx_all.reshape(N_ROW, S_DEV)
    las = log_source_mass.reshape(N_ROW, S_DEV)
    g = jnp.zeros((NT,), jnp.float32)
    f = jnp.zeros((NS,), jnp.float32)
    for step in range(ITERS):
        def row_pass(item):
            xb, sqb = item
            scores = log_target_mass[None, :] + (g[None, :] - block_cost(xb, sqb, target, sqy)) / blur
            peak = jnp.max(scores, axis=1)
            return -blur * (peak + jnp.log(jnp.sum(jnp.exp(scores - peak[:, None]), axis=1)))
        f = lax.map(row_pass, (xs, sqxs)).reshape(NS)
        fs = f.reshape(N_ROW, S_DEV)

        def col_pass(carry, item):
            peak, total = carry
            xb, sqb, fb, lab = item
            scores = lab[:, None] + (fb[:, None] - block_cost(xb, sqb, target, sqy)) / blur
            local = jnp.max(scores, axis=0)
            top = jnp.maximum(peak, local)
            total = total * jnp.exp(peak - top) + jnp.sum(jnp.exp(scores - top[None, :]), axis=0)
            return (top, total), None
        init = (jnp.full((NT,), -jnp.inf, jnp.float32), jnp.zeros((NT,), jnp.float32))
        (peak, total), unused = lax.scan(col_pass, init, (xs, sqxs, fs, las))
        g = -blur * (peak + jnp.log(total))
    fs = f.reshape(N_ROW, S_DEV)

    def final_pass(carry, item):
        numer, denom = carry
        xb, sqb, fb, lab = item
        plan = jnp.exp(lab[:, None] + log_target_mass[None, :] + (fb[:, None] + g[None, :] - block_cost(xb, sqb, target, sqy)) / blur)
        weights = plan.astype(jnp.bfloat16).astype(jnp.float32)
        src = jnp.dot(weights, target.astype(jnp.float32), precision=lax.Precision.HIGHEST) / jnp.sum(plan, axis=1)[:, None]
        numer = numer + jnp.dot(weights.T, xb.astype(jnp.float32), precision=lax.Precision.HIGHEST)
        denom = denom + jnp.sum(plan, axis=0)
        return (numer, denom), src
    init = (jnp.zeros((NT, D), jnp.float32), jnp.zeros((NT,), jnp.float32))
    (numer, denom), src = lax.scan(final_pass, init, (xs, sqxs, fs, las))
    return src.reshape(NS, D), numer / denom[:, None]
```

```python
import math

import jax
import jax.numpy as jnp
from jax import lax
from jax.experimental import pallas as pl
from jax.experimental.pallas import tpu as pltpu
from jax.sharding import PartitionSpec as P

ITERS = 2
BLUR = 0.1
LOG2E = math.log2(math.e)
LANES = 128
NT_DIMS = (((1,), (1,)), ((), ()))
VMEM = pl.BlockSpec(memory_space=pltpu.VMEM)
HBM = pl.BlockSpec(memory_space=pltpu.HBM)
ANY = pl.BlockSpec(memory_space=pl.ANY)
DMA = pltpu.SemaphoreType.DMA


def call(kernel, out_shape, *args, in_specs=None, out_specs=None, scratch=(), limit=40):
    return pl.pallas_call(
        kernel,
        out_shape=out_shape,
        in_specs=in_specs or [VMEM] * len(args),
        out_specs=out_specs or jax.tree.map(lambda _: VMEM, out_shape),
        scratch_shapes=list(scratch),
        compiler_params=pltpu.CompilerParams(vmem_limit_bytes=limit << 20),
    )(*args)


def f32(*shape):
    return jax.ShapeDtypeStruct(shape, jnp.float32)


def bf16(*shape):
    return jax.ShapeDtypeStruct(shape, jnp.bfloat16)


def scale(width):
    return LOG2E / (width * BLUR)


def to_column(dense):
    n = dense.shape[0]
    square = jnp.concatenate([dense, jnp.zeros((LANES - n, LANES), jnp.float32)], axis=0).T
    return jnp.concatenate([square[:, b : b + 1] for b in range(n)], axis=0)


def to_dense(columns):
    lane = lax.broadcasted_iota(jnp.int32, (LANES, LANES), 1)
    square = jnp.zeros((LANES, LANES), jnp.float32)
    for b, column in enumerate(columns):
        square = jnp.where(lane == b, column, square)
    return square.T[: len(columns)]


def to_row(dense):
    return jnp.concatenate([dense[b : b + 1, :] for b in range(dense.shape[0])], axis=1)


def over_targets(scores):
    peak = jnp.max(scores, axis=0, keepdims=True)
    total = jnp.sum(jnp.exp2(scores - peak), axis=0, keepdims=True)
    return peak + jnp.log2(total)


def half_at(ref, place):
    half = ref.shape[0] // 2
    return ref[pl.ds(place * half, half), :]


def merge_all(parts):
    peak = parts[0]
    for part in parts[1:]:
        peak = jnp.maximum(peak, part)
    return peak + jnp.log2(sum(jnp.exp2(part - peak) for part in parts))


def norms(block):
    wide = block.astype(jnp.float32)
    return jnp.sum(wide * wide, axis=1, keepdims=True) * scale(block.shape[1])


def half_kernel(y_hbm, out_ref, held, sem):
    half = out_ref.shape[0]
    core = lax.axis_index("row") % 2
    copy = pltpu.make_async_copy(y_hbm.at[pl.ds(core * half, half), :], held, sem)
    copy.start()
    copy.wait()
    out_ref[...] = held[...].astype(jnp.float32)


def first_kernel(y_hbm, x_hbm, tile_ref, sqx_ref, sqy_ref, y_ref, x_ref, x_sems, y_sem):
    wide = 256
    blocks = [pl.ds(b * wide, wide) for b in range(x_hbm.shape[0] // wide)]
    y_copy = pltpu.make_async_copy(y_hbm, y_ref, y_sem)
    x_copies = [pltpu.make_async_copy(x_hbm.at[at, :], x_ref.at[at, :], x_sems.at[b]) for b, at in enumerate(blocks)]
    for copy in (y_copy, *x_copies):
        copy.start()
    y_copy.wait()
    y = y_ref[...]
    unit = scale(y.shape[1])
    sqy_ref[...] = to_dense([norms(y[b : b + LANES]) for b in range(0, y.shape[0], LANES)])
    columns = []
    for b, at in enumerate(blocks):
        x_copies[b].wait()
        x = x_ref[at, :]
        tile_ref[:, at] = lax.dot_general(y, x, NT_DIMS, preferred_element_type=jnp.float32) * (2.0 * unit)
        columns += [norms(x[c : c + LANES]) for c in range(0, wide, LANES)]
    sqx_ref[...] = to_dense(columns)


def targets_kernel(tile_ref, lt_ref, sqy_ref, total_ref, lse_ref):
    g_pot = sqy_ref[...] - total_ref[...]
    bias = to_column(lt_ref[...] * LOG2E + g_pot - sqy_ref[...])
    for b in range(tile_ref.shape[1] // LANES):
        row = over_targets(tile_ref[:, pl.ds(b * LANES, LANES)] + bias)
        for k in range(lse_ref.shape[0]):
            lse_ref[k, pl.ds(b, 1), :] = row


def sources_kernel(tile_ref, ls_ref, sqx_ref, parts_ref, bias_ref, lse_ref):
    f_pot = sqx_ref[...] - merge_all([parts_ref[k] for k in range(parts_ref.shape[0])])
    bias = ls_ref[...] * LOG2E + f_pot - sqx_ref[...]
    bias_ref[...] = bias
    blocks = range(bias.shape[0])
    columns = []
    for j in range(tile_ref.shape[0] // LANES):
        at = pl.ds(j * LANES, LANES)
        scores = [tile_ref[at, pl.ds(b * LANES, LANES)] + bias[b : b + 1, :] for b in blocks]
        top = scores[0]
        for block in scores[1:]:
            top = jnp.maximum(top, block)
        peak = jnp.max(top, axis=1, keepdims=True)
        total = jnp.sum(sum(jnp.exp2(block - peak) for block in scores), axis=1, keepdims=True)
        columns.append(peak + jnp.log2(total))
    lse_ref[...] = to_dense(columns)


def means_kernel(tile_ref, x_ref, bias_ref, total_ref, *refs):
    bias_refs, (sent_ref, mine_ref, biases_ref) = refs[:-3], refs[-3:]
    for k, ref in enumerate(bias_refs):
        biases_ref[k] = ref[...]
    bias = bias_ref[...]
    x = x_ref[...]
    half = mine_ref.shape[0]
    n_rows = half // LANES
    core = lax.axis_index("row") % 2
    for out_ref, place in ((sent_ref, 1 - core), (mine_ref, core)):
        total = to_column(total_ref[pl.ds(place * n_rows, n_rows), :])
        for j in range(n_rows):
            at = pl.ds(pl.multiple_of(place * half + j * LANES, LANES), LANES)
            norm = total[j * LANES : (j + 1) * LANES]
            exps = [
                jnp.exp2(tile_ref[at, pl.ds(b * LANES, LANES)] + bias[b : b + 1, :] - norm)
                for b in range(bias.shape[0])
            ]
            weights = jnp.concatenate([block.astype(jnp.bfloat16) for block in exps], axis=1)
            out_ref[pl.ds(j * LANES, LANES), :] = jnp.dot(weights, x, preferred_element_type=jnp.float32)


def pack_kernel(parts_hbm, total_ref, out_ref, sem):
    copy = pltpu.make_async_copy(parts_hbm, out_ref, sem)
    copy.start()
    copy.wait()


def add_kernel(one_ref, two_ref, *refs):
    refs[-1][...] = one_ref[...] + two_ref[...]


def join_kernel(n_parts, *refs):
    means, lses, out_ref = refs[:n_parts], refs[n_parts:-1], refs[-1]
    rows = out_ref.shape[0]
    total = merge_all([ref[...] for ref in lses])
    shares = [to_column(jnp.exp2(ref[...] - total))[:rows] for ref in lses]
    out_ref[...] = sum(ref[...] * share for ref, share in zip(means, shares))


def place_kernel(mine_ref, other_ref, out_hbm, sems):
    half = mine_ref.shape[0]
    core = lax.axis_index("row") % 2
    mine = pltpu.make_async_copy(mine_ref, out_hbm.at[pl.ds(core * half, half), :], sems.at[0])
    other = pltpu.make_async_copy(other_ref, out_hbm.at[pl.ds((1 - core) * half, half), :], sems.at[1])
    mine.start()
    other.start()
    mine.wait()
    other.wait()


def images(flip, n_x, x_ref, y_ref, biases_ref, mean_ref, lse_ref, scores_ref):
    rows = mean_ref.shape[0]
    n_shards = biases_ref.shape[0]
    n_tgt = y_ref.shape[0] // n_shards
    col = lax.axis_index("col")
    own = x_ref[pl.ds(pl.multiple_of((col ^ flip) * rows, rows), rows), :]
    unit = scale(own.shape[1])
    peak = jnp.full((rows, 1), -jnp.inf, jnp.float32)
    for k in range(n_shards):
        at = pl.ds(k * n_tgt, n_tgt)
        inner = lax.dot_general(own, y_ref[at, :], NT_DIMS, preferred_element_type=jnp.float32)
        scores = inner * (2.0 * unit) + to_row(biases_ref[k])
        scores_ref[:, at] = scores
        peak = jnp.maximum(peak, jnp.max(scores, axis=1, keepdims=True))
    total = jnp.zeros((rows, 1), jnp.float32)
    numer = jnp.zeros((rows, own.shape[1]), jnp.float32)
    for k in range(n_shards):
        at = pl.ds(k * n_tgt, n_tgt)
        plan = jnp.exp2(scores_ref[:, at] - peak)
        total = total + jnp.sum(plan, axis=1, keepdims=True)
        numer = numer + jnp.dot(plan.astype(jnp.bfloat16), y_ref[at, :], preferred_element_type=jnp.float32)
    mean_ref[...] = numer * (1.0 / total)
    lse = peak + jnp.log2(total)
    if rows % LANES:
        lse = jnp.concatenate([lse, jnp.zeros((-rows % LANES, 1), jnp.float32)], axis=0)
    lse_ref[...] = to_dense([lse[b * LANES : (b + 1) * LANES] for b in range(lse.shape[0] // LANES)])


def others_kernel(n_x, x_ref, mine_ref, other_ref, biases_ref, *refs):
    n_z, half, _ = mine_ref.shape
    y_ref, scores_ref = refs[0], refs[-1]
    core = lax.axis_index("row") % 2
    z = lax.axis_index("col") // n_x
    for k in range(n_z):
        for ref, place in ((mine_ref, core), (other_ref, 1 - core)):
            at = pl.ds(pl.multiple_of((2 * k + place) * half, half), half)
            y_ref[at, :] = ref[z ^ k].astype(jnp.bfloat16)
    for flip in range(1, n_x):
        images(flip, n_x, x_ref, y_ref, biases_ref, refs[2 * flip - 1], refs[2 * flip], scores_ref)


def own_kernel(n_x, x_ref, y_ref, biases_ref, mean_ref, lse_ref, scores_ref):
    images(0, n_x, x_ref, y_ref, biases_ref, mean_ref, lse_ref, scores_ref)


def swap(value, axis, distance):
    n = lax.axis_size(axis)
    return lax.ppermute(value, axis, [(i, i ^ distance) for i in range(n)])


def bits_of(n):
    return [1 << b for b in range(n.bit_length() - 1)]


def on_device(source, target, log_source_mass, log_target_mass):
    n_src, width = source.shape
    n_tgt = target.shape[0]
    n_col, n_row = lax.axis_size("col"), lax.axis_size("row")
    count = n_src // n_col
    n_x = 1 << (len(bits_of(n_col)) // 2)
    n_z = n_col // n_x
    along_z = [[z * n_x + x for z in range(n_z)] for x in range(n_x)]
    ls = log_source_mass.reshape(-1, LANES)
    lt = log_target_mass.reshape(-1, LANES)
    src_dense, tgt_dense = f32(*ls.shape), f32(*lt.shape)
    half = n_tgt // 2

    own_half = call(
        half_kernel, f32(half, width), target,
        in_specs=[ANY], scratch=[pltpu.VMEM((half, width), target.dtype), DMA], limit=58,
    )
    gathered = lax.all_gather(own_half, "col", axis_index_groups=along_z)

    tile, sqx, sqy = call(
        first_kernel,
        (f32(n_tgt, n_src), src_dense, tgt_dense),
        target, source,
        in_specs=[ANY] * 2,
        scratch=[
            pltpu.VMEM(target.shape, target.dtype), pltpu.VMEM(source.shape, source.dtype), DMA((n_src // 256,)), DMA
        ],
        limit=58,
    )

    def iteration(step, carry):
        total, _ = carry
        copies = call(targets_kernel, f32(n_col, *ls.shape), tile, lt, sqy, total)
        parts = lax.all_to_all(copies, "col", 0, 0)
        bias, lse = call(sources_kernel, (src_dense, tgt_dense), tile, ls, sqx, parts)
        return merge_all([lse] + [swap(lse, "row", k) for k in range(1, n_row)]), bias

    total, src_bias = lax.fori_loop(0, ITERS, iteration, (sqy, sqx))

    gathered = call(
        pack_kernel, f32(*gathered.shape), gathered, total, in_specs=[ANY, VMEM], scratch=[DMA], limit=58
    )
    bias = lt * LOG2E + (sqy - total) - sqy
    biases = [bias] + [swap(bias, "col", k * n_x) for k in range(1, n_z)]

    sent, mine, biases = call(
        means_kernel,
        (f32(half, width), f32(half, width), f32(n_z, *lt.shape)),
        tile, source, src_bias, total, *biases,
    )
    mine = call(add_kernel, f32(half, width), mine, swap(sent, "row", 1))
    rest = bits_of(n_row)[1:]
    for distance in rest[:-1]:
        mine = call(add_kernel, f32(half, width), mine, swap(mine, "row", distance))
    came = swap(mine, "row", rest[-1])

    scores = pltpu.VMEM((count, n_z * n_tgt), jnp.float32)
    image = [f32(count, width), f32(pl.cdiv(count, LANES), LANES)]
    all_y, *others = call(
        lambda *refs: others_kernel(n_x, *refs),
        (bf16(n_z * n_tgt, width), *image * (n_x - 1)),
        source, gathered, swap(gathered, "row", 1), biases,
        scratch=[scores],
    )
    joined = [swap(part, "col", 1 + k // 2) for k, part in enumerate(others)]
    own, own_lse = call(
        lambda *refs: own_kernel(n_x, *refs), tuple(image), source, all_y, biases, scratch=[scores]
    )
    mine = call(add_kernel, f32(half, width), mine, came, own_lse)
    target_image = call(
        place_kernel, f32(n_tgt, width), mine, swap(mine, "row", 1), out_specs=HBM, scratch=[DMA((2,))]
    )
    source_image = call(
        lambda *refs: join_kernel(n_x, *refs), f32(count, width), own, *joined[::2], own_lse, *joined[1::2]
    )
    return source_image, target_image


def solution(mesh):
    in_specs = (P("row", None), P("col", None), P("row"), P("col"))
    out_specs = (P(("row", "col"), None), P("col", None))
    return jax.shard_map(
        on_device, mesh=mesh, in_specs=in_specs, out_specs=out_specs, check_vma=False
    )
```

```python
import math

import jax
import jax.numpy as jnp
from jax import lax
from jax.experimental import pallas as pl
from jax.experimental.pallas import tpu as pltpu
from jax.sharding import PartitionSpec as P

ITERS = 2
BLUR = 0.1
LOG2E = math.log2(math.e)
LANES = 128
NT_DIMS = (((1,), (1,)), ((), ()))
VMEM = pl.BlockSpec(memory_space=pltpu.VMEM)
HBM = pl.BlockSpec(memory_space=pltpu.HBM)
ANY = pl.BlockSpec(memory_space=pl.ANY)
DMA = pltpu.SemaphoreType.DMA


def call(kernel, out_shape, *args, in_specs=None, out_specs=None, scratch=(), limit=24):
    return pl.pallas_call(
        kernel,
        out_shape=out_shape,
        in_specs=in_specs or [VMEM] * len(args),
        out_specs=out_specs or jax.tree.map(lambda _: VMEM, out_shape),
        scratch_shapes=list(scratch),
        compiler_params=pltpu.CompilerParams(vmem_limit_bytes=limit << 20),
    )(*args)


def f32(*shape):
    return jax.ShapeDtypeStruct(shape, jnp.float32)


def bf16(*shape):
    return jax.ShapeDtypeStruct(shape, jnp.bfloat16)


def scale(width):
    return LOG2E / (width * BLUR)


def to_column(dense):
    n = dense.shape[0]
    square = jnp.concatenate([dense, jnp.zeros((LANES - n, LANES), jnp.float32)], axis=0).T
    return jnp.concatenate([square[:, b : b + 1] for b in range(n)], axis=0)


def to_dense(columns):
    lane = lax.broadcasted_iota(jnp.int32, (LANES, LANES), 1)
    square = jnp.zeros((LANES, LANES), jnp.float32)
    for b, column in enumerate(columns):
        square = jnp.where(lane == b, column, square)
    return square.T[: len(columns)]


def to_row(dense):
    return jnp.concatenate([dense[b : b + 1, :] for b in range(dense.shape[0])], axis=1)


def over_targets(scores):
    peak = jnp.max(scores, axis=0, keepdims=True)
    total = jnp.sum(jnp.exp2(scores - peak), axis=0, keepdims=True)
    return peak + jnp.log2(total)


def half_at(ref, place):
    half = ref.shape[0] // 2
    return ref[pl.ds(place * half, half), :]


def merge_all(parts):
    peak = parts[0]
    for part in parts[1:]:
        peak = jnp.maximum(peak, part)
    return peak + jnp.log2(sum(jnp.exp2(part - peak) for part in parts))


def norms(block):
    wide = block.astype(jnp.float32)
    return jnp.sum(wide * wide, axis=1, keepdims=True) * scale(block.shape[1])


def half_kernel(y_ref, *out_refs):
    part = out_refs[0].shape[0]
    start = lax.axis_index("row") % 2 * part * len(out_refs)
    for k, ref in enumerate(out_refs):
        ref[...] = y_ref[pl.ds(pl.multiple_of(start + k * part, part), part), :].astype(jnp.float32)


def first_kernel(y_ref, x_ref, lt_ref, tile_ref, lse_ref, sqx_ref, sqy_ref):
    wide = 256
    y = y_ref[...]
    unit = scale(y.shape[1])
    sqy = norms(y)
    sqy_ref[...] = to_dense([sqy[b : b + LANES] for b in range(0, y.shape[0], LANES)])
    bias = to_column(lt_ref[...]) * LOG2E - sqy
    columns = []
    for b in range(x_ref.shape[0] // wide):
        at = pl.ds(b * wide, wide)
        x = x_ref[at, :]
        tile = lax.dot_general(y, x, NT_DIMS, preferred_element_type=jnp.float32) * (2.0 * unit)
        tile_ref[:, at] = tile
        row = over_targets(tile + bias)
        for c in range(wide // LANES):
            lse_ref[pl.ds(b * (wide // LANES) + c, 1), :] = row[:, c * LANES : (c + 1) * LANES]
        columns += [norms(x[c : c + LANES]) for c in range(0, wide, LANES)]
    sqx_ref[...] = to_dense(columns)


def targets_kernel(tile_ref, lt_ref, sqy_ref, *refs):
    parts, lse_ref = refs[:-1], refs[-1]
    g_pot = sqy_ref[...] - merge_all([ref[...] for ref in parts])
    bias = to_column(lt_ref[...] * LOG2E + g_pot - sqy_ref[...])
    for b in range(tile_ref.shape[1] // LANES):
        lse_ref[pl.ds(b, 1), :] = over_targets(tile_ref[:, pl.ds(b * LANES, LANES)] + bias)


def sources_kernel(tile_ref, ls_ref, sqx_ref, *refs):
    parts, (bias_ref, lse_ref) = refs[:-2], refs[-2:]
    f_pot = sqx_ref[...] - merge_all([ref[...] for ref in parts])
    bias = ls_ref[...] * LOG2E + f_pot - sqx_ref[...]
    bias_ref[...] = bias
    blocks = range(bias.shape[0])
    columns = []
    for j in range(tile_ref.shape[0] // LANES):
        at = pl.ds(j * LANES, LANES)
        scores = [tile_ref[at, pl.ds(b * LANES, LANES)] + bias[b : b + 1, :] for b in blocks]
        top = scores[0]
        for block in scores[1:]:
            top = jnp.maximum(top, block)
        peak = jnp.max(top, axis=1, keepdims=True)
        total = jnp.sum(sum(jnp.exp2(block - peak) for block in scores), axis=1, keepdims=True)
        columns.append(peak + jnp.log2(total))
    lse_ref[...] = to_dense(columns)


def means_kernel(tile_ref, x_ref, bias_ref, total_ref, after_ref, sent_ref, mine_ref):
    bias = bias_ref[...]
    x = x_ref[...]
    half = mine_ref.shape[0]
    n_rows = half // LANES
    core = lax.axis_index("row") % 2
    for out_ref, place in ((sent_ref, 1 - core), (mine_ref, core)):
        total = to_column(total_ref[pl.ds(place * n_rows, n_rows), :])
        for j in range(n_rows):
            at = pl.ds(pl.multiple_of(place * half + j * LANES, LANES), LANES)
            norm = total[j * LANES : (j + 1) * LANES]
            exps = [
                jnp.exp2(tile_ref[at, pl.ds(b * LANES, LANES)] + bias[b : b + 1, :] - norm)
                for b in range(bias.shape[0])
            ]
            weights = jnp.concatenate([block.astype(jnp.bfloat16) for block in exps], axis=1)
            out_ref[pl.ds(j * LANES, LANES), :] = jnp.dot(weights, x, preferred_element_type=jnp.float32)


def add_kernel(one_ref, two_ref, *refs):
    refs[-1][...] = one_ref[...] + two_ref[...]


def join_kernel(own_ref, shares_ref, *refs):
    out_ref = refs[-1]
    rows = out_ref.shape[0]
    out_ref[...] = own_ref[...] + sum(ref[...] * to_column(shares_ref[k])[:rows] for k, ref in enumerate(refs[:-1]))


def place_kernel(mine_ref, other_ref, out_hbm, sems):
    half = mine_ref.shape[0]
    core = lax.axis_index("row") % 2
    mine = pltpu.make_async_copy(mine_ref, out_hbm.at[pl.ds(core * half, half), :], sems.at[0])
    other = pltpu.make_async_copy(other_ref, out_hbm.at[pl.ds((1 - core) * half, half), :], sems.at[1])
    mine.start()
    other.start()
    mine.wait()
    other.wait()


def scores_kernel(n_x, x_ref, *refs):
    parts, (y_ref, inner_ref) = refs[:-2], refs[-2:]
    rows = inner_ref.shape[0]
    start = lax.axis_index("col") // n_x * rows
    own = x_ref[pl.ds(pl.multiple_of(start, rows), rows), :]
    unit = scale(own.shape[1])
    piece = 128
    wide = piece * len(parts)
    for b in range(y_ref.shape[0] // wide):
        at = pl.ds(b * wide, wide)
        y = jnp.concatenate([ref[pl.ds(b * piece, piece), :] for ref in parts], axis=0).astype(jnp.bfloat16)
        y_ref[at, :] = y
        inner_ref[:, at] = lax.dot_general(own, y, NT_DIMS, preferred_element_type=jnp.float32) * (2.0 * unit)


def images(flip, n_x, inner_ref, y_ref, bias_refs, scores_ref):
    rows = scores_ref.shape[0]
    n_shards = len(bias_refs)
    n_tgt = y_ref.shape[0] // n_shards
    start = ((lax.axis_index("col") ^ flip) % n_x) * rows
    block = pl.ds(pl.multiple_of(start, rows), rows)
    peak = jnp.full((rows, 1), -jnp.inf, jnp.float32)
    z = lax.axis_index("col") // n_x
    for k in range(n_shards):
        at = pl.ds(pl.multiple_of((z ^ k) * n_tgt, n_tgt), n_tgt)
        scores = inner_ref[block, at] + to_row(bias_refs[k][...])
        scores_ref[:, at] = scores
        peak = jnp.maximum(peak, jnp.max(scores, axis=1, keepdims=True))
    total = jnp.zeros((rows, 1), jnp.float32)
    numer = jnp.zeros((rows, y_ref.shape[1]), jnp.float32)
    for k in range(n_shards):
        at = pl.ds(k * n_tgt, n_tgt)
        plan = jnp.exp2(scores_ref[:, at] - peak)
        total = total + jnp.sum(plan, axis=1, keepdims=True)
        numer = numer + jnp.dot(plan.astype(jnp.bfloat16), y_ref[at, :], preferred_element_type=jnp.float32)
    return numer, total, peak


def lanes_of(column):
    rows = column.shape[0]
    if rows % LANES:
        column = jnp.concatenate([column, jnp.zeros((-rows % LANES, 1), jnp.float32)], axis=0)
    return to_dense([column[b : b + LANES] for b in range(0, column.shape[0], LANES)])


def others_kernel(n_x, n_z, inner_ref, y_ref, *refs):
    bias_refs, refs = refs[:n_z], refs[n_z:]
    for flip in range(1, n_x):
        numer, total, peak = images(flip, n_x, inner_ref, y_ref, bias_refs, refs[-1])
        refs[2 * flip - 2][...] = numer * (1.0 / total)
        refs[2 * flip - 1][...] = lanes_of(peak + jnp.log2(total))


def own_kernel(n_x, n_z, inner_ref, y_ref, *refs):
    bias_refs, lses, (out_ref, shares_ref, scores_ref) = refs[:n_z], refs[n_z:-3], refs[-3:]
    numer, total, peak = images(0, n_x, inner_ref, y_ref, bias_refs, scores_ref)
    rows = numer.shape[0]
    lse = lanes_of(peak + jnp.log2(total))
    came = [ref[...] for ref in lses]
    whole = merge_all([lse] + came)
    out_ref[...] = numer * (to_column(jnp.exp2(lse - whole))[:rows] / total)
    for k, part in enumerate(came):
        shares_ref[k] = jnp.exp2(part - whole)


def swap(value, axis, distance):
    n = lax.axis_size(axis)
    return lax.ppermute(value, axis, [(i, i ^ distance) for i in range(n)])


def bits_of(n):
    return [1 << b for b in range(n.bit_length() - 1)]


def on_device(source, target, log_source_mass, log_target_mass):
    n_src, width = source.shape
    n_tgt = target.shape[0]
    n_col, n_row = lax.axis_size("col"), lax.axis_size("row")
    count = n_src // n_col
    n_x = 1 << (len(bits_of(n_col)) // 2)
    n_z = n_col // n_x
    along_z = [[z * n_x + x for z in range(n_z)] for x in range(n_x)]
    around = [
        [(y + core) * n_col + col for col in group for core in range(2)] for y in range(0, n_row, 2) for group in along_z
    ]
    ls = log_source_mass.reshape(-1, LANES)
    lt = log_target_mass.reshape(-1, LANES)
    src_dense, tgt_dense = f32(*ls.shape), f32(*lt.shape)
    half = n_tgt // 2

    n_parts = 2
    parts = call(half_kernel, (f32(half // n_parts, width),) * n_parts, target)
    gathered = [lax.all_gather(part, ("row", "col"), axis_index_groups=around, tiled=True) for part in parts]

    tile, lse, sqx, sqy = call(
        first_kernel, (f32(n_tgt, n_src), src_dense, src_dense, tgt_dense), target, source, lt
    )
    for step in range(ITERS):
        if step > 0:
            lse = call(targets_kernel, src_dense, tile, lt, sqy, *parts)
        for distance in bits_of(n_x):
            lse = merge_all([lse, swap(lse, "col", distance)])
        parts = [lse] + [swap(lse, "col", k * n_x) for k in range(1, n_z)]
        src_bias, lse = call(sources_kernel, (src_dense, tgt_dense), tile, ls, sqx, *parts)
        parts = [lse] + [swap(lse, "row", k) for k in range(1, n_row)]
    total = merge_all(parts)

    bias = lt * LOG2E + (sqy - total) - sqy
    biases = [bias] + [swap(bias, "col", k * n_x) for k in range(1, n_z)]

    sent, mine = call(
        means_kernel, (f32(half, width), f32(half, width)), tile, source, src_bias, total, biases[1]
    )
    mine = call(add_kernel, f32(half, width), mine, swap(sent, "row", 1))
    rest = bits_of(n_row)[1:]
    for distance in rest[:-1]:
        mine = call(add_kernel, f32(half, width), mine, swap(mine, "row", distance))
    came = swap(mine, "row", rest[-1])

    n_all = n_z * n_tgt
    all_y, inner = call(
        lambda *refs: scores_kernel(n_x, *refs),
        (bf16(n_all, width), f32(n_x * count, n_all)),
        source, *gathered,
    )
    scores = pltpu.VMEM((count, n_all), jnp.float32)
    lse_dense = f32(pl.cdiv(count, LANES), LANES)
    others = call(
        lambda *refs: others_kernel(n_x, n_z, *refs),
        (f32(count, width), lse_dense) * (n_x - 1),
        inner, all_y, *biases,
        scratch=[scores],
    )
    joined = [swap(part, "col", 1 + k // 2) for k, part in enumerate(others)]
    own, own_shares = call(
        lambda *refs: own_kernel(n_x, n_z, *refs),
        (f32(count, width), f32(n_x - 1, *lse_dense.shape)),
        inner, all_y, *biases, *joined[1::2],
        scratch=[scores],
    )
    mine = call(add_kernel, f32(half, width), mine, came, joined[0], own_shares)
    target_image = call(
        place_kernel, f32(n_tgt, width), mine, swap(mine, "row", 1), out_specs=HBM, scratch=[DMA((2,))]
    )
    source_image = call(join_kernel, f32(count, width), own, own_shares, *joined[::2])
    return source_image, target_image


def solution(mesh):
    in_specs = (P("row", None), P("col", None), P("row"), P("col"))
    out_specs = (P(("row", "col"), None), P("col", None))
    return jax.shard_map(
        on_device, mesh=mesh, in_specs=in_specs, out_specs=out_specs, check_vma=False
    )
```

```python
import math

import jax
import jax.numpy as jnp
from jax import lax
from jax.experimental import pallas as pl
from jax.experimental.pallas import tpu as pltpu
from jax.sharding import PartitionSpec as P

ITERS = 2
BLUR = 0.1
LOG2E = math.log2(math.e)
LANES = 128
NT_DIMS = (((1,), (1,)), ((), ()))
VMEM = pl.BlockSpec(memory_space=pltpu.VMEM)
HBM = pl.BlockSpec(memory_space=pltpu.HBM)
ANY = pl.BlockSpec(memory_space=pl.ANY)
DMA = pltpu.SemaphoreType.DMA


def call(kernel, out_shape, *args, in_specs=None, out_specs=None, scratch=(), limit=24):
    return pl.pallas_call(
        kernel,
        out_shape=out_shape,
        in_specs=in_specs or [VMEM] * len(args),
        out_specs=out_specs or jax.tree.map(lambda _: VMEM, out_shape),
        scratch_shapes=list(scratch),
        compiler_params=pltpu.CompilerParams(vmem_limit_bytes=limit << 20),
    )(*args)


def f32(*shape):
    return jax.ShapeDtypeStruct(shape, jnp.float32)


def bf16(*shape):
    return jax.ShapeDtypeStruct(shape, jnp.bfloat16)


def scale(width):
    return LOG2E / (width * BLUR)


def to_column(dense):
    n = dense.shape[0]
    square = jnp.concatenate([dense, jnp.zeros((LANES - n, LANES), jnp.float32)], axis=0).T
    return jnp.concatenate([square[:, b : b + 1] for b in range(n)], axis=0)


def to_dense(columns):
    lane = lax.broadcasted_iota(jnp.int32, (LANES, LANES), 1)
    square = jnp.zeros((LANES, LANES), jnp.float32)
    for b, column in enumerate(columns):
        square = jnp.where(lane == b, column, square)
    return square.T[: len(columns)]


def to_row(dense):
    return jnp.concatenate([dense[b : b + 1, :] for b in range(dense.shape[0])], axis=1)


def over_targets(scores):
    peak = jnp.max(scores, axis=0, keepdims=True)
    total = jnp.sum(jnp.exp2(scores - peak), axis=0, keepdims=True)
    return peak + jnp.log2(total)


def half_at(ref, place):
    half = ref.shape[0] // 2
    return ref[pl.ds(place * half, half), :]


def merge_all(parts):
    peak = parts[0]
    for part in parts[1:]:
        peak = jnp.maximum(peak, part)
    return peak + jnp.log2(sum(jnp.exp2(part - peak) for part in parts))


def norms(block):
    wide = block.astype(jnp.float32)
    return jnp.sum(wide * wide, axis=1, keepdims=True) * scale(block.shape[1])


def half_kernel(y_ref, *out_refs):
    part = out_refs[0].shape[0]
    start = lax.axis_index("row") % 2 * part * len(out_refs)
    for k, ref in enumerate(out_refs):
        ref[...] = y_ref[pl.ds(pl.multiple_of(start + k * part, part), part), :].astype(jnp.float32)


def first_kernel(y_ref, x_ref, lt_ref, tile_ref, lse_ref, sqx_ref, sqy_ref):
    wide = 256
    y = y_ref[...]
    unit = scale(y.shape[1])
    sqy = norms(y)
    sqy_ref[...] = to_dense([sqy[b : b + LANES] for b in range(0, y.shape[0], LANES)])
    bias = to_column(lt_ref[...]) * LOG2E - sqy
    columns = []
    for b in range(x_ref.shape[0] // wide):
        at = pl.ds(b * wide, wide)
        x = x_ref[at, :]
        tile = lax.dot_general(y, x, NT_DIMS, preferred_element_type=jnp.float32) * (2.0 * unit)
        tile_ref[:, at] = tile
        row = over_targets(tile + bias)
        for c in range(wide // LANES):
            lse_ref[pl.ds(b * (wide // LANES) + c, 1), :] = row[:, c * LANES : (c + 1) * LANES]
        columns += [norms(x[c : c + LANES]) for c in range(0, wide, LANES)]
    sqx_ref[...] = to_dense(columns)


def targets_kernel(tile_ref, lt_ref, sqy_ref, *refs):
    parts, lse_ref = refs[:-1], refs[-1]
    g_pot = sqy_ref[...] - merge_all([ref[...] for ref in parts])
    bias = to_column(lt_ref[...] * LOG2E + g_pot - sqy_ref[...])
    for b in range(tile_ref.shape[1] // LANES):
        lse_ref[pl.ds(b, 1), :] = over_targets(tile_ref[:, pl.ds(b * LANES, LANES)] + bias)


def sources_kernel(tile_ref, ls_ref, sqx_ref, *refs):
    parts, (bias_ref, lse_ref) = refs[:-2], refs[-2:]
    f_pot = sqx_ref[...] - merge_all([ref[...] for ref in parts])
    bias = ls_ref[...] * LOG2E + f_pot - sqx_ref[...]
    bias_ref[...] = bias
    blocks = range(bias.shape[0])
    columns = []
    for j in range(tile_ref.shape[0] // LANES):
        at = pl.ds(j * LANES, LANES)
        scores = [tile_ref[at, pl.ds(b * LANES, LANES)] + bias[b : b + 1, :] for b in blocks]
        top = scores[0]
        for block in scores[1:]:
            top = jnp.maximum(top, block)
        peak = jnp.max(top, axis=1, keepdims=True)
        total = jnp.sum(sum(jnp.exp2(block - peak) for block in scores), axis=1, keepdims=True)
        columns.append(peak + jnp.log2(total))
    lse_ref[...] = to_dense(columns)


def means_kernel(tile_ref, x_ref, bias_ref, total_ref, after_ref, sent_ref, mine_ref):
    bias = bias_ref[...]
    x = x_ref[...]
    half = mine_ref.shape[0]
    n_rows = half // LANES
    core = lax.axis_index("row") % 2
    for out_ref, place in ((sent_ref, 1 - core), (mine_ref, core)):
        total = to_column(total_ref[pl.ds(place * n_rows, n_rows), :])
        for j in range(n_rows):
            at = pl.ds(pl.multiple_of(place * half + j * LANES, LANES), LANES)
            norm = total[j * LANES : (j + 1) * LANES]
            exps = [
                jnp.exp2(tile_ref[at, pl.ds(b * LANES, LANES)] + bias[b : b + 1, :] - norm)
                for b in range(bias.shape[0])
            ]
            weights = jnp.concatenate([block.astype(jnp.bfloat16) for block in exps], axis=1)
            out_ref[pl.ds(j * LANES, LANES), :] = jnp.dot(weights, x, preferred_element_type=jnp.float32)


def add_kernel(one_ref, two_ref, *refs):
    refs[-1][...] = one_ref[...] + two_ref[...]


def join_kernel(*refs):
    parts, out_ref = refs[:-1], refs[-1]
    rows = out_ref.shape[0]
    lses = [ref[rows : rows + pl.cdiv(rows, LANES), :LANES] for ref in parts]
    whole = merge_all(lses)
    shares = [to_column(jnp.exp2(lse - whole))[:rows] for lse in lses]
    out_ref[...] = sum(ref[:rows, :] * share for ref, share in zip(parts, shares))


def place_kernel(mine_ref, other_ref, out_hbm, sems):
    half = mine_ref.shape[0]
    core = lax.axis_index("row") % 2
    mine = pltpu.make_async_copy(mine_ref, out_hbm.at[pl.ds(core * half, half), :], sems.at[0])
    other = pltpu.make_async_copy(other_ref, out_hbm.at[pl.ds((1 - core) * half, half), :], sems.at[1])
    mine.start()
    other.start()
    mine.wait()
    other.wait()


def scores_kernel(n_x, x_ref, all_ref, y_ref, inner_ref):
    rows = inner_ref.shape[0]
    start = lax.axis_index("col") // n_x * rows
    own = x_ref[pl.ds(pl.multiple_of(start, rows), rows), :]
    unit = scale(own.shape[1])
    wide = 512
    for b in range(y_ref.shape[0] // wide):
        at = pl.ds(b * wide, wide)
        y = all_ref[at, :].astype(jnp.bfloat16)
        y_ref[at, :] = y
        inner_ref[:, at] = lax.dot_general(own, y, NT_DIMS, preferred_element_type=jnp.float32) * (2.0 * unit)


def images(flip, n_x, inner_ref, y_ref, bias_refs, scores_ref):
    rows = scores_ref.shape[0]
    n_shards = len(bias_refs)
    n_tgt = y_ref.shape[0] // n_shards
    col = lax.axis_index("col")
    block = pl.ds(pl.multiple_of((col ^ flip) % n_x * rows, rows), rows)
    peak = jnp.full((rows, 1), -jnp.inf, jnp.float32)
    for k in range(n_shards):
        at = pl.ds(pl.multiple_of((col // n_x ^ k) * n_tgt, n_tgt), n_tgt)
        scores = inner_ref[block, at] + to_row(bias_refs[k][...])
        scores_ref[:, at] = scores
        peak = jnp.maximum(peak, jnp.max(scores, axis=1, keepdims=True))
    total = jnp.zeros((rows, 1), jnp.float32)
    numer = jnp.zeros((rows, y_ref.shape[1]), jnp.float32)
    for k in range(n_shards):
        at = pl.ds(k * n_tgt, n_tgt)
        plan = jnp.exp2(scores_ref[:, at] - peak)
        total = total + jnp.sum(plan, axis=1, keepdims=True)
        numer = numer + jnp.dot(plan.astype(jnp.bfloat16), y_ref[at, :], preferred_element_type=jnp.float32)
    return numer, total, peak


def lanes_of(column):
    rows = column.shape[0]
    if rows % LANES:
        column = jnp.concatenate([column, jnp.zeros((-rows % LANES, 1), jnp.float32)], axis=0)
    return to_dense([column[b : b + LANES] for b in range(0, column.shape[0], LANES)])


EXTRA = 8


def others_kernel(n_x, inner_ref, y_ref, *refs):
    bias_refs, image_refs, scores_ref = refs[: -n_x], refs[-n_x:-1], refs[-1]
    for flip, image_ref in enumerate(image_refs, 1):
        numer, total, peak = images(flip, n_x, inner_ref, y_ref, bias_refs, scores_ref)
        rows = numer.shape[0]
        lse = lanes_of(peak + jnp.log2(total))
        image_ref[:rows, :] = numer * (1.0 / total)
        image_ref[rows:, :] = jnp.zeros((EXTRA, image_ref.shape[1]), jnp.float32)
        image_ref[rows : rows + lse.shape[0], :LANES] = lse


def own_kernel(n_x, inner_ref, y_ref, *refs):
    bias_refs, (image_ref, scores_ref) = refs[:-2], refs[-2:]
    numer, total, peak = images(0, n_x, inner_ref, y_ref, bias_refs, scores_ref)
    rows = numer.shape[0]
    lse = lanes_of(peak + jnp.log2(total))
    image_ref[:rows, :] = numer * (1.0 / total)
    image_ref[rows:, :] = jnp.zeros((EXTRA, image_ref.shape[1]), jnp.float32)
    image_ref[rows : rows + lse.shape[0], :LANES] = lse


def swap(value, axis, distance):
    n = lax.axis_size(axis)
    return lax.ppermute(value, axis, [(i, i ^ distance) for i in range(n)])


def bits_of(n):
    return [1 << b for b in range(n.bit_length() - 1)]


def on_device(source, target, log_source_mass, log_target_mass):
    n_src, width = source.shape
    n_tgt = target.shape[0]
    n_col, n_row = lax.axis_size("col"), lax.axis_size("row")
    count = n_src // n_col
    n_x = 1 << (len(bits_of(n_col)) // 2)
    n_z = n_col // n_x
    around = [
        [(y + core) * n_col + z * n_x + x for z in range(n_z) for core in range(2)]
        for y in range(0, n_row, 2)
        for x in range(n_x)
    ]
    ls = log_source_mass.reshape(-1, LANES)
    lt = log_target_mass.reshape(-1, LANES)
    src_dense, tgt_dense = f32(*ls.shape), f32(*lt.shape)
    half = n_tgt // 2

    n_parts = 1
    parts = call(half_kernel, (f32(half // n_parts, width),) * n_parts, target)
    gathered = [lax.all_gather(part, ("row", "col"), axis_index_groups=around, tiled=True) for part in parts]

    tile, lse, sqx, sqy = call(
        first_kernel, (f32(n_tgt, n_src), src_dense, src_dense, tgt_dense), target, source, lt
    )
    for step in range(ITERS):
        if step > 0:
            lse = call(targets_kernel, src_dense, tile, lt, sqy, *parts)
        for distance in bits_of(n_x):
            lse = merge_all([lse, swap(lse, "col", distance)])
        parts = [lse] + [swap(lse, "col", k * n_x) for k in range(1, n_z)]
        src_bias, lse = call(sources_kernel, (src_dense, tgt_dense), tile, ls, sqx, *parts)
        parts = [lse] + [swap(lse, "row", k) for k in range(1, n_row)]
    total = merge_all(parts)

    bias = lt * LOG2E + (sqy - total) - sqy
    biases = [bias] + [swap(bias, "col", k * n_x) for k in range(1, n_z)]

    sent, mine = call(
        means_kernel, (f32(half, width), f32(half, width)), tile, source, src_bias, total, biases[1]
    )
    mine = call(add_kernel, f32(half, width), mine, swap(sent, "row", 1))
    rest = bits_of(n_row)[1:]
    for distance in rest[:-1]:
        mine = call(add_kernel, f32(half, width), mine, swap(mine, "row", distance))
    came = swap(mine, "row", rest[-1])

    n_all = n_z * n_tgt
    all_y, inner = call(
        lambda *refs: scores_kernel(n_x, *refs),
        (bf16(n_all, width), f32(n_x * count, n_all)),
        source, *gathered,
        limit=44,
    )
    scores = pltpu.VMEM((count, n_all), jnp.float32)
    image = f32(count + EXTRA, width)
    others = call(
        lambda *refs: others_kernel(n_x, *refs), (image,) * (n_x - 1), inner, all_y, *biases, scratch=[scores]
    )
    joined = [swap(part, "col", flip) for flip, part in enumerate(others, 1)]
    own = call(lambda *refs: own_kernel(n_x, *refs), image, inner, all_y, *biases, scratch=[scores])
    mine = call(add_kernel, f32(half, width), mine, came, joined[0], own)
    target_image = call(
        place_kernel, f32(n_tgt, width), mine, swap(mine, "row", 1), out_specs=HBM, scratch=[DMA((2,))]
    )
    source_image = call(join_kernel, f32(count, width), own, *joined)
    return source_image, target_image


def solution(mesh):
    in_specs = (P("row", None), P("col", None), P("row"), P("col"))
    out_specs = (P(("row", "col"), None), P("col", None))
    return jax.shard_map(
        on_device, mesh=mesh, in_specs=in_specs, out_specs=out_specs, check_vma=False
    )
```

```python
import math

import jax
import jax.numpy as jnp
from jax import lax
from jax.experimental import pallas as pl
from jax.experimental.pallas import tpu as pltpu
from jax.sharding import PartitionSpec as P

ITERS = 2
BLUR = 0.1
LOG2E = math.log2(math.e)
LANES = 128
NT_DIMS = (((1,), (1,)), ((), ()))
VMEM = pl.BlockSpec(memory_space=pltpu.VMEM)
HBM = pl.BlockSpec(memory_space=pltpu.HBM)
ANY = pl.BlockSpec(memory_space=pl.ANY)
DMA = pltpu.SemaphoreType.DMA


def call(kernel, out_shape, *args, in_specs=None, out_specs=None, scratch=(), limit=24):
    return pl.pallas_call(
        kernel,
        out_shape=out_shape,
        in_specs=in_specs or [VMEM] * len(args),
        out_specs=out_specs or jax.tree.map(lambda _: VMEM, out_shape),
        scratch_shapes=list(scratch),
        compiler_params=pltpu.CompilerParams(vmem_limit_bytes=limit << 20),
    )(*args)


def f32(*shape):
    return jax.ShapeDtypeStruct(shape, jnp.float32)


def bf16(*shape):
    return jax.ShapeDtypeStruct(shape, jnp.bfloat16)


def scale(width):
    return LOG2E / (width * BLUR)


def to_column(dense):
    n = dense.shape[0]
    square = jnp.concatenate([dense, jnp.zeros((LANES - n, LANES), jnp.float32)], axis=0).T
    return jnp.concatenate([square[:, b : b + 1] for b in range(n)], axis=0)


def to_dense(columns):
    lane = lax.broadcasted_iota(jnp.int32, (LANES, LANES), 1)
    square = jnp.zeros((LANES, LANES), jnp.float32)
    for b, column in enumerate(columns):
        square = jnp.where(lane == b, column, square)
    return square.T[: len(columns)]


def to_row(dense):
    return jnp.concatenate([dense[b : b + 1, :] for b in range(dense.shape[0])], axis=1)


def over_targets(scores):
    peak = jnp.max(scores, axis=0, keepdims=True)
    total = jnp.sum(jnp.exp2(scores - peak), axis=0, keepdims=True)
    return peak + jnp.log2(total)


def half_at(ref, place):
    half = ref.shape[0] // 2
    return ref[pl.ds(place * half, half), :]


def merge_all(parts):
    peak = parts[0]
    for part in parts[1:]:
        peak = jnp.maximum(peak, part)
    return peak + jnp.log2(sum(jnp.exp2(part - peak) for part in parts))


def norms(block):
    wide = block.astype(jnp.float32)
    return jnp.sum(wide * wide, axis=1, keepdims=True) * scale(block.shape[1])


def quarter_kernel(y_ref, out_ref):
    rows = out_ref.shape[0]
    out_ref[...] = y_ref[pl.ds(pl.multiple_of(lax.axis_index("row") * rows, rows), rows), :].astype(jnp.float32)


def first_kernel(y_ref, x_ref, lt_ref, tile_ref, lse_ref, sqx_ref, sqy_ref):
    wide = 256
    y = y_ref[...]
    unit = scale(y.shape[1])
    sqy = norms(y)
    sqy_ref[...] = to_dense([sqy[b : b + LANES] for b in range(0, y.shape[0], LANES)])
    bias = to_column(lt_ref[...]) * LOG2E - sqy
    columns = []
    for b in range(x_ref.shape[0] // wide):
        at = pl.ds(b * wide, wide)
        x = x_ref[at, :]
        tile = lax.dot_general(y, x, NT_DIMS, preferred_element_type=jnp.float32) * (2.0 * unit)
        tile_ref[:, at] = tile
        row = over_targets(tile + bias)
        for c in range(wide // LANES):
            lse_ref[pl.ds(b * (wide // LANES) + c, 1), :] = row[:, c * LANES : (c + 1) * LANES]
        columns += [norms(x[c : c + LANES]) for c in range(0, wide, LANES)]
    sqx_ref[...] = to_dense(columns)


def targets_kernel(n_parts, tile_ref, lt_ref, sqy_ref, *refs):
    parts, pieces, (lse_ref, pack_ref) = refs[:n_parts], refs[n_parts:-2], refs[-2:]
    half = pieces[0].shape[0] // 2
    pack_ref[:half, :] = pieces[0][half:, :]
    for k, piece in enumerate(pieces[1:]):
        pack_ref[pl.ds(half + 2 * half * k, 2 * half), :] = piece[...]
    g_pot = sqy_ref[...] - merge_all([ref[...] for ref in parts])
    bias = to_column(lt_ref[...] * LOG2E + g_pot - sqy_ref[...])
    for b in range(tile_ref.shape[1] // LANES):
        lse_ref[pl.ds(b, 1), :] = over_targets(tile_ref[:, pl.ds(b * LANES, LANES)] + bias)


def merge_kernel(one_ref, two_ref, *refs):
    n_pieces = len(refs) // 2
    pieces, (out_ref, pack_ref, *copies) = refs[:n_pieces], refs[n_pieces:]
    out_ref[...] = merge_all([one_ref[...], two_ref[...]])
    rows = pieces[0].shape[0]
    pack_ref[:rows, :] = pieces[0][...]
    pack_ref[rows:, :] = pieces[1][: rows // 2, :]
    for piece, copy in zip(pieces[1:], copies):
        copy[...] = piece[...]


def sources_kernel(n_parts, tile_ref, ls_ref, sqx_ref, *refs):
    sources_pass(tile_ref, ls_ref, sqx_ref, refs[:n_parts], *refs[-2:])


def last_sources_kernel(n_parts, tile_ref, ls_ref, sqx_ref, *refs):
    pieces, (bias_ref, lse_ref, pack_ref) = refs[n_parts:-3], refs[-3:]
    n_shards, n_y, rows, _ = pack_ref.shape
    y = lax.axis_index("row") // 2
    early, late = pieces[:n_y], pieces[n_y:]
    half = rows // 2
    for j in range(n_y):
        place = y ^ j
        pack_ref[0, place] = early[j][:rows, :]
        pack_ref[1, place, :half, :] = early[j][rows:, :]
        pack_ref[1, place, half:, :] = late[j][:half, :]
        for k in range(2, n_shards):
            pack_ref[k, place] = late[j][pl.ds(half + (k - 2) * rows, rows), :]
    sources_pass(tile_ref, ls_ref, sqx_ref, refs[:n_parts], bias_ref, lse_ref)


def sources_pass(tile_ref, ls_ref, sqx_ref, parts, bias_ref, lse_ref):
    f_pot = sqx_ref[...] - merge_all([ref[...] for ref in parts])
    bias = ls_ref[...] * LOG2E + f_pot - sqx_ref[...]
    bias_ref[...] = bias
    blocks = range(bias.shape[0])
    columns = []
    for j in range(tile_ref.shape[0] // LANES):
        at = pl.ds(j * LANES, LANES)
        scores = [tile_ref[at, pl.ds(b * LANES, LANES)] + bias[b : b + 1, :] for b in blocks]
        top = scores[0]
        for block in scores[1:]:
            top = jnp.maximum(top, block)
        peak = jnp.max(top, axis=1, keepdims=True)
        total = jnp.sum(sum(jnp.exp2(block - peak) for block in scores), axis=1, keepdims=True)
        columns.append(peak + jnp.log2(total))
    lse_ref[...] = to_dense(columns)


def means_kernel(tile_ref, x_ref, bias_ref, total_ref, sent_ref, mine_ref):
    bias = bias_ref[...]
    x = x_ref[...]
    half = mine_ref.shape[0]
    n_rows = half // LANES
    core = lax.axis_index("row") % 2
    for out_ref, place in ((sent_ref, 1 - core), (mine_ref, core)):
        total = to_column(total_ref[pl.ds(place * n_rows, n_rows), :])
        for j in range(n_rows):
            at = pl.ds(pl.multiple_of(place * half + j * LANES, LANES), LANES)
            norm = total[j * LANES : (j + 1) * LANES]
            exps = [
                jnp.exp2(tile_ref[at, pl.ds(b * LANES, LANES)] + bias[b : b + 1, :] - norm)
                for b in range(bias.shape[0])
            ]
            weights = jnp.concatenate([block.astype(jnp.bfloat16) for block in exps], axis=1)
            out_ref[pl.ds(j * LANES, LANES), :] = jnp.dot(weights, x, preferred_element_type=jnp.float32)


def add_kernel(one_ref, two_ref, *refs):
    refs[-1][...] = one_ref[...] + two_ref[...]


def join_kernel(*refs):
    parts, out_ref = refs[:-1], refs[-1]
    rows = out_ref.shape[0]
    lses = [ref[rows : rows + pl.cdiv(rows, LANES), :LANES] for ref in parts]
    whole = merge_all(lses)
    shares = [to_column(jnp.exp2(lse - whole))[:rows] for lse in lses]
    out_ref[...] = sum(ref[:rows, :] * share for ref, share in zip(parts, shares))


def place_kernel(mine_ref, other_ref, out_hbm, sems):
    half = mine_ref.shape[0]
    core = lax.axis_index("row") % 2
    mine = pltpu.make_async_copy(mine_ref, out_hbm.at[pl.ds(core * half, half), :], sems.at[0])
    other = pltpu.make_async_copy(other_ref, out_hbm.at[pl.ds((1 - core) * half, half), :], sems.at[1])
    mine.start()
    other.start()
    mine.wait()
    other.wait()


def scores_kernel(near, x_ref, own_ref, mine_ref, other_ref, y_ref, inner_ref):
    rows = inner_ref.shape[0] // 2
    n_tgt = own_ref.shape[0]
    n_came, n_y, part, _ = mine_ref.shape
    col, core = lax.axis_index("col"), lax.axis_index("row") % 2
    y_ref[:n_tgt, :] = own_ref[...]
    for k in range(n_came):
        for ref, place in ((mine_ref, core), (other_ref, 1 - core)):
            for y in range(n_y):
                start = (k + 1) * n_tgt + (2 * y + place) * part
                y_ref[pl.ds(pl.multiple_of(start, part), part), :] = ref[k, y].astype(jnp.bfloat16)
    blocks = [x_ref[pl.ds(pl.multiple_of((col ^ flip) * rows, rows), rows), :] for flip in (0, near)]
    x = jnp.concatenate(blocks, axis=0)
    unit = scale(x.shape[1])
    for b in range(y_ref.shape[0] // n_tgt):
        at = pl.ds(b * n_tgt, n_tgt)
        inner_ref[:, at] = lax.dot_general(x, y_ref[at, :], NT_DIMS, preferred_element_type=jnp.float32) * (2.0 * unit)


EXTRA = 8


def images(flip, inner_ref, y_ref, bias_refs, scores_ref):
    rows = scores_ref.shape[0]
    n_shards = len(bias_refs)
    n_tgt = y_ref.shape[0] // n_shards
    block = pl.ds(flip * rows, rows)
    peak = jnp.full((rows, 1), -jnp.inf, jnp.float32)
    for k in range(n_shards):
        at = pl.ds(k * n_tgt, n_tgt)
        scores = inner_ref[block, at] + to_row(bias_refs[k][...])
        scores_ref[:, at] = scores
        peak = jnp.maximum(peak, jnp.max(scores, axis=1, keepdims=True))
    total = jnp.zeros((rows, 1), jnp.float32)
    numer = jnp.zeros((rows, y_ref.shape[1]), jnp.float32)
    for k in range(n_shards):
        at = pl.ds(k * n_tgt, n_tgt)
        plan = jnp.exp2(scores_ref[:, at] - peak)
        total = total + jnp.sum(plan, axis=1, keepdims=True)
        numer = numer + jnp.dot(plan.astype(jnp.bfloat16), y_ref[at, :], preferred_element_type=jnp.float32)
    return numer, total, peak


def lanes_of(column):
    rows = column.shape[0]
    if rows % LANES:
        column = jnp.concatenate([column, jnp.zeros((-rows % LANES, 1), jnp.float32)], axis=0)
    return to_dense([column[b : b + LANES] for b in range(0, column.shape[0], LANES)])


EXTRA = 8


def image_kernel(flip, inner_ref, y_ref, *refs):
    bias_refs, (image_ref, scores_ref) = refs[:-3], refs[-2:]
    numer, total, peak = images(flip, inner_ref, y_ref, bias_refs, scores_ref)
    rows = numer.shape[0]
    lse = lanes_of(peak + jnp.log2(total))
    image_ref[:rows, :] = numer * (1.0 / total)
    image_ref[rows:, :] = jnp.zeros((EXTRA, image_ref.shape[1]), jnp.float32)
    image_ref[rows : rows + lse.shape[0], :LANES] = lse


def swap(value, axis, distance):
    n = lax.axis_size(axis)
    return lax.ppermute(value, axis, [(i, i ^ distance) for i in range(n)])


def bits_of(n):
    return [1 << b for b in range(n.bit_length() - 1)]


def on_device(source, target, log_source_mass, log_target_mass):
    n_src, width = source.shape
    n_tgt = target.shape[0]
    n_col, n_row = lax.axis_size("col"), lax.axis_size("row")
    count = n_src // n_col
    n_x = 1 << (len(bits_of(n_col)) // 2)
    n_z = n_col // n_x
    y_bits = bits_of(n_row)[1:]
    ls = log_source_mass.reshape(-1, LANES)
    lt = log_target_mass.reshape(-1, LANES)
    src_dense, tgt_dense = f32(*ls.shape), f32(*lt.shape)
    half = n_tgt // 2

    part = f32(n_tgt // n_row, width)
    pieces = {0: call(quarter_kernel, part, target)}
    for distance in [bit for bit in bits_of(n_col) if bit > n_x][::-1]:
        pieces |= {k ^ distance: swap(piece, "col", distance) for k, piece in pieces.items()}
    early = swap(pieces[0], "col", 1)

    def along_y(piece):
        held = [piece]
        for distance in y_bits:
            held += [swap(one, "row", distance) for one in held]
        return held

    tile, lse, sqx, sqy = call(
        first_kernel, (f32(n_tgt, n_src), src_dense, src_dense, tgt_dense), target, source, lt
    )
    for step in range(ITERS):
        if step > 0:
            apart = [0, 1] + [k for k in pieces if k > 1]
            lse, late = call(
                lambda *refs: targets_kernel(n_row, *refs),
                (src_dense, f32((2 * len(apart) - 5) * part.shape[0] // 2, width)),
                tile, lt, sqy, *parts, *[pieces[k] for k in apart[2:]],
            )
            late = along_y(late)
        for distance in bits_of(n_x):
            came = swap(lse, "col", distance)
            if step > 0 or distance > 1:
                lse = merge_all([lse, came])
                continue
            far = [k for k in pieces if k > 0]
            lse, early, *copies = call(
                merge_kernel,
                (src_dense, f32(part.shape[0] * 3 // 2, width), *(part,) * len(far)),
                lse, came, early, *[pieces[k] for k in far],
            )
            early = along_y(early)
            pieces |= dict(zip(far, copies))
            for bit in bits_of(n_x)[::-1]:
                pieces |= {k ^ bit: swap(piece, "col", bit) for k, piece in pieces.items() if k ^ bit != 1}
        parts = [lse] + [swap(lse, "col", k * n_x) for k in range(1, n_z)]
        if step < ITERS - 1:
            src_bias, lse = call(
                lambda *refs: sources_kernel(n_z, *refs), (src_dense, tgt_dense), tile, ls, sqx, *parts, *early
            )
        else:
            src_bias, lse, came = call(
                lambda *refs: last_sources_kernel(n_z, *refs),
                (src_dense, tgt_dense, f32(len(apart) - 1, n_row // 2, *part.shape)),
                tile, ls, sqx, *parts, *early, *late,
            )
        parts = [lse] + [swap(lse, "row", k) for k in range(1, n_row)]
    total = merge_all(parts)

    bias = lt * LOG2E + (sqy - total) - sqy
    biases = [bias] + [swap(bias, "col", distance) for distance in apart[1:]]

    sent, mine = call(means_kernel, (f32(half, width), f32(half, width)), tile, source, src_bias, total)
    mine = call(add_kernel, f32(half, width), mine, swap(sent, "row", 1))
    rest = bits_of(n_row)[1:]
    for distance in rest[:-1]:
        mine = call(add_kernel, f32(half, width), mine, swap(mine, "row", distance))
    mine_came = swap(mine, "row", rest[-1])

    n_all = len(apart) * n_tgt
    all_y, inner = call(
        lambda *refs: scores_kernel(n_x, *refs),
        (bf16(n_all, width), f32(2 * count, n_all)),
        source, target, came, swap(came, "row", 1),
        limit=32,
    )

    def image(flip, after):
        return call(
            lambda *refs: image_kernel(flip, *refs),
            f32(count + EXTRA, width),
            inner, all_y, *biases, after,
            scratch=[pltpu.VMEM((count, n_all), jnp.float32)],
        )

    sent = image(1, mine)
    came = swap(sent, "col", n_x)
    own = image(0, sent)
    mine = call(add_kernel, f32(half, width), mine, mine_came, came, own)
    target_image = call(
        place_kernel, f32(n_tgt, width), mine, swap(mine, "row", 1), out_specs=HBM, scratch=[DMA((2,))]
    )
    source_image = call(join_kernel, f32(count, width), own, came)
    return source_image, target_image


def solution(mesh):
    in_specs = (P("row", None), P("col", None), P("row"), P("col"))
    out_specs = (P(("row", "col"), None), P("col", None))
    return jax.shard_map(
        on_device, mesh=mesh, in_specs=in_specs, out_specs=out_specs, check_vma=False
    )
```

```python
import math

import jax
import jax.numpy as jnp
from jax import lax
from jax.experimental import pallas as pl
from jax.experimental.pallas import tpu as pltpu
from jax.sharding import PartitionSpec as P

ITERS = 2
BLUR = 0.1
LOG2E = math.log2(math.e)
LANES = 128
NT_DIMS = (((1,), (1,)), ((), ()))
VMEM = pl.BlockSpec(memory_space=pltpu.VMEM)
HBM = pl.BlockSpec(memory_space=pltpu.HBM)
ANY = pl.BlockSpec(memory_space=pl.ANY)
DMA = pltpu.SemaphoreType.DMA


def call(kernel, out_shape, *args, in_specs=None, out_specs=None, scratch=(), limit=24):
    return pl.pallas_call(
        kernel,
        out_shape=out_shape,
        in_specs=in_specs or [VMEM] * len(args),
        out_specs=out_specs or jax.tree.map(lambda _: VMEM, out_shape),
        scratch_shapes=list(scratch),
        compiler_params=pltpu.CompilerParams(vmem_limit_bytes=limit << 20),
    )(*args)


def f32(*shape):
    return jax.ShapeDtypeStruct(shape, jnp.float32)


def bf16(*shape):
    return jax.ShapeDtypeStruct(shape, jnp.bfloat16)


def scale(width):
    return LOG2E / (width * BLUR)


def to_column(dense):
    n = dense.shape[0]
    square = jnp.concatenate([dense, jnp.zeros((LANES - n, LANES), jnp.float32)], axis=0).T
    return jnp.concatenate([square[:, b : b + 1] for b in range(n)], axis=0)


def to_dense(columns):
    lane = lax.broadcasted_iota(jnp.int32, (LANES, LANES), 1)
    square = jnp.zeros((LANES, LANES), jnp.float32)
    for b, column in enumerate(columns):
        square = jnp.where(lane == b, column, square)
    return square.T[: len(columns)]


def to_row(dense):
    return jnp.concatenate([dense[b : b + 1, :] for b in range(dense.shape[0])], axis=1)


def over_targets(scores):
    peak = jnp.max(scores, axis=0, keepdims=True)
    total = jnp.sum(jnp.exp2(scores - peak), axis=0, keepdims=True)
    return peak + jnp.log2(total)


def half_at(ref, place):
    half = ref.shape[0] // 2
    return ref[pl.ds(place * half, half), :]


def merge_all(parts):
    peak = parts[0]
    for part in parts[1:]:
        peak = jnp.maximum(peak, part)
    return peak + jnp.log2(sum(jnp.exp2(part - peak) for part in parts))


def norms(block):
    wide = block.astype(jnp.float32)
    return jnp.sum(wide * wide, axis=1, keepdims=True) * scale(block.shape[1])


def quarter_kernel(y_ref, out_ref):
    rows = out_ref.shape[0]
    out_ref[...] = y_ref[pl.ds(pl.multiple_of(lax.axis_index("row") * rows, rows), rows), :].astype(jnp.float32)


def first_kernel(y_ref, x_ref, lt_ref, tile_ref, lse_ref, sqx_ref, sqy_ref):
    wide = 256
    y = y_ref[...]
    unit = scale(y.shape[1])
    sqy = norms(y)
    sqy_ref[...] = to_dense([sqy[b : b + LANES] for b in range(0, y.shape[0], LANES)])
    bias = to_column(lt_ref[...]) * LOG2E - sqy
    columns = []
    for b in range(x_ref.shape[0] // wide):
        at = pl.ds(b * wide, wide)
        x = x_ref[at, :]
        tile = lax.dot_general(y, x, NT_DIMS, preferred_element_type=jnp.float32) * (2.0 * unit)
        tile_ref[:, at] = tile
        row = over_targets(tile + bias)
        for c in range(wide // LANES):
            lse_ref[pl.ds(b * (wide // LANES) + c, 1), :] = row[:, c * LANES : (c + 1) * LANES]
        columns += [norms(x[c : c + LANES]) for c in range(0, wide, LANES)]
    sqx_ref[...] = to_dense(columns)


def targets_kernel(n_parts, tile_ref, lt_ref, sqy_ref, *refs):
    parts, pieces, (lse_ref, pack_ref) = refs[:n_parts], refs[n_parts:-2], refs[-2:]
    half = pieces[0].shape[0] // 2
    pack_ref[:half, :] = pieces[0][half:, :]
    for k, piece in enumerate(pieces[1:]):
        pack_ref[pl.ds(half + 2 * half * k, 2 * half), :] = piece[...]
    g_pot = sqy_ref[...] - merge_all([ref[...] for ref in parts])
    bias = to_column(lt_ref[...] * LOG2E + g_pot - sqy_ref[...])
    for b in range(tile_ref.shape[1] // LANES):
        lse_ref[pl.ds(b, 1), :] = over_targets(tile_ref[:, pl.ds(b * LANES, LANES)] + bias)


def merge_kernel(one_ref, two_ref, *refs):
    n_pieces = len(refs) // 2
    pieces, (out_ref, pack_ref, *copies) = refs[:n_pieces], refs[n_pieces:]
    out_ref[...] = merge_all([one_ref[...], two_ref[...]])
    rows = pieces[-1].shape[0]
    pack_ref[:rows, :] = pieces[-1][...]
    pack_ref[rows:, :] = pieces[0][: rows // 2, :]
    for piece, copy in zip(pieces[:-1], copies):
        copy[...] = piece[...]


def sources_kernel(n_parts, tile_ref, ls_ref, sqx_ref, *refs):
    sources_pass(tile_ref, ls_ref, sqx_ref, refs[:n_parts], *refs[-2:])


def last_sources_kernel(n_parts, tile_ref, ls_ref, sqx_ref, *refs):
    pieces, (bias_ref, lse_ref, pack_ref) = refs[n_parts:-3], refs[-3:]
    n_shards, n_y, rows, _ = pack_ref.shape
    y = lax.axis_index("row") // 2
    early, late = pieces[:n_y], pieces[n_y:]
    half = rows // 2
    for j in range(n_y):
        place = y ^ j
        pack_ref[0, place] = early[j][:rows, :]
        pack_ref[1, place, :half, :] = early[j][rows:, :]
        pack_ref[1, place, half:, :] = late[j][:half, :]
        for k in range(2, n_shards):
            pack_ref[k, place] = late[j][pl.ds(half + (k - 2) * rows, rows), :]
    sources_pass(tile_ref, ls_ref, sqx_ref, refs[:n_parts], bias_ref, lse_ref)


def sources_pass(tile_ref, ls_ref, sqx_ref, parts, bias_ref, lse_ref):
    f_pot = sqx_ref[...] - merge_all([ref[...] for ref in parts])
    bias = ls_ref[...] * LOG2E + f_pot - sqx_ref[...]
    bias_ref[...] = bias
    blocks = range(bias.shape[0])
    columns = []
    for j in range(tile_ref.shape[0] // LANES):
        at = pl.ds(j * LANES, LANES)
        scores = [tile_ref[at, pl.ds(b * LANES, LANES)] + bias[b : b + 1, :] for b in blocks]
        top = scores[0]
        for block in scores[1:]:
            top = jnp.maximum(top, block)
        peak = jnp.max(top, axis=1, keepdims=True)
        total = jnp.sum(sum(jnp.exp2(block - peak) for block in scores), axis=1, keepdims=True)
        columns.append(peak + jnp.log2(total))
    lse_ref[...] = to_dense(columns)


def means_kernel(tile_ref, x_ref, bias_ref, total_ref, sent_ref, mine_ref):
    bias = bias_ref[...]
    x = x_ref[...]
    half = mine_ref.shape[0]
    n_rows = half // LANES
    core = lax.axis_index("row") % 2
    for out_ref, place in ((sent_ref, 1 - core), (mine_ref, core)):
        total = to_column(total_ref[pl.ds(place * n_rows, n_rows), :])
        for j in range(n_rows):
            at = pl.ds(pl.multiple_of(place * half + j * LANES, LANES), LANES)
            norm = total[j * LANES : (j + 1) * LANES]
            exps = [
                jnp.exp2(tile_ref[at, pl.ds(b * LANES, LANES)] + bias[b : b + 1, :] - norm)
                for b in range(bias.shape[0])
            ]
            weights = jnp.concatenate([block.astype(jnp.bfloat16) for block in exps], axis=1)
            out_ref[pl.ds(j * LANES, LANES), :] = jnp.dot(weights, x, preferred_element_type=jnp.float32)


def add_kernel(one_ref, two_ref, *refs):
    refs[-1][...] = one_ref[...] + two_ref[...]


def join_kernel(*refs):
    parts, out_ref = refs[:-1], refs[-1]
    rows = out_ref.shape[0]
    lses = [ref[rows : rows + pl.cdiv(rows, LANES), :LANES] for ref in parts]
    whole = merge_all(lses)
    shares = [to_column(jnp.exp2(lse - whole))[:rows] for lse in lses]
    out_ref[...] = sum(ref[:rows, :] * share for ref, share in zip(parts, shares))


def place_kernel(mine_ref, other_ref, out_hbm, sems):
    half = mine_ref.shape[0]
    core = lax.axis_index("row") % 2
    mine = pltpu.make_async_copy(mine_ref, out_hbm.at[pl.ds(core * half, half), :], sems.at[0])
    other = pltpu.make_async_copy(other_ref, out_hbm.at[pl.ds((1 - core) * half, half), :], sems.at[1])
    mine.start()
    other.start()
    mine.wait()
    other.wait()


def scores_kernel(near, x_ref, own_ref, mine_ref, other_ref, y_ref, inner_ref):
    rows = inner_ref.shape[0] // 2
    n_tgt = own_ref.shape[0]
    n_came, n_y, part, _ = mine_ref.shape
    col, core = lax.axis_index("col"), lax.axis_index("row") % 2
    y_ref[:n_tgt, :] = own_ref[...]
    for k in range(n_came):
        for ref, place in ((mine_ref, core), (other_ref, 1 - core)):
            for y in range(n_y):
                start = (k + 1) * n_tgt + (2 * y + place) * part
                y_ref[pl.ds(pl.multiple_of(start, part), part), :] = ref[k, y].astype(jnp.bfloat16)
    blocks = [x_ref[pl.ds(pl.multiple_of((col ^ flip) * rows, rows), rows), :] for flip in (0, near)]
    x = jnp.concatenate(blocks, axis=0)
    unit = scale(x.shape[1])
    for b in range(y_ref.shape[0] // n_tgt):
        at = pl.ds(b * n_tgt, n_tgt)
        inner_ref[:, at] = lax.dot_general(x, y_ref[at, :], NT_DIMS, preferred_element_type=jnp.float32) * (2.0 * unit)


EXTRA = 8


def images(flip, inner_ref, y_ref, bias_refs, scores_ref):
    rows = scores_ref.shape[0]
    n_shards = len(bias_refs)
    n_tgt = y_ref.shape[0] // n_shards
    block = pl.ds(flip * rows, rows)
    peak = jnp.full((rows, 1), -jnp.inf, jnp.float32)
    for k, bias_ref in enumerate(bias_refs[::-1]):
        at = pl.ds(k * n_tgt, n_tgt)
        scores = inner_ref[block, at] + to_row(bias_ref[...])
        scores_ref[:, at] = scores
        peak = jnp.maximum(peak, jnp.max(scores, axis=1, keepdims=True))
    total = jnp.zeros((rows, 1), jnp.float32)
    numer = jnp.zeros((rows, y_ref.shape[1]), jnp.float32)
    for k in range(n_shards):
        at = pl.ds(k * n_tgt, n_tgt)
        plan = jnp.exp2(scores_ref[:, at] - peak)
        total = total + jnp.sum(plan, axis=1, keepdims=True)
        numer = numer + jnp.dot(plan.astype(jnp.bfloat16), y_ref[at, :], preferred_element_type=jnp.float32)
    return numer, total, peak


def lanes_of(column):
    rows = column.shape[0]
    if rows % LANES:
        column = jnp.concatenate([column, jnp.zeros((-rows % LANES, 1), jnp.float32)], axis=0)
    return to_dense([column[b : b + LANES] for b in range(0, column.shape[0], LANES)])


EXTRA = 8


def image_kernel(flip, inner_ref, y_ref, *refs):
    bias_refs, (image_ref, scores_ref) = refs[:-3], refs[-2:]
    numer, total, peak = images(flip, inner_ref, y_ref, bias_refs, scores_ref)
    rows = numer.shape[0]
    lse = lanes_of(peak + jnp.log2(total))
    image_ref[:rows, :] = numer * (1.0 / total)
    image_ref[rows:, :] = jnp.zeros((EXTRA, image_ref.shape[1]), jnp.float32)
    image_ref[rows : rows + lse.shape[0], :LANES] = lse


def swap(value, axis, distance):
    n = lax.axis_size(axis)
    return lax.ppermute(value, axis, [(i, i ^ distance) for i in range(n)])


def bits_of(n):
    return [1 << b for b in range(n.bit_length() - 1)]


def on_device(source, target, log_source_mass, log_target_mass):
    n_src, width = source.shape
    n_tgt = target.shape[0]
    n_col, n_row = lax.axis_size("col"), lax.axis_size("row")
    count = n_src // n_col
    n_x = 1 << (len(bits_of(n_col)) // 2)
    n_z = n_col // n_x
    y_bits = bits_of(n_row)[1:]
    ls = log_source_mass.reshape(-1, LANES)
    lt = log_target_mass.reshape(-1, LANES)
    src_dense, tgt_dense = f32(*ls.shape), f32(*lt.shape)
    half = n_tgt // 2

    part = f32(n_tgt // n_row, width)
    pieces = {0: call(quarter_kernel, part, target)}
    for distance in [bit for bit in bits_of(n_col) if bit > n_x][::-1]:
        pieces |= {k ^ distance: swap(piece, "col", distance) for k, piece in pieces.items()}
    early = swap(pieces[0], "col", 1)

    def along_y(piece):
        held = [piece]
        for distance in y_bits:
            held += [swap(one, "row", distance) for one in held]
        return held

    tile, lse, sqx, sqy = call(
        first_kernel, (f32(n_tgt, n_src), src_dense, src_dense, tgt_dense), target, source, lt
    )
    for step in range(ITERS):
        if step > 0:
            apart = [0, 1] + [k for k in pieces if k > 1]
            lse, late = call(
                lambda *refs: targets_kernel(n_row, *refs),
                (src_dense, f32((2 * len(apart) - 5) * part.shape[0] // 2, width)),
                tile, lt, sqy, *parts, *[pieces[k] for k in apart[2:]],
            )
            late = along_y(late)
        for distance in bits_of(n_x):
            came = swap(lse, "col", distance)
            if step > 0 or distance > 1:
                lse = merge_all([lse, came])
                continue
            far = [k for k in pieces if k > 0]
            lse, early, *copies = call(
                merge_kernel,
                (src_dense, f32(part.shape[0] * 3 // 2, width), *(part,) * len(far)),
                lse, came, *[pieces[k] for k in far], early,
            )
            early = along_y(early)
            pieces |= dict(zip(far, copies))
            for bit in bits_of(n_x)[::-1]:
                pieces |= {k ^ bit: swap(piece, "col", bit) for k, piece in pieces.items() if k ^ bit != 1}
        parts = [merge_all([lse, swap(lse, "col", (n_z - 1) * n_x)])]
        parts += [swap(lse, "col", k * n_x) for k in range(n_z - 2, 0, -1)]
        if step < ITERS - 1:
            src_bias, lse = call(
                lambda *refs: sources_kernel(n_z - 1, *refs), (src_dense, tgt_dense), tile, ls, sqx, *parts, *early
            )
        else:
            src_bias, lse, came = call(
                lambda *refs: last_sources_kernel(n_z - 1, *refs),
                (src_dense, tgt_dense, f32(len(apart) - 1, n_row // 2, *part.shape)),
                tile, ls, sqx, *parts, *early, *late,
            )
        parts = [lse] + [swap(lse, "row", k) for k in range(1, n_row)]
    total = merge_all(parts)

    bias = lt * LOG2E + (sqy - total) - sqy
    biases = [bias] + [swap(bias, "col", distance) for distance in apart[1:]]

    sent, mine = call(means_kernel, (f32(half, width), f32(half, width)), tile, source, src_bias, total)
    mine = call(add_kernel, f32(half, width), mine, swap(sent, "row", 1))
    rest = bits_of(n_row)[1:]
    for distance in rest[:-1]:
        mine = call(add_kernel, f32(half, width), mine, swap(mine, "row", distance))
    mine_came = swap(mine, "row", rest[-1])

    n_all = len(apart) * n_tgt
    all_y, inner = call(
        lambda *refs: scores_kernel(n_x, *refs),
        (bf16(n_all, width), f32(2 * count, n_all)),
        source, target, came, swap(came, "row", 1),
        limit=32,
    )

    def image(flip, after):
        return call(
            lambda *refs: image_kernel(flip, *refs),
            f32(count + EXTRA, width),
            inner, all_y, *biases[::-1], after,
            scratch=[pltpu.VMEM((count, n_all), jnp.float32)],
        )

    sent = image(1, mine)
    came = swap(sent, "col", n_x)
    own = image(0, sent)
    mine = call(add_kernel, f32(half, width), mine, mine_came, came, own)
    target_image = call(
        place_kernel, f32(n_tgt, width), mine, swap(mine, "row", 1), out_specs=HBM, scratch=[DMA((2,))]
    )
    source_image = call(join_kernel, f32(count, width), own, came)
    return source_image, target_image


def solution(mesh):
    in_specs = (P("row", None), P("col", None), P("row"), P("col"))
    out_specs = (P(("row", "col"), None), P("col", None))
    return jax.shard_map(
        on_device, mesh=mesh, in_specs=in_specs, out_specs=out_specs, check_vma=False
    )
```

```python
import math

import jax
import jax.numpy as jnp
from jax import lax
from jax.experimental import pallas as pl
from jax.experimental.pallas import tpu as pltpu
from jax.sharding import PartitionSpec as P

ITERS = 2
BLUR = 0.1
LOG2E = math.log2(math.e)
LANES = 128
NT_DIMS = (((1,), (1,)), ((), ()))
VMEM = pl.BlockSpec(memory_space=pltpu.VMEM)
HBM = pl.BlockSpec(memory_space=pltpu.HBM)
ANY = pl.BlockSpec(memory_space=pl.ANY)
DMA = pltpu.SemaphoreType.DMA


def call(kernel, out_shape, *args, in_specs=None, out_specs=None, scratch=(), limit=24):
    return pl.pallas_call(
        kernel,
        out_shape=out_shape,
        in_specs=in_specs or [VMEM] * len(args),
        out_specs=out_specs or jax.tree.map(lambda _: VMEM, out_shape),
        scratch_shapes=list(scratch),
        compiler_params=pltpu.CompilerParams(vmem_limit_bytes=limit << 20),
    )(*args)


def f32(*shape):
    return jax.ShapeDtypeStruct(shape, jnp.float32)


def bf16(*shape):
    return jax.ShapeDtypeStruct(shape, jnp.bfloat16)


def scale(width):
    return LOG2E / (width * BLUR)


def to_column(dense):
    n = dense.shape[0]
    square = jnp.concatenate([dense, jnp.zeros((LANES - n, LANES), jnp.float32)], axis=0).T
    return jnp.concatenate([square[:, b : b + 1] for b in range(n)], axis=0)


def to_dense(columns):
    lane = lax.broadcasted_iota(jnp.int32, (LANES, LANES), 1)
    square = jnp.zeros((LANES, LANES), jnp.float32)
    for b, column in enumerate(columns):
        square = jnp.where(lane == b, column, square)
    return square.T[: len(columns)]


def to_row(dense):
    return jnp.concatenate([dense[b : b + 1, :] for b in range(dense.shape[0])], axis=1)


def over_targets(scores):
    peak = jnp.max(scores, axis=0, keepdims=True)
    total = jnp.sum(jnp.exp2(scores - peak), axis=0, keepdims=True)
    return peak + jnp.log2(total)


def half_at(ref, place):
    half = ref.shape[0] // 2
    return ref[pl.ds(place * half, half), :]


def merge_all(parts):
    peak = parts[0]
    for part in parts[1:]:
        peak = jnp.maximum(peak, part)
    return peak + jnp.log2(sum(jnp.exp2(part - peak) for part in parts))


def norms(block):
    wide = block.astype(jnp.float32)
    return jnp.sum(wide * wide, axis=1, keepdims=True) * scale(block.shape[1])


def quarter_kernel(y_ref, out_ref):
    rows = out_ref.shape[0]
    out_ref[...] = y_ref[pl.ds(pl.multiple_of(lax.axis_index("row") * rows, rows), rows), :].astype(jnp.float32)


def first_kernel(y_ref, x_ref, lt_ref, tile_ref, lse_ref, sqx_ref, sqy_ref):
    wide = 256
    y = y_ref[...]
    unit = scale(y.shape[1])
    sqy = norms(y)
    sqy_ref[...] = to_dense([sqy[b : b + LANES] for b in range(0, y.shape[0], LANES)])
    bias = to_column(lt_ref[...]) * LOG2E - sqy
    columns = []
    for b in range(x_ref.shape[0] // wide):
        at = pl.ds(b * wide, wide)
        x = x_ref[at, :]
        tile = lax.dot_general(y, x, NT_DIMS, preferred_element_type=jnp.float32) * (2.0 * unit)
        tile_ref[:, at] = tile
        row = over_targets(tile + bias)
        for c in range(wide // LANES):
            lse_ref[pl.ds(b * (wide // LANES) + c, 1), :] = row[:, c * LANES : (c + 1) * LANES]
        columns += [norms(x[c : c + LANES]) for c in range(0, wide, LANES)]
    sqx_ref[...] = to_dense(columns)


def early_rows(rows):
    return rows // 4


def targets_kernel(n_parts, tile_ref, lt_ref, sqy_ref, *refs):
    parts, pieces, (lse_ref, pack_ref) = refs[:n_parts], refs[n_parts:-3], refs[-2:]
    rows = pieces[0].shape[0]
    cut = early_rows(rows)
    pack_ref[: rows - cut, :] = pieces[0][cut:, :]
    for k, piece in enumerate(pieces[1:], 1):
        pack_ref[pl.ds(rows * k - cut, rows), :] = piece[...]
    g_pot = sqy_ref[...] - merge_all([ref[...] for ref in parts])
    bias = to_column(lt_ref[...] * LOG2E + g_pot - sqy_ref[...])
    for b in range(tile_ref.shape[1] // LANES):
        lse_ref[pl.ds(b, 1), :] = over_targets(tile_ref[:, pl.ds(b * LANES, LANES)] + bias)


def merge_kernel(one_ref, two_ref, *refs):
    n_pieces = len(refs) // 2
    pieces, (out_ref, pack_ref, *copies) = refs[:n_pieces], refs[n_pieces:]
    out_ref[...] = merge_all([one_ref[...], two_ref[...]])
    rows = pieces[-1].shape[0]
    pack_ref[:rows, :] = pieces[-1][...]
    pack_ref[rows:, :] = pieces[0][: early_rows(rows), :]
    for piece, copy in zip(pieces[:-1], copies):
        copy[...] = piece[...]


def sources_kernel(n_parts, tile_ref, ls_ref, sqx_ref, *refs):
    bias = source_bias(ls_ref, sqx_ref, refs[:n_parts])
    columns = []
    for j in range(tile_ref.shape[0] // LANES):
        peak, total, _ = over_sources(tile_ref, pl.ds(j * LANES, LANES), bias)
        columns.append(peak + jnp.log2(total))
    refs[-1][...] = to_dense(columns)


def last_sources_kernel(n_parts, tile_ref, x_ref, ls_ref, sqx_ref, *refs):
    pieces, (lse_ref, sent_ref, mine_ref, pack_ref) = refs[n_parts:-4], refs[-4:]
    n_shards, n_y, rows, _ = pack_ref.shape
    y = lax.axis_index("row") // 2
    early, late = pieces[:n_y], pieces[n_y:]
    cut = early_rows(rows)
    for j in range(n_y):
        place = y ^ j
        pack_ref[0, place] = early[j][:rows, :]
        pack_ref[1, place, :cut, :] = early[j][rows:, :]
        pack_ref[1, place, cut:, :] = late[j][: rows - cut, :]
        for k in range(2, n_shards):
            pack_ref[k, place] = late[j][pl.ds((k - 1) * rows - cut, rows), :]
    bias = source_bias(ls_ref, sqx_ref, refs[:n_parts])
    x = x_ref[...]
    n_rows = mine_ref.shape[0] // LANES
    core = lax.axis_index("row") % 2
    for out_ref, place in ((sent_ref, 1 - core), (mine_ref, core)):
        columns = []
        for j in range(n_rows):
            at = pl.ds(pl.multiple_of((place * n_rows + j) * LANES, LANES), LANES)
            peak, total, exps = over_sources(tile_ref, at, bias)
            columns.append(peak + jnp.log2(total))
            weights = jnp.concatenate([block.astype(jnp.bfloat16) for block in exps], axis=1)
            mean = jnp.dot(weights, x, preferred_element_type=jnp.float32)
            out_ref[pl.ds(j * LANES, LANES), :] = mean * (1.0 / total)
        lse_ref[pl.ds(place * n_rows, n_rows), :] = to_dense(columns)


def source_bias(ls_ref, sqx_ref, parts):
    f_pot = sqx_ref[...] - merge_all([ref[...] for ref in parts])
    return ls_ref[...] * LOG2E + f_pot - sqx_ref[...]


def over_sources(tile_ref, at, bias):
    scores = [tile_ref[at, pl.ds(b * LANES, LANES)] + bias[b : b + 1, :] for b in range(bias.shape[0])]
    top = scores[0]
    for block in scores[1:]:
        top = jnp.maximum(top, block)
    peak = jnp.max(top, axis=1, keepdims=True)
    exps = [jnp.exp2(block - peak) for block in scores]
    return peak, jnp.sum(sum(exps), axis=1, keepdims=True), exps


def share_kernel(mine_ref, came_ref, total_ref, lse_ref, came_lse_ref, out_ref):
    half = mine_ref.shape[0] // LANES
    at = pl.ds(lax.axis_index("row") % 2 * half, half)
    total = total_ref[at, :]
    share, came_share = to_column(jnp.exp2(lse_ref[at, :] - total)), to_column(jnp.exp2(came_lse_ref[at, :] - total))
    out_ref[...] = mine_ref[...] * share + came_ref[...] * came_share


def add_kernel(one_ref, two_ref, *out_refs):
    rows = out_refs[0].shape[0]
    for k, ref in enumerate(out_refs):
        at = pl.ds(k * rows, rows)
        ref[...] = one_ref[at, :] + two_ref[at, :]


def join_kernel(*refs):
    parts, out_ref = refs[:-1], refs[-1]
    rows = out_ref.shape[0]
    lses = [ref[rows : rows + pl.cdiv(rows, LANES), :LANES] for ref in parts]
    whole = merge_all(lses)
    shares = [to_column(jnp.exp2(lse - whole))[:rows] for lse in lses]
    out_ref[...] = sum(ref[:rows, :] * share for ref, share in zip(parts, shares))


def place_kernel(*refs):
    n = (len(refs) - 2) // 2
    mine, others, out_hbm, sems = refs[:n], refs[n : 2 * n], refs[-2], refs[-1]
    rows = mine[0].shape[0]
    core = lax.axis_index("row") % 2
    copies = []
    for place, pieces in ((core, mine), (1 - core, others)):
        for k, piece in enumerate(pieces):
            at = pl.ds(pl.multiple_of((place * n + k) * rows, rows), rows)
            copies.append(pltpu.make_async_copy(piece, out_hbm.at[at, :], sems.at[len(copies)]))
            copies[-1].start()
    for copy in copies:
        copy.wait()


def scores_kernel(near, x_ref, own_ref, mine_ref, other_ref, y_ref, inner_ref):
    rows = inner_ref.shape[0] // 2
    n_tgt = own_ref.shape[0]
    n_came, n_y, part, _ = mine_ref.shape
    col, core = lax.axis_index("col"), lax.axis_index("row") % 2
    y_ref[:n_tgt, :] = own_ref[...]
    for k in range(n_came):
        for ref, place in ((mine_ref, core), (other_ref, 1 - core)):
            for y in range(n_y):
                start = (k + 1) * n_tgt + (2 * y + place) * part
                y_ref[pl.ds(pl.multiple_of(start, part), part), :] = ref[k, y].astype(jnp.bfloat16)
    blocks = [x_ref[pl.ds(pl.multiple_of((col ^ flip) * rows, rows), rows), :] for flip in (0, near)]
    x = jnp.concatenate(blocks, axis=0)
    unit = scale(x.shape[1])
    for b in range(y_ref.shape[0] // n_tgt):
        at = pl.ds(b * n_tgt, n_tgt)
        inner_ref[:, at] = lax.dot_general(x, y_ref[at, :], NT_DIMS, preferred_element_type=jnp.float32) * (2.0 * unit)


EXTRA = 8


def images(flip, inner_ref, y_ref, bias_refs, scores_ref):
    rows = scores_ref.shape[0]
    n_shards = len(bias_refs)
    n_tgt = y_ref.shape[0] // n_shards
    block = pl.ds(flip * rows, rows)
    peak = jnp.full((rows, 1), -jnp.inf, jnp.float32)
    for k, bias_ref in enumerate(bias_refs[::-1]):
        at = pl.ds(k * n_tgt, n_tgt)
        scores = inner_ref[block, at] + to_row(bias_ref[...])
        scores_ref[:, at] = scores
        peak = jnp.maximum(peak, jnp.max(scores, axis=1, keepdims=True))
    total = jnp.zeros((rows, 1), jnp.float32)
    numer = jnp.zeros((rows, y_ref.shape[1]), jnp.float32)
    for k in range(n_shards):
        at = pl.ds(k * n_tgt, n_tgt)
        plan = jnp.exp2(scores_ref[:, at] - peak)
        total = total + jnp.sum(plan, axis=1, keepdims=True)
        numer = numer + jnp.dot(plan.astype(jnp.bfloat16), y_ref[at, :], preferred_element_type=jnp.float32)
    return numer, total, peak


def lanes_of(column):
    rows = column.shape[0]
    if rows % LANES:
        column = jnp.concatenate([column, jnp.zeros((-rows % LANES, 1), jnp.float32)], axis=0)
    return to_dense([column[b : b + LANES] for b in range(0, column.shape[0], LANES)])


EXTRA = 8


def image_kernel(flip, inner_ref, y_ref, *refs):
    bias_refs, (image_ref, scores_ref) = refs[:-2], refs[-2:]
    numer, total, peak = images(flip, inner_ref, y_ref, bias_refs, scores_ref)
    rows = numer.shape[0]
    lse = lanes_of(peak + jnp.log2(total))
    image_ref[:rows, :] = numer * (1.0 / total)
    image_ref[rows:, :] = jnp.zeros((EXTRA, image_ref.shape[1]), jnp.float32)
    image_ref[rows : rows + lse.shape[0], :LANES] = lse


def swap(value, axis, distance):
    n = lax.axis_size(axis)
    return lax.ppermute(value, axis, [(i, i ^ distance) for i in range(n)])


def bits_of(n):
    return [1 << b for b in range(n.bit_length() - 1)]


def on_device(source, target, log_source_mass, log_target_mass):
    n_src, width = source.shape
    n_tgt = target.shape[0]
    n_col, n_row = lax.axis_size("col"), lax.axis_size("row")
    count = n_src // n_col
    n_x = 1 << (len(bits_of(n_col)) // 2)
    n_z = n_col // n_x
    y_bits = bits_of(n_row)[1:]
    ls = log_source_mass.reshape(-1, LANES)
    lt = log_target_mass.reshape(-1, LANES)
    src_dense, tgt_dense = f32(*ls.shape), f32(*lt.shape)
    half = n_tgt // 2

    part = f32(n_tgt // n_row, width)
    pieces = {0: call(quarter_kernel, part, target)}
    for distance in [bit for bit in bits_of(n_col) if bit > n_x][::-1]:
        pieces |= {k ^ distance: swap(piece, "col", distance) for k, piece in pieces.items()}
    early = swap(pieces[0], "col", 1)

    def along_y(piece):
        held = [piece]
        for distance in y_bits:
            held += [swap(one, "row", distance) for one in held]
        return held

    tile, lse, sqx, sqy = call(
        first_kernel, (f32(n_tgt, n_src), src_dense, src_dense, tgt_dense), target, source, lt
    )
    cut = early_rows(part.shape[0])
    for step in range(ITERS):
        if step > 0:
            apart = [0, 1] + [k for k in pieces if k > 1]
            lse, late = call(
                lambda *refs: targets_kernel(n_row, *refs),
                (src_dense, f32((len(apart) - 2) * part.shape[0] - cut, width)),
                tile, lt, sqy, *parts, *[pieces[k] for k in apart[2:]], early[-1],
            )
            late = along_y(late)
        for distance in bits_of(n_col)[:-1]:
            came = swap(lse, "col", distance)
            if step > 0 or distance != n_x:
                lse = merge_all([lse, came])
                continue
            far = [k for k in pieces if k > 0]
            lse, early, *copies = call(
                merge_kernel,
                (src_dense, f32(part.shape[0] + cut, width), *(part,) * len(far)),
                lse, came, *[pieces[k] for k in far], early,
            )
            early = along_y(early)
            pieces |= dict(zip(far, copies))
            for bit in bits_of(n_x)[::-1]:
                pieces |= {k ^ bit: swap(piece, "col", bit) for k, piece in pieces.items() if k ^ bit != 1}
        parts = [lse, swap(lse, "col", n_col // 2)]
        if step < ITERS - 1:
            lse = call(lambda *refs: sources_kernel(2, *refs), tgt_dense, tile, ls, sqx, *parts)
        else:
            lse, sent, mine, came = call(
                lambda *refs: last_sources_kernel(2, *refs),
                (tgt_dense, f32(half, width), f32(half, width), f32(len(apart) - 1, n_row // 2, *part.shape)),
                tile, source, ls, sqx, *parts, *early, *late,
            )
        parts = [lse] + [swap(lse, "row", k) for k in range(1, n_row)]
    total = merge_all(parts)

    bias = lt * LOG2E + (sqy - total) - sqy
    biases = [bias] + [swap(bias, "col", distance) for distance in apart[1:]]

    mine = call(share_kernel, f32(half, width), mine, swap(sent, "row", 1), total, lse, parts[1])
    rest = bits_of(n_row)[1:]
    for distance in rest[:-1]:
        mine, = call(add_kernel, (f32(half, width),), mine, swap(mine, "row", distance))
    mine_came = swap(mine, "row", rest[-1])

    n_all = len(apart) * n_tgt
    all_y, inner = call(
        lambda *refs: scores_kernel(n_x, *refs),
        (bf16(n_all, width), f32(2 * count, n_all)),
        source, target, came, swap(came, "row", 1),
        limit=32,
    )

    def image(flip):
        return call(
            lambda *refs: image_kernel(flip, *refs),
            f32(count + EXTRA, width),
            inner, all_y, *biases[::-1],
            scratch=[pltpu.VMEM((count, n_all), jnp.float32)],
        )

    came = swap(image(1), "col", n_x)
    own = image(0)
    n_last = 4
    mine = call(add_kernel, (f32(half // n_last, width),) * n_last, mine, mine_came)
    target_image = call(
        place_kernel, f32(n_tgt, width), *mine, *[swap(piece, "row", 1) for piece in mine],
        out_specs=HBM, scratch=[DMA((2 * n_last,))],
    )
    source_image = call(join_kernel, f32(count, width), own, came)
    return source_image, target_image


def solution(mesh):
    in_specs = (P("row", None), P("col", None), P("row"), P("col"))
    out_specs = (P(("row", "col"), None), P("col", None))
    return jax.shard_map(
        on_device, mesh=mesh, in_specs=in_specs, out_specs=out_specs, check_vma=False
    )
```

```python
import math

import jax
import jax.numpy as jnp
from jax import lax
from jax.experimental import pallas as pl
from jax.experimental.pallas import tpu as pltpu
from jax.sharding import PartitionSpec as P

ITERS = 2
BLUR = 0.1
LOG2E = math.log2(math.e)
LANES = 128
NT_DIMS = (((1,), (1,)), ((), ()))
VMEM = pl.BlockSpec(memory_space=pltpu.VMEM)
HBM = pl.BlockSpec(memory_space=pltpu.HBM)
ANY = pl.BlockSpec(memory_space=pl.ANY)
DMA = pltpu.SemaphoreType.DMA


def call(kernel, out_shape, *args, in_specs=None, out_specs=None, scratch=(), limit=24):
    return pl.pallas_call(
        kernel,
        out_shape=out_shape,
        in_specs=in_specs or [VMEM] * len(args),
        out_specs=out_specs or jax.tree.map(lambda _: VMEM, out_shape),
        scratch_shapes=list(scratch),
        compiler_params=pltpu.CompilerParams(vmem_limit_bytes=limit << 20),
    )(*args)


def f32(*shape):
    return jax.ShapeDtypeStruct(shape, jnp.float32)


def bf16(*shape):
    return jax.ShapeDtypeStruct(shape, jnp.bfloat16)


def scale(width):
    return LOG2E / (width * BLUR)


def to_column(dense):
    n = dense.shape[0]
    square = jnp.concatenate([dense, jnp.zeros((LANES - n, LANES), jnp.float32)], axis=0).T
    return jnp.concatenate([square[:, b : b + 1] for b in range(n)], axis=0)


def to_dense(columns):
    lane = lax.broadcasted_iota(jnp.int32, (LANES, LANES), 1)
    square = jnp.zeros((LANES, LANES), jnp.float32)
    for b, column in enumerate(columns):
        square = jnp.where(lane == b, column, square)
    return square.T[: len(columns)]


def to_row(dense):
    return jnp.concatenate([dense[b : b + 1, :] for b in range(dense.shape[0])], axis=1)


def over_targets(scores):
    peak = jnp.max(scores, axis=0, keepdims=True)
    total = jnp.sum(jnp.exp2(scores - peak), axis=0, keepdims=True)
    return peak + jnp.log2(total)


def half_at(ref, place):
    half = ref.shape[0] // 2
    return ref[pl.ds(place * half, half), :]


def merge_all(parts):
    peak = parts[0]
    for part in parts[1:]:
        peak = jnp.maximum(peak, part)
    return peak + jnp.log2(sum(jnp.exp2(part - peak) for part in parts))


def norms(block):
    wide = block.astype(jnp.float32)
    return jnp.sum(wide * wide, axis=1, keepdims=True) * scale(block.shape[1])


def quarter_kernel(y_ref, out_ref):
    rows = out_ref.shape[0]
    out_ref[...] = y_ref[pl.ds(pl.multiple_of(lax.axis_index("row") * rows, rows), rows), :].astype(jnp.float32)


def norms_kernel(x_ref, sqx_ref):
    columns = [norms(x_ref[pl.ds(b, LANES), :]) for b in range(0, x_ref.shape[0], LANES)]
    sqx_ref[...] = to_dense(columns)


def first_kernel(y_ref, x_ref, lt_ref, tile_ref, lse_ref, sqy_ref):
    wide = 256
    y = y_ref[...]
    unit = scale(y.shape[1])
    sqy = norms(y)
    sqy_ref[...] = to_dense([sqy[b : b + LANES] for b in range(0, y.shape[0], LANES)])
    bias = to_column(lt_ref[...]) * LOG2E - sqy
    for b in range(x_ref.shape[0] // wide):
        at = pl.ds(b * wide, wide)
        x = x_ref[at, :]
        tile = lax.dot_general(y, x, NT_DIMS, preferred_element_type=jnp.float32) * (2.0 * unit)
        tile_ref[:, at] = tile
        row = over_targets(tile + bias)
        for c in range(wide // LANES):
            lse_ref[pl.ds(b * (wide // LANES) + c, 1), :] = row[:, c * LANES : (c + 1) * LANES]


def early_rows(rows):
    return rows * 7 // 128 * 8


def targets_kernel(n_parts, tile_ref, lt_ref, sqy_ref, *refs):
    parts, pieces, (lse_ref, pack_ref) = refs[:n_parts], refs[n_parts:-3], refs[-2:]
    rows = pieces[0].shape[0]
    cut = early_rows(rows)
    pack_ref[: rows - cut, :] = pieces[0][cut:, :]
    for k, piece in enumerate(pieces[1:], 1):
        pack_ref[pl.ds(rows * k - cut, rows), :] = piece[...]
    g_pot = sqy_ref[...] - merge_all([ref[...] for ref in parts])
    bias = to_column(lt_ref[...] * LOG2E + g_pot - sqy_ref[...])
    for b in range(tile_ref.shape[1] // LANES):
        lse_ref[pl.ds(b, 1), :] = over_targets(tile_ref[:, pl.ds(b * LANES, LANES)] + bias)


def merge_kernel(one_ref, two_ref, *refs):
    n_pieces = len(refs) // 2
    pieces, (out_ref, pack_ref, *copies) = refs[:n_pieces], refs[n_pieces:]
    out_ref[...] = merge_all([one_ref[...], two_ref[...]])
    rows = pieces[-1].shape[0]
    pack_ref[:rows, :] = pieces[-1][...]
    pack_ref[rows:, :] = pieces[0][: early_rows(rows), :]
    for piece, copy in zip(pieces[:-1], copies):
        copy[...] = piece[...]


def sources_kernel(n_parts, tile_ref, ls_ref, sqx_ref, *refs):
    bias = source_bias(ls_ref, sqx_ref, refs[:n_parts])
    columns = []
    for j in range(tile_ref.shape[0] // LANES):
        peak, total, _ = over_sources(tile_ref, pl.ds(j * LANES, LANES), bias)
        columns.append(peak + jnp.log2(total))
    refs[-1][...] = to_dense(columns)


def last_sources_kernel(n_parts, tile_ref, x_ref, ls_ref, sqx_ref, *refs):
    pieces, (lse_ref, sent_ref, mine_ref, pack_ref) = refs[n_parts:-4], refs[-4:]
    n_shards, n_y, rows, _ = pack_ref.shape
    y = lax.axis_index("row") // 2
    early, late = pieces[:n_y], pieces[n_y:]
    cut = early_rows(rows)
    for j in range(n_y):
        place = y ^ j
        pack_ref[0, place] = early[j][:rows, :]
        pack_ref[1, place, :cut, :] = early[j][rows:, :]
        pack_ref[1, place, cut:, :] = late[j][: rows - cut, :]
        for k in range(2, n_shards):
            pack_ref[k, place] = late[j][pl.ds((k - 1) * rows - cut, rows), :]
    bias = source_bias(ls_ref, sqx_ref, refs[:n_parts])
    x = x_ref[...]
    n_rows = mine_ref.shape[0] // LANES
    core = lax.axis_index("row") % 2
    for out_ref, place in ((sent_ref, 1 - core), (mine_ref, core)):
        columns = []
        for j in range(n_rows):
            at = pl.ds(pl.multiple_of((place * n_rows + j) * LANES, LANES), LANES)
            peak, total, exps = over_sources(tile_ref, at, bias)
            columns.append(peak + jnp.log2(total))
            weights = jnp.concatenate([block.astype(jnp.bfloat16) for block in exps], axis=1)
            mean = jnp.dot(weights, x, preferred_element_type=jnp.float32)
            out_ref[pl.ds(j * LANES, LANES), :] = mean * (1.0 / total)
        lse_ref[pl.ds(place * n_rows, n_rows), :] = to_dense(columns)


def source_bias(ls_ref, sqx_ref, parts):
    f_pot = sqx_ref[...] - merge_all([ref[...] for ref in parts])
    return ls_ref[...] * LOG2E + f_pot - sqx_ref[...]


def over_sources(tile_ref, at, bias):
    scores = [tile_ref[at, pl.ds(b * LANES, LANES)] + bias[b : b + 1, :] for b in range(bias.shape[0])]
    top = scores[0]
    for block in scores[1:]:
        top = jnp.maximum(top, block)
    peak = jnp.max(top, axis=1, keepdims=True)
    exps = [jnp.exp2(block - peak) for block in scores]
    return peak, jnp.sum(sum(exps), axis=1, keepdims=True), exps


def share_kernel(mine_ref, came_ref, total_ref, lse_ref, came_lse_ref, out_ref):
    half = mine_ref.shape[0] // LANES
    at = pl.ds(lax.axis_index("row") % 2 * half, half)
    total = total_ref[at, :]
    share, came_share = to_column(jnp.exp2(lse_ref[at, :] - total)), to_column(jnp.exp2(came_lse_ref[at, :] - total))
    out_ref[...] = mine_ref[...] * share + came_ref[...] * came_share


def add_kernel(one_ref, two_ref, *out_refs):
    rows = out_refs[0].shape[0]
    for k, ref in enumerate(out_refs):
        at = pl.ds(k * rows, rows)
        ref[...] = one_ref[at, :] + two_ref[at, :]


def join_kernel(*refs):
    parts, out_ref = refs[:-1], refs[-1]
    rows = out_ref.shape[0]
    lses = [ref[rows : rows + pl.cdiv(rows, LANES), :LANES] for ref in parts]
    whole = merge_all(lses)
    shares = [to_column(jnp.exp2(lse - whole))[:rows] for lse in lses]
    out_ref[...] = sum(ref[:rows, :] * share for ref, share in zip(parts, shares))


def place_kernel(*refs):
    n = (len(refs) - 2) // 2
    mine, others, out_hbm, sems = refs[:n], refs[n : 2 * n], refs[-2], refs[-1]
    rows = mine[0].shape[0]
    core = lax.axis_index("row") % 2
    copies = []
    for place, pieces in ((core, mine), (1 - core, others)):
        for k, piece in enumerate(pieces):
            at = pl.ds(pl.multiple_of((place * n + k) * rows, rows), rows)
            copies.append(pltpu.make_async_copy(piece, out_hbm.at[at, :], sems.at[len(copies)]))
            copies[-1].start()
    for copy in copies:
        copy.wait()


def scores_kernel(near, x_ref, own_ref, mine_ref, other_ref, y_ref, inner_ref):
    rows = inner_ref.shape[0] // 2
    n_tgt = own_ref.shape[0]
    n_came, n_y, part, _ = mine_ref.shape
    col, core = lax.axis_index("col"), lax.axis_index("row") % 2
    y_ref[:n_tgt, :] = own_ref[...]
    for k in range(n_came):
        for ref, place in ((mine_ref, core), (other_ref, 1 - core)):
            for y in range(n_y):
                start = (k + 1) * n_tgt + (2 * y + place) * part
                y_ref[pl.ds(pl.multiple_of(start, part), part), :] = ref[k, y].astype(jnp.bfloat16)
    blocks = [x_ref[pl.ds(pl.multiple_of((col ^ flip) * rows, rows), rows), :] for flip in (0, near)]
    x = jnp.concatenate(blocks, axis=0)
    unit = scale(x.shape[1])
    for b in range(y_ref.shape[0] // n_tgt):
        at = pl.ds(b * n_tgt, n_tgt)
        inner_ref[:, at] = lax.dot_general(x, y_ref[at, :], NT_DIMS, preferred_element_type=jnp.float32) * (2.0 * unit)


EXTRA = 8


def images(flip, inner_ref, y_ref, bias_refs, scores_ref):
    rows = scores_ref.shape[0]
    n_shards = len(bias_refs)
    n_tgt = y_ref.shape[0] // n_shards
    block = pl.ds(flip * rows, rows)
    peak = jnp.full((rows, 1), -jnp.inf, jnp.float32)
    for k, bias_ref in enumerate(bias_refs[::-1]):
        at = pl.ds(k * n_tgt, n_tgt)
        scores = inner_ref[block, at] + to_row(bias_ref[...])
        scores_ref[:, at] = scores
        peak = jnp.maximum(peak, jnp.max(scores, axis=1, keepdims=True))
    total = jnp.zeros((rows, 1), jnp.float32)
    numer = jnp.zeros((rows, y_ref.shape[1]), jnp.float32)
    for k in range(n_shards):
        at = pl.ds(k * n_tgt, n_tgt)
        plan = jnp.exp2(scores_ref[:, at] - peak)
        total = total + jnp.sum(plan, axis=1, keepdims=True)
        numer = numer + jnp.dot(plan.astype(jnp.bfloat16), y_ref[at, :], preferred_element_type=jnp.float32)
    return numer, total, peak


def lanes_of(column):
    rows = column.shape[0]
    if rows % LANES:
        column = jnp.concatenate([column, jnp.zeros((-rows % LANES, 1), jnp.float32)], axis=0)
    return to_dense([column[b : b + LANES] for b in range(0, column.shape[0], LANES)])


EXTRA = 8


def image_kernel(flip, inner_ref, y_ref, *refs):
    bias_refs, (image_ref, scores_ref) = refs[:-2], refs[-2:]
    numer, total, peak = images(flip, inner_ref, y_ref, bias_refs, scores_ref)
    rows = numer.shape[0]
    lse = lanes_of(peak + jnp.log2(total))
    image_ref[:rows, :] = numer * (1.0 / total)
    image_ref[rows:, :] = jnp.zeros((EXTRA, image_ref.shape[1]), jnp.float32)
    image_ref[rows : rows + lse.shape[0], :LANES] = lse


def swap(value, axis, distance):
    n = lax.axis_size(axis)
    return lax.ppermute(value, axis, [(i, i ^ distance) for i in range(n)])


def bits_of(n):
    return [1 << b for b in range(n.bit_length() - 1)]


def on_device(source, target, log_source_mass, log_target_mass):
    n_src, width = source.shape
    n_tgt = target.shape[0]
    n_col, n_row = lax.axis_size("col"), lax.axis_size("row")
    count = n_src // n_col
    n_x = 1 << (len(bits_of(n_col)) // 2)
    n_z = n_col // n_x
    y_bits = bits_of(n_row)[1:]
    ls = log_source_mass.reshape(-1, LANES)
    lt = log_target_mass.reshape(-1, LANES)
    src_dense, tgt_dense = f32(*ls.shape), f32(*lt.shape)
    half = n_tgt // 2

    part = f32(n_tgt // n_row, width)
    pieces = {0: call(quarter_kernel, part, target)}
    for distance in [bit for bit in bits_of(n_col) if bit > n_x][::-1]:
        pieces |= {k ^ distance: swap(piece, "col", distance) for k, piece in pieces.items()}
    early = swap(pieces[0], "col", 1)

    def along_y(piece):
        held = [piece]
        for distance in y_bits:
            held += [swap(one, "row", distance) for one in held]
        return held

    tile, lse, sqy = call(first_kernel, (f32(n_tgt, n_src), src_dense, tgt_dense), target, source, lt)
    sqx = call(norms_kernel, src_dense, source)
    cut = early_rows(part.shape[0])
    for step in range(ITERS):
        if step > 0:
            apart = [0, 1] + [k for k in pieces if k > 1]
            lse, late = call(
                lambda *refs: targets_kernel(n_row, *refs),
                (src_dense, f32((len(apart) - 2) * part.shape[0] - cut, width)),
                tile, lt, sqy, *parts, *[pieces[k] for k in apart[2:]], early[-1],
            )
            late = along_y(late)
        for distance in bits_of(n_col)[:-1]:
            came = swap(lse, "col", distance)
            if step > 0 or distance != n_x:
                lse = merge_all([lse, came])
                continue
            far = [k for k in pieces if k > 0]
            lse, early, *copies = call(
                merge_kernel,
                (src_dense, f32(part.shape[0] + cut, width), *(part,) * len(far)),
                lse, came, *[pieces[k] for k in far], early,
            )
            early = along_y(early)
            pieces |= dict(zip(far, copies))
            for bit in bits_of(n_x)[::-1]:
                pieces |= {k ^ bit: swap(piece, "col", bit) for k, piece in pieces.items() if k ^ bit != 1}
        parts = [lse, swap(lse, "col", n_col // 2)]
        if step < ITERS - 1:
            lse = call(lambda *refs: sources_kernel(2, *refs), tgt_dense, tile, ls, sqx, *parts)
        else:
            lse, sent, mine, came = call(
                lambda *refs: last_sources_kernel(2, *refs),
                (tgt_dense, f32(half, width), f32(half, width), f32(len(apart) - 1, n_row // 2, *part.shape)),
                tile, source, ls, sqx, *parts, *early, *late,
            )
        parts = [lse] + [swap(lse, "row", k) for k in range(1, n_row)]
    total = merge_all(parts)

    bias = lt * LOG2E + (sqy - total) - sqy
    biases = [bias] + [swap(bias, "col", distance) for distance in apart[1:]]

    mine = call(share_kernel, f32(half, width), mine, swap(sent, "row", 1), total, lse, parts[1])
    rest = bits_of(n_row)[1:]
    for distance in rest[:-1]:
        mine, = call(add_kernel, (f32(half, width),), mine, swap(mine, "row", distance))
    mine_came = swap(mine, "row", rest[-1])

    n_all = len(apart) * n_tgt
    all_y, inner = call(
        lambda *refs: scores_kernel(n_x, *refs),
        (bf16(n_all, width), f32(2 * count, n_all)),
        source, target, came, swap(came, "row", 1),
        limit=32,
    )

    def image(flip):
        return call(
            lambda *refs: image_kernel(flip, *refs),
            f32(count + EXTRA, width),
            inner, all_y, *biases[::-1],
            scratch=[pltpu.VMEM((count, n_all), jnp.float32)],
        )

    came = swap(image(1), "col", n_x)
    own = image(0)
    n_last = 4
    mine = call(add_kernel, (f32(half // n_last, width),) * n_last, mine, mine_came)
    target_image = call(
        place_kernel, f32(n_tgt, width), *mine, *[swap(piece, "row", 1) for piece in mine],
        out_specs=HBM, scratch=[DMA((2 * n_last,))],
    )
    source_image = call(join_kernel, f32(count, width), own, came)
    return source_image, target_image


def solution(mesh):
    in_specs = (P("row", None), P("col", None), P("row"), P("col"))
    out_specs = (P(("row", "col"), None), P("col", None))
    return jax.shard_map(
        on_device, mesh=mesh, in_specs=in_specs, out_specs=out_specs, check_vma=False
    )
```

```python
import math

import jax
import jax.numpy as jnp
from jax import lax
from jax.experimental import pallas as pl
from jax.experimental.pallas import tpu as pltpu
from jax.sharding import PartitionSpec as P

ITERS = 2
BLUR = 0.1
LOG2E = math.log2(math.e)
LANES = 128
NT_DIMS = (((1,), (1,)), ((), ()))
VMEM = pl.BlockSpec(memory_space=pltpu.VMEM)
HBM = pl.BlockSpec(memory_space=pltpu.HBM)
ANY = pl.BlockSpec(memory_space=pl.ANY)
DMA = pltpu.SemaphoreType.DMA


def call(kernel, out_shape, *args, in_specs=None, out_specs=None, scratch=(), limit=24):
    return pl.pallas_call(
        kernel,
        out_shape=out_shape,
        in_specs=in_specs or [VMEM] * len(args),
        out_specs=out_specs or jax.tree.map(lambda _: VMEM, out_shape),
        scratch_shapes=list(scratch),
        compiler_params=pltpu.CompilerParams(vmem_limit_bytes=limit << 20),
    )(*args)


def f32(*shape):
    return jax.ShapeDtypeStruct(shape, jnp.float32)


def bf16(*shape):
    return jax.ShapeDtypeStruct(shape, jnp.bfloat16)


def scale(width):
    return LOG2E / (width * BLUR)


def to_column(dense):
    n = dense.shape[0]
    square = jnp.concatenate([dense, jnp.zeros((LANES - n, LANES), jnp.float32)], axis=0).T
    return jnp.concatenate([square[:, b : b + 1] for b in range(n)], axis=0)


def to_dense(columns):
    lane = lax.broadcasted_iota(jnp.int32, (LANES, LANES), 1)
    square = jnp.zeros((LANES, LANES), jnp.float32)
    for b, column in enumerate(columns):
        square = jnp.where(lane == b, column, square)
    return square.T[: len(columns)]


def to_row(dense):
    return jnp.concatenate([dense[b : b + 1, :] for b in range(dense.shape[0])], axis=1)


def over_targets(scores):
    peak = jnp.max(scores, axis=0, keepdims=True)
    total = jnp.sum(jnp.exp2(scores - peak), axis=0, keepdims=True)
    return peak + jnp.log2(total)


def half_at(ref, place):
    half = ref.shape[0] // 2
    return ref[pl.ds(place * half, half), :]


def merge_all(parts):
    peak = parts[0]
    for part in parts[1:]:
        peak = jnp.maximum(peak, part)
    return peak + jnp.log2(sum(jnp.exp2(part - peak) for part in parts))


def norms(block):
    wide = block.astype(jnp.float32)
    return jnp.sum(wide * wide, axis=1, keepdims=True) * scale(block.shape[1])


def quarter_kernel(y_ref, out_ref):
    rows = out_ref.shape[0]
    out_ref[...] = y_ref[pl.ds(pl.multiple_of(lax.axis_index("row") * rows, rows), rows), :].astype(jnp.float32)


def norms_kernel(x_ref, sqx_ref):
    columns = [norms(x_ref[pl.ds(b, LANES), :]) for b in range(0, x_ref.shape[0], LANES)]
    sqx_ref[...] = to_dense(columns)


def first_kernel(y_ref, x_ref, lt_ref, tile_ref, lse_ref, sqy_ref):
    wide = 256
    y = y_ref[...]
    unit = scale(y.shape[1])
    sqy = norms(y)
    sqy_ref[...] = to_dense([sqy[b : b + LANES] for b in range(0, y.shape[0], LANES)])
    bias = to_column(lt_ref[...]) * LOG2E - sqy
    for b in range(x_ref.shape[0] // wide):
        at = pl.ds(b * wide, wide)
        x = x_ref[at, :]
        tile = lax.dot_general(y, x, NT_DIMS, preferred_element_type=jnp.float32) * (2.0 * unit)
        tile_ref[:, at] = tile
        row = over_targets(tile + bias)
        for c in range(wide // LANES):
            lse_ref[pl.ds(b * (wide // LANES) + c, 1), :] = row[:, c * LANES : (c + 1) * LANES]


def early_rows(rows):
    return rows // 2


def targets_kernel(n_parts, tile_ref, lt_ref, sqy_ref, *refs):
    parts, pieces, (lse_ref, pack_ref) = refs[:n_parts], refs[n_parts:-3], refs[-2:]
    rows = pieces[0].shape[0]
    cut = early_rows(rows)
    pack_ref[: rows - cut, :] = pieces[0][cut:, :]
    for k, piece in enumerate(pieces[1:], 1):
        pack_ref[pl.ds(rows * k - cut, rows), :] = piece[...]
    g_pot = sqy_ref[...] - merge_all([ref[...] for ref in parts])
    bias = to_column(lt_ref[...] * LOG2E + g_pot - sqy_ref[...])
    for b in range(tile_ref.shape[1] // LANES):
        lse_ref[pl.ds(b, 1), :] = over_targets(tile_ref[:, pl.ds(b * LANES, LANES)] + bias)


def merge_kernel(n_parts, *refs):
    parts, refs = refs[:n_parts], refs[n_parts:]
    n_pieces = len(refs) // 2
    pieces, (out_ref, pack_ref, *copies) = refs[:n_pieces], refs[n_pieces:]
    out_ref[...] = merge_all([ref[...] for ref in parts])
    rows = pieces[-1].shape[0]
    pack_ref[:rows, :] = pieces[-1][...]
    pack_ref[rows:, :] = pieces[0][: early_rows(rows), :]
    for piece, copy in zip(pieces[:-1], copies):
        copy[...] = piece[...]


def sources_kernel(n_parts, tile_ref, ls_ref, sqx_ref, *refs):
    bias = source_bias(ls_ref, sqx_ref, refs[:n_parts])
    columns = []
    for j in range(tile_ref.shape[0] // LANES):
        peak, total, _ = over_sources(tile_ref, pl.ds(j * LANES, LANES), bias)
        columns.append(peak + jnp.log2(total))
    refs[-1][...] = to_dense(columns)


def last_sources_kernel(n_parts, tile_ref, x_ref, ls_ref, sqx_ref, *refs):
    pieces, (lse_ref, sent_ref, mine_ref, pack_ref) = refs[n_parts:-4], refs[-4:]
    n_shards, n_y, rows, _ = pack_ref.shape
    y = lax.axis_index("row") // 2
    early, late = pieces[:n_y], pieces[n_y:]
    cut = early_rows(rows)
    for j in range(n_y):
        place = y ^ j
        pack_ref[0, place] = early[j][:rows, :]
        pack_ref[1, place, :cut, :] = early[j][rows:, :]
        pack_ref[1, place, cut:, :] = late[j][: rows - cut, :]
        for k in range(2, n_shards):
            pack_ref[k, place] = late[j][pl.ds((k - 1) * rows - cut, rows), :]
    bias = source_bias(ls_ref, sqx_ref, refs[:n_parts])
    x = x_ref[...]
    n_rows = mine_ref.shape[0] // LANES
    core = lax.axis_index("row") % 2
    for out_ref, place in ((sent_ref, 1 - core), (mine_ref, core)):
        columns, totals, weights = [], [], []
        for j in range(n_rows):
            at = pl.ds(pl.multiple_of((place * n_rows + j) * LANES, LANES), LANES)
            peak, total, exps = over_sources(tile_ref, at, bias)
            columns.append(peak + jnp.log2(total))
            totals.append(total)
            weights.append(jnp.concatenate([block.astype(jnp.bfloat16) for block in exps], axis=1))
        mean = jnp.dot(jnp.concatenate(weights, axis=0), x, preferred_element_type=jnp.float32)
        out_ref[...] = mean * (1.0 / jnp.concatenate(totals, axis=0))
        lse_ref[pl.ds(place * n_rows, n_rows), :] = to_dense(columns)


def source_bias(ls_ref, sqx_ref, parts):
    f_pot = sqx_ref[...] - merge_all([ref[...] for ref in parts])
    return ls_ref[...] * LOG2E + f_pot - sqx_ref[...]


def over_sources(tile_ref, at, bias):
    scores = [tile_ref[at, pl.ds(b * LANES, LANES)] + bias[b : b + 1, :] for b in range(bias.shape[0])]
    top = scores[0]
    for block in scores[1:]:
        top = jnp.maximum(top, block)
    peak = jnp.max(top, axis=1, keepdims=True)
    exps = [jnp.exp2(block - peak) for block in scores]
    return peak, jnp.sum(sum(exps), axis=1, keepdims=True), exps


def share_kernel(mine_ref, came_ref, total_ref, lse_ref, came_lse_ref, out_ref):
    half = mine_ref.shape[0] // LANES
    at = pl.ds(lax.axis_index("row") % 2 * half, half)
    total = total_ref[at, :]
    share, came_share = to_column(jnp.exp2(lse_ref[at, :] - total)), to_column(jnp.exp2(came_lse_ref[at, :] - total))
    out_ref[...] = mine_ref[...] * share + came_ref[...] * came_share


def add_kernel(one_ref, two_ref, *out_refs):
    rows = out_refs[0].shape[0]
    for k, ref in enumerate(out_refs):
        at = pl.ds(k * rows, rows)
        ref[...] = one_ref[at, :] + two_ref[at, :]


def join_kernel(*refs):
    parts, out_ref = refs[:-1], refs[-1]
    rows = out_ref.shape[0]
    lses = [ref[rows : rows + pl.cdiv(rows, LANES), :LANES] for ref in parts]
    whole = merge_all(lses)
    shares = [to_column(jnp.exp2(lse - whole))[:rows] for lse in lses]
    out_ref[...] = sum(ref[:rows, :] * share for ref, share in zip(parts, shares))


def place_kernel(*refs):
    n = (len(refs) - 2) // 2
    mine, others, out_hbm, sems = refs[:n], refs[n : 2 * n], refs[-2], refs[-1]
    rows = mine[0].shape[0]
    core = lax.axis_index("row") % 2
    copies = []
    for place, pieces in ((core, mine), (1 - core, others)):
        for k, piece in enumerate(pieces):
            at = pl.ds(pl.multiple_of((place * n + k) * rows, rows), rows)
            copies.append(pltpu.make_async_copy(piece, out_hbm.at[at, :], sems.at[len(copies)]))
            copies[-1].start()
    for copy in copies:
        copy.wait()


def scores_kernel(near, x_ref, own_ref, mine_ref, other_ref, y_ref, inner_ref):
    rows = inner_ref.shape[0] // 2
    n_tgt = own_ref.shape[0]
    n_came, n_y, part, _ = mine_ref.shape
    col, core = lax.axis_index("col"), lax.axis_index("row") % 2
    y_ref[:n_tgt, :] = own_ref[...]
    for k in range(n_came):
        for ref, place in ((mine_ref, core), (other_ref, 1 - core)):
            for y in range(n_y):
                start = (k + 1) * n_tgt + (2 * y + place) * part
                y_ref[pl.ds(pl.multiple_of(start, part), part), :] = ref[k, y].astype(jnp.bfloat16)
    blocks = [x_ref[pl.ds(pl.multiple_of((col ^ flip) * rows, rows), rows), :] for flip in (0, near)]
    x = jnp.concatenate(blocks, axis=0)
    unit = scale(x.shape[1])
    for b in range(y_ref.shape[0] // n_tgt):
        at = pl.ds(b * n_tgt, n_tgt)
        inner_ref[:, at] = lax.dot_general(x, y_ref[at, :], NT_DIMS, preferred_element_type=jnp.float32) * (2.0 * unit)


EXTRA = 8


def images(flip, inner_ref, y_ref, bias_refs, scores_ref):
    rows = scores_ref.shape[0]
    n_shards = len(bias_refs)
    n_tgt = y_ref.shape[0] // n_shards
    block = pl.ds(flip * rows, rows)
    peak = jnp.full((rows, 1), -jnp.inf, jnp.float32)
    for k, bias_ref in enumerate(bias_refs[::-1]):
        at = pl.ds(k * n_tgt, n_tgt)
        scores = inner_ref[block, at] + to_row(bias_ref[...])
        scores_ref[:, at] = scores
        peak = jnp.maximum(peak, jnp.max(scores, axis=1, keepdims=True))
    total = jnp.zeros((rows, 1), jnp.float32)
    numer = jnp.zeros((rows, y_ref.shape[1]), jnp.float32)
    for k in range(n_shards):
        at = pl.ds(k * n_tgt, n_tgt)
        plan = jnp.exp2(scores_ref[:, at] - peak)
        total = total + jnp.sum(plan, axis=1, keepdims=True)
        numer = numer + jnp.dot(plan.astype(jnp.bfloat16), y_ref[at, :], preferred_element_type=jnp.float32)
    return numer, total, peak


def lanes_of(column):
    rows = column.shape[0]
    if rows % LANES:
        column = jnp.concatenate([column, jnp.zeros((-rows % LANES, 1), jnp.float32)], axis=0)
    return to_dense([column[b : b + LANES] for b in range(0, column.shape[0], LANES)])


EXTRA = 8


def image_kernel(flip, inner_ref, y_ref, *refs):
    bias_refs, (image_ref, scores_ref) = refs[:-2], refs[-2:]
    numer, total, peak = images(flip, inner_ref, y_ref, bias_refs, scores_ref)
    rows = numer.shape[0]
    lse = lanes_of(peak + jnp.log2(total))
    image_ref[:rows, :] = numer * (1.0 / total)
    image_ref[rows:, :] = jnp.zeros((EXTRA, image_ref.shape[1]), jnp.float32)
    image_ref[rows : rows + lse.shape[0], :LANES] = lse


def swap(value, axis, distance):
    n = lax.axis_size(axis)
    return lax.ppermute(value, axis, [(i, i ^ distance) for i in range(n)])


def bits_of(n):
    return [1 << b for b in range(n.bit_length() - 1)]


def on_device(source, target, log_source_mass, log_target_mass):
    n_src, width = source.shape
    n_tgt = target.shape[0]
    n_col, n_row = lax.axis_size("col"), lax.axis_size("row")
    count = n_src // n_col
    n_x = 1 << (len(bits_of(n_col)) // 2)
    n_z = n_col // n_x
    y_bits = bits_of(n_row)[1:]
    ls = log_source_mass.reshape(-1, LANES)
    lt = log_target_mass.reshape(-1, LANES)
    src_dense, tgt_dense = f32(*ls.shape), f32(*lt.shape)
    half = n_tgt // 2

    part = f32(n_tgt // n_row, width)
    pieces = {0: call(quarter_kernel, part, target)}
    for distance in [bit for bit in bits_of(n_col) if bit > n_x][::-1]:
        pieces |= {k ^ distance: swap(piece, "col", distance) for k, piece in pieces.items()}
    early = swap(pieces[0], "col", 1)

    def along_y(piece):
        held = [piece]
        for distance in y_bits:
            held += [swap(one, "row", distance) for one in held]
        return held

    tile, lse, sqy = call(first_kernel, (f32(n_tgt, n_src), src_dense, tgt_dense), target, source, lt)
    sqx = call(norms_kernel, src_dense, source)
    cut = early_rows(part.shape[0])
    for step in range(ITERS):
        if step > 0:
            apart = [0, 1] + [k for k in pieces if k > 1]
            lse, late = call(
                lambda *refs: targets_kernel(n_row, *refs),
                (src_dense, f32((len(apart) - 2) * part.shape[0] - cut, width)),
                tile, lt, sqy, *parts, *[pieces[k] for k in apart[2:]], early[-1],
            )
            late = along_y(late)
        if step > 0:
            for distance in bits_of(2 * n_x):
                lse = merge_all([lse, swap(lse, "col", distance)])
        else:
            near = [lse] + [swap(lse, "col", distance) for distance in range(2 * n_x - 1, 0, -1)]
            far = [k for k in pieces if k > 0]
            lse, early, *copies = call(
                lambda *refs: merge_kernel(2 * n_x, *refs),
                (src_dense, f32(part.shape[0] + cut, width), *(part,) * len(far)),
                *near, *[pieces[k] for k in far], early,
            )
            early = along_y(early)
            pieces |= dict(zip(far, copies))
            for bit in bits_of(n_x)[::-1]:
                pieces |= {k ^ bit: swap(piece, "col", bit) for k, piece in pieces.items() if k ^ bit != 1}
        for distance in [bit for bit in bits_of(n_col) if bit > n_x][:-1]:
            lse = merge_all([lse, swap(lse, "col", distance)])
        parts = [lse, swap(lse, "col", n_col // 2)]
        if step < ITERS - 1:
            lse = call(lambda *refs: sources_kernel(2, *refs), tgt_dense, tile, ls, sqx, *parts)
        else:
            lse, sent, mine, came = call(
                lambda *refs: last_sources_kernel(2, *refs),
                (tgt_dense, f32(half, width), f32(half, width), f32(len(apart) - 1, n_row // 2, *part.shape)),
                tile, source, ls, sqx, *parts, *early, *late,
            )
        parts = [lse] + [swap(lse, "row", k) for k in range(1, n_row)]
    total = merge_all(parts)

    bias = lt * LOG2E + (sqy - total) - sqy
    biases = [bias] + [swap(bias, "col", distance) for distance in apart[1:]]

    mine = call(share_kernel, f32(half, width), mine, swap(sent, "row", 1), total, lse, parts[1])
    rest = bits_of(n_row)[1:]
    for distance in rest[:-1]:
        mine, = call(add_kernel, (f32(half, width),), mine, swap(mine, "row", distance))
    mine_came = swap(mine, "row", rest[-1])

    n_all = len(apart) * n_tgt
    all_y, inner = call(
        lambda *refs: scores_kernel(n_x, *refs),
        (bf16(n_all, width), f32(2 * count, n_all)),
        source, target, came, swap(came, "row", 1),
        limit=32,
    )

    def image(flip):
        return call(
            lambda *refs: image_kernel(flip, *refs),
            f32(count + EXTRA, width),
            inner, all_y, *biases[::-1],
            scratch=[pltpu.VMEM((count, n_all), jnp.float32)],
        )

    came = swap(image(1), "col", n_x)
    own = image(0)
    n_last = 4
    mine = call(add_kernel, (f32(half // n_last, width),) * n_last, mine, mine_came)
    target_image = call(
        place_kernel, f32(n_tgt, width), *mine, *[swap(piece, "row", 1) for piece in mine],
        out_specs=HBM, scratch=[DMA((2 * n_last,))],
    )
    source_image = call(join_kernel, f32(count, width), own, came)
    return source_image, target_image


def solution(mesh):
    in_specs = (P("row", None), P("col", None), P("row"), P("col"))
    out_specs = (P(("row", "col"), None), P("col", None))
    return jax.shard_map(
        on_device, mesh=mesh, in_specs=in_specs, out_specs=out_specs, check_vma=False
    )
```

```python
import math

import jax
import jax.numpy as jnp
from jax import lax
from jax.experimental import pallas as pl
from jax.experimental.pallas import tpu as pltpu
from jax.sharding import PartitionSpec as P

ITERS = 2
BLUR = 0.1
LOG2E = math.log2(math.e)
LANES = 128
NT_DIMS = (((1,), (1,)), ((), ()))
VMEM = pl.BlockSpec(memory_space=pltpu.VMEM)
HBM = pl.BlockSpec(memory_space=pltpu.HBM)
ANY = pl.BlockSpec(memory_space=pl.ANY)
DMA = pltpu.SemaphoreType.DMA


def call(kernel, out_shape, *args, in_specs=None, out_specs=None, scratch=(), limit=24):
    return pl.pallas_call(
        kernel,
        out_shape=out_shape,
        in_specs=in_specs or [VMEM] * len(args),
        out_specs=out_specs or jax.tree.map(lambda _: VMEM, out_shape),
        scratch_shapes=list(scratch),
        compiler_params=pltpu.CompilerParams(vmem_limit_bytes=limit << 20),
    )(*args)


def f32(*shape):
    return jax.ShapeDtypeStruct(shape, jnp.float32)


def bf16(*shape):
    return jax.ShapeDtypeStruct(shape, jnp.bfloat16)


def scale(width):
    return LOG2E / (width * BLUR)


def to_column(dense):
    n = dense.shape[0]
    square = jnp.concatenate([dense, jnp.zeros((LANES - n, LANES), jnp.float32)], axis=0).T
    return jnp.concatenate([square[:, b : b + 1] for b in range(n)], axis=0)


def to_dense(columns):
    lane = lax.broadcasted_iota(jnp.int32, (LANES, LANES), 1)
    square = jnp.zeros((LANES, LANES), jnp.float32)
    for b, column in enumerate(columns):
        square = jnp.where(lane == b, column, square)
    return square.T[: len(columns)]


def to_row(dense):
    return jnp.concatenate([dense[b : b + 1, :] for b in range(dense.shape[0])], axis=1)


def over_targets(scores):
    peak = jnp.max(scores, axis=0, keepdims=True)
    total = jnp.sum(jnp.exp2(scores - peak), axis=0, keepdims=True)
    return peak + jnp.log2(total)


def half_at(ref, place):
    half = ref.shape[0] // 2
    return ref[pl.ds(place * half, half), :]


def merge_all(parts):
    peak = parts[0]
    for part in parts[1:]:
        peak = jnp.maximum(peak, part)
    return peak + jnp.log2(sum(jnp.exp2(part - peak) for part in parts))


def norms(block):
    wide = block.astype(jnp.float32)
    return jnp.sum(wide * wide, axis=1, keepdims=True) * scale(block.shape[1])


def quarter_kernel(y_ref, out_ref):
    rows = out_ref.shape[0]
    out_ref[...] = y_ref[pl.ds(pl.multiple_of(lax.axis_index("row") * rows, rows), rows), :].astype(jnp.float32)


def norms_kernel(x_ref, sqx_ref):
    columns = [norms(x_ref[pl.ds(b, LANES), :]) for b in range(0, x_ref.shape[0], LANES)]
    sqx_ref[...] = to_dense(columns)


def first_kernel(y_ref, x_ref, lt_ref, tile_ref, lse_ref, sqy_ref):
    wide = 256
    y = y_ref[...]
    unit = scale(y.shape[1])
    sqy = norms(y)
    sqy_ref[...] = to_dense([sqy[b : b + LANES] for b in range(0, y.shape[0], LANES)])
    bias = to_column(lt_ref[...]) * LOG2E - sqy
    for b in range(x_ref.shape[0] // wide):
        at = pl.ds(b * wide, wide)
        x = x_ref[at, :]
        tile = lax.dot_general(y, x, NT_DIMS, preferred_element_type=jnp.float32) * (2.0 * unit)
        tile_ref[:, at] = tile
        row = over_targets(tile + bias)
        for c in range(wide // LANES):
            lse_ref[pl.ds(b * (wide // LANES) + c, 1), :] = row[:, c * LANES : (c + 1) * LANES]


def early_rows(rows):
    return rows // 2


def targets_kernel(n_parts, tile_ref, lt_ref, sqy_ref, *refs):
    parts, pieces, (lse_ref, pack_ref) = refs[:n_parts], refs[n_parts:-3], refs[-2:]
    rows = pieces[0].shape[0]
    cut = early_rows(rows)
    pack_ref[: rows - cut, :] = pieces[0][cut:, :]
    for k, piece in enumerate(pieces[1:], 1):
        pack_ref[pl.ds(rows * k - cut, rows), :] = piece[...]
    g_pot = sqy_ref[...] - merge_all([ref[...] for ref in parts])
    bias = to_column(lt_ref[...] * LOG2E + g_pot - sqy_ref[...])
    for b in range(tile_ref.shape[1] // LANES):
        lse_ref[pl.ds(b, 1), :] = over_targets(tile_ref[:, pl.ds(b * LANES, LANES)] + bias)


def merge_kernel(n_parts, *refs):
    parts, refs = refs[:n_parts], refs[n_parts:]
    n_pieces = len(refs) // 2
    pieces, (out_ref, pack_ref, *copies) = refs[:n_pieces], refs[n_pieces:]
    out_ref[...] = merge_all([ref[...] for ref in parts])
    rows = pieces[-1].shape[0]
    pack_ref[:rows, :] = pieces[-1][...]
    pack_ref[rows:, :] = pieces[0][: early_rows(rows), :]
    for piece, copy in zip(pieces[:-1], copies):
        copy[...] = piece[...]


def sources_kernel(n_parts, tile_ref, ls_ref, sqx_ref, *refs):
    bias = source_bias(ls_ref, sqx_ref, refs[:n_parts])
    columns = []
    for j in range(tile_ref.shape[0] // LANES):
        peak, total, _ = over_sources(tile_ref, pl.ds(j * LANES, LANES), bias)
        columns.append(peak + jnp.log2(total))
    refs[-1][...] = to_dense(columns)


def last_sources_kernel(tile_ref, x_ref, ls_ref, sqx_ref, *refs):
    parts, (lse_ref, sent_ref, mine_ref) = refs[:-4], refs[-3:]
    bias = source_bias(ls_ref, sqx_ref, parts)
    x = x_ref[...]
    n_rows = mine_ref.shape[0] // LANES
    core = lax.axis_index("row") % 2
    for out_ref, place in ((sent_ref, 1 - core), (mine_ref, core)):
        columns = []
        for j in range(n_rows):
            at = pl.ds(pl.multiple_of((place * n_rows + j) * LANES, LANES), LANES)
            peak, total, exps = over_sources(tile_ref, at, bias)
            columns.append(peak + jnp.log2(total))
            weights = jnp.concatenate([block.astype(jnp.bfloat16) for block in exps], axis=1)
            mean = jnp.dot(weights, x, preferred_element_type=jnp.float32)
            out_ref[pl.ds(j * LANES, LANES), :] = mean * (1.0 / total)
        lse_ref[pl.ds(place * n_rows, n_rows), :] = to_dense(columns)


def source_bias(ls_ref, sqx_ref, parts):
    f_pot = sqx_ref[...] - merge_all([ref[...] for ref in parts])
    return ls_ref[...] * LOG2E + f_pot - sqx_ref[...]


def over_sources(tile_ref, at, bias):
    scores = [tile_ref[at, pl.ds(b * LANES, LANES)] + bias[b : b + 1, :] for b in range(bias.shape[0])]
    top = scores[0]
    for block in scores[1:]:
        top = jnp.maximum(top, block)
    peak = jnp.max(top, axis=1, keepdims=True)
    exps = [jnp.exp2(block - peak) for block in scores]
    return peak, jnp.sum(sum(exps), axis=1, keepdims=True), exps


def share_kernel(mine_ref, came_ref, total_ref, lse_ref, came_lse_ref, *refs):
    pieces, (out_ref, pack_ref) = refs[:-2], refs[-2:]
    half = mine_ref.shape[0] // LANES
    at = pl.ds(lax.axis_index("row") % 2 * half, half)
    total = total_ref[at, :]
    share, came_share = to_column(jnp.exp2(lse_ref[at, :] - total)), to_column(jnp.exp2(came_lse_ref[at, :] - total))
    out_ref[...] = mine_ref[...] * share + came_ref[...] * came_share
    n_shards, n_y, rows, _ = pack_ref.shape
    y = lax.axis_index("row") // 2
    early, late = pieces[:n_y], pieces[n_y:]
    cut = early_rows(rows)
    for j in range(n_y):
        place = y ^ j
        pack_ref[0, place] = early[j][:rows, :]
        pack_ref[1, place, :cut, :] = early[j][rows:, :]
        pack_ref[1, place, cut:, :] = late[j][: rows - cut, :]
        for k in range(2, n_shards):
            pack_ref[k, place] = late[j][pl.ds((k - 1) * rows - cut, rows), :]


def add_kernel(one_ref, two_ref, *out_refs):
    rows = out_refs[0].shape[0]
    for k, ref in enumerate(out_refs):
        at = pl.ds(k * rows, rows)
        ref[...] = one_ref[at, :] + two_ref[at, :]


def join_kernel(*refs):
    parts, out_ref = refs[:-1], refs[-1]
    rows = out_ref.shape[0]
    lses = [ref[rows : rows + pl.cdiv(rows, LANES), :LANES] for ref in parts]
    whole = merge_all(lses)
    shares = [to_column(jnp.exp2(lse - whole))[:rows] for lse in lses]
    out_ref[...] = sum(ref[:rows, :] * share for ref, share in zip(parts, shares))


def place_kernel(*refs):
    n = (len(refs) - 2) // 2
    mine, others, out_hbm, sems = refs[:n], refs[n : 2 * n], refs[-2], refs[-1]
    rows = mine[0].shape[0]
    core = lax.axis_index("row") % 2
    copies = []
    for place, pieces in ((core, mine), (1 - core, others)):
        for k, piece in enumerate(pieces):
            at = pl.ds(pl.multiple_of((place * n + k) * rows, rows), rows)
            copies.append(pltpu.make_async_copy(piece, out_hbm.at[at, :], sems.at[len(copies)]))
            copies[-1].start()
    for copy in copies:
        copy.wait()


def scores_kernel(near, x_ref, own_ref, mine_ref, other_ref, y_ref, inner_ref):
    rows = inner_ref.shape[0] // 2
    n_tgt = own_ref.shape[0]
    n_came, n_y, part, _ = mine_ref.shape
    col, core = lax.axis_index("col"), lax.axis_index("row") % 2
    y_ref[:n_tgt, :] = own_ref[...]
    for k in range(n_came):
        for ref, place in ((mine_ref, core), (other_ref, 1 - core)):
            for y in range(n_y):
                start = (k + 1) * n_tgt + (2 * y + place) * part
                y_ref[pl.ds(pl.multiple_of(start, part), part), :] = ref[k, y].astype(jnp.bfloat16)
    blocks = [x_ref[pl.ds(pl.multiple_of((col ^ flip) * rows, rows), rows), :] for flip in (0, near)]
    x = jnp.concatenate(blocks, axis=0)
    unit = scale(x.shape[1])
    for b in range(y_ref.shape[0] // n_tgt):
        at = pl.ds(b * n_tgt, n_tgt)
        inner_ref[:, at] = lax.dot_general(x, y_ref[at, :], NT_DIMS, preferred_element_type=jnp.float32) * (2.0 * unit)


EXTRA = 8


def images(flip, inner_ref, y_ref, bias_refs, scores_ref):
    rows = scores_ref.shape[0]
    n_shards = len(bias_refs)
    n_tgt = y_ref.shape[0] // n_shards
    block = pl.ds(flip * rows, rows)
    peak = jnp.full((rows, 1), -jnp.inf, jnp.float32)
    for k, bias_ref in enumerate(bias_refs[::-1]):
        at = pl.ds(k * n_tgt, n_tgt)
        scores = inner_ref[block, at] + to_row(bias_ref[...])
        scores_ref[:, at] = scores
        peak = jnp.maximum(peak, jnp.max(scores, axis=1, keepdims=True))
    total = jnp.zeros((rows, 1), jnp.float32)
    numer = jnp.zeros((rows, y_ref.shape[1]), jnp.float32)
    for k in range(n_shards):
        at = pl.ds(k * n_tgt, n_tgt)
        plan = jnp.exp2(scores_ref[:, at] - peak)
        total = total + jnp.sum(plan, axis=1, keepdims=True)
        numer = numer + jnp.dot(plan.astype(jnp.bfloat16), y_ref[at, :], preferred_element_type=jnp.float32)
    return numer, total, peak


def lanes_of(column):
    rows = column.shape[0]
    if rows % LANES:
        column = jnp.concatenate([column, jnp.zeros((-rows % LANES, 1), jnp.float32)], axis=0)
    return to_dense([column[b : b + LANES] for b in range(0, column.shape[0], LANES)])


EXTRA = 8


def image_kernel(flip, inner_ref, y_ref, *refs):
    bias_refs, (image_ref, scores_ref) = refs[:-2], refs[-2:]
    numer, total, peak = images(flip, inner_ref, y_ref, bias_refs, scores_ref)
    rows = numer.shape[0]
    lse = lanes_of(peak + jnp.log2(total))
    image_ref[:rows, :] = numer * (1.0 / total)
    image_ref[rows:, :] = jnp.zeros((EXTRA, image_ref.shape[1]), jnp.float32)
    image_ref[rows : rows + lse.shape[0], :LANES] = lse


def swap(value, axis, distance):
    n = lax.axis_size(axis)
    return lax.ppermute(value, axis, [(i, i ^ distance) for i in range(n)])


def bits_of(n):
    return [1 << b for b in range(n.bit_length() - 1)]


def on_device(source, target, log_source_mass, log_target_mass):
    n_src, width = source.shape
    n_tgt = target.shape[0]
    n_col, n_row = lax.axis_size("col"), lax.axis_size("row")
    count = n_src // n_col
    n_x = 1 << (len(bits_of(n_col)) // 2)
    n_z = n_col // n_x
    y_bits = bits_of(n_row)[1:]
    ls = log_source_mass.reshape(-1, LANES)
    lt = log_target_mass.reshape(-1, LANES)
    src_dense, tgt_dense = f32(*ls.shape), f32(*lt.shape)
    half = n_tgt // 2

    part = f32(n_tgt // n_row, width)
    pieces = {0: call(quarter_kernel, part, target)}
    for distance in [bit for bit in bits_of(n_col) if bit > n_x][::-1]:
        pieces |= {k ^ distance: swap(piece, "col", distance) for k, piece in pieces.items()}
    early = swap(pieces[0], "col", 1)

    def along_y(piece):
        held = [piece]
        for distance in y_bits:
            held += [swap(one, "row", distance) for one in held]
        return held

    tile, lse, sqy = call(first_kernel, (f32(n_tgt, n_src), src_dense, tgt_dense), target, source, lt)
    sqx = call(norms_kernel, src_dense, source)
    cut = early_rows(part.shape[0])
    for step in range(ITERS):
        if step > 0:
            apart = [0, 1] + [k for k in pieces if k > 1]
            lse, late = call(
                lambda *refs: targets_kernel(n_row, *refs),
                (src_dense, f32((len(apart) - 2) * part.shape[0] - cut, width)),
                tile, lt, sqy, *parts, *[pieces[k] for k in apart[2:]], early[-1],
            )
            late = along_y(late)
        if step > 0:
            rest = bits_of(n_col)
        else:
            group, rest = [*bits_of(n_x), n_col // 2], [bit for bit in bits_of(n_col // 2) if bit >= n_x]
            ways = [0]
            for bit in group:
                ways += [way | bit for way in ways]
            near = [lse] + [swap(lse, "col", way) for way in ways[:0:-1]]
            far = [k for k in pieces if k > 0]
            lse, early, *copies = call(
                lambda *refs: merge_kernel(len(ways), *refs),
                (src_dense, f32(part.shape[0] + cut, width), *(part,) * len(far)),
                *near, *[pieces[k] for k in far], early,
            )
            early = along_y(early)
            pieces |= dict(zip(far, copies))
            for bit in bits_of(n_x)[::-1]:
                pieces |= {k ^ bit: swap(piece, "col", bit) for k, piece in pieces.items() if k ^ bit != 1}
        for distance in rest[:-1]:
            lse = merge_all([lse, swap(lse, "col", distance)])
        parts = [lse, swap(lse, "col", rest[-1])]
        if step < ITERS - 1:
            lse = call(lambda *refs: sources_kernel(2, *refs), tgt_dense, tile, ls, sqx, *parts)
        else:
            lse, sent, mine = call(
                last_sources_kernel,
                (tgt_dense, f32(half, width), f32(half, width)),
                tile, source, ls, sqx, *parts, late[-1],
            )
        parts = [lse] + [swap(lse, "row", k) for k in range(1, n_row)]
    total = merge_all(parts)

    bias = lt * LOG2E + (sqy - total) - sqy
    biases = [bias] + [swap(bias, "col", distance) for distance in apart[1:]]

    mine, came = call(
        share_kernel,
        (f32(half, width), f32(len(apart) - 1, n_row // 2, *part.shape)),
        mine, swap(sent, "row", 1), total, lse, parts[1], *early, *late,
    )
    rest = bits_of(n_row)[1:]
    for distance in rest[:-1]:
        mine, = call(add_kernel, (f32(half, width),), mine, swap(mine, "row", distance))
    mine_came = swap(mine, "row", rest[-1])

    n_all = len(apart) * n_tgt
    all_y, inner = call(
        lambda *refs: scores_kernel(n_x, *refs),
        (bf16(n_all, width), f32(2 * count, n_all)),
        source, target, came, swap(came, "row", 1),
        limit=32,
    )

    def image(flip):
        return call(
            lambda *refs: image_kernel(flip, *refs),
            f32(count + EXTRA, width),
            inner, all_y, *biases[::-1],
            scratch=[pltpu.VMEM((count, n_all), jnp.float32)],
        )

    came = swap(image(1), "col", n_x)
    own = image(0)
    n_last = 4
    mine = call(add_kernel, (f32(half // n_last, width),) * n_last, mine, mine_came)
    target_image = call(
        place_kernel, f32(n_tgt, width), *mine, *[swap(piece, "row", 1) for piece in mine],
        out_specs=HBM, scratch=[DMA((2 * n_last,))],
    )
    source_image = call(join_kernel, f32(count, width), own, came)
    return source_image, target_image


def solution(mesh):
    in_specs = (P("row", None), P("col", None), P("row"), P("col"))
    out_specs = (P(("row", "col"), None), P("col", None))
    return jax.shard_map(
        on_device, mesh=mesh, in_specs=in_specs, out_specs=out_specs, check_vma=False
    )
```

```python
import math

import jax
import jax.numpy as jnp
from jax import lax
from jax.experimental import pallas as pl
from jax.experimental.pallas import tpu as pltpu
from jax.sharding import PartitionSpec as P

ITERS = 2
BLUR = 0.1
LOG2E = math.log2(math.e)
LANES = 128
NT_DIMS = (((1,), (1,)), ((), ()))
VMEM = pl.BlockSpec(memory_space=pltpu.VMEM)
HBM = pl.BlockSpec(memory_space=pltpu.HBM)
ANY = pl.BlockSpec(memory_space=pl.ANY)
DMA = pltpu.SemaphoreType.DMA


def call(kernel, out_shape, *args, in_specs=None, out_specs=None, scratch=(), limit=24):
    return pl.pallas_call(
        kernel,
        out_shape=out_shape,
        in_specs=in_specs or [VMEM] * len(args),
        out_specs=out_specs or jax.tree.map(lambda _: VMEM, out_shape),
        scratch_shapes=list(scratch),
        compiler_params=pltpu.CompilerParams(vmem_limit_bytes=limit << 20),
    )(*args)


def f32(*shape):
    return jax.ShapeDtypeStruct(shape, jnp.float32)


def bf16(*shape):
    return jax.ShapeDtypeStruct(shape, jnp.bfloat16)


def scale(width):
    return LOG2E / (width * BLUR)


def to_column(dense):
    n = dense.shape[0]
    square = jnp.concatenate([dense, jnp.zeros((LANES - n, LANES), jnp.float32)], axis=0).T
    return jnp.concatenate([square[:, b : b + 1] for b in range(n)], axis=0)


def to_dense(columns):
    lane = lax.broadcasted_iota(jnp.int32, (LANES, LANES), 1)
    square = jnp.zeros((LANES, LANES), jnp.float32)
    for b, column in enumerate(columns):
        square = jnp.where(lane == b, column, square)
    return square.T[: len(columns)]


def to_row(dense):
    return jnp.concatenate([dense[b : b + 1, :] for b in range(dense.shape[0])], axis=1)


def over_targets(scores):
    peak = jnp.max(scores, axis=0, keepdims=True)
    total = jnp.sum(jnp.exp2(scores - peak), axis=0, keepdims=True)
    return peak + jnp.log2(total)


def half_at(ref, place):
    half = ref.shape[0] // 2
    return ref[pl.ds(place * half, half), :]


def merge_all(parts):
    peak = parts[0]
    for part in parts[1:]:
        peak = jnp.maximum(peak, part)
    return peak + jnp.log2(sum(jnp.exp2(part - peak) for part in parts))


def norms(block):
    wide = block.astype(jnp.float32)
    return jnp.sum(wide * wide, axis=1, keepdims=True) * scale(block.shape[1])


def quarter_kernel(y_ref, out_ref):
    rows = out_ref.shape[0]
    out_ref[...] = y_ref[pl.ds(pl.multiple_of(lax.axis_index("row") * rows, rows), rows), :].astype(jnp.float32)


def norms_kernel(x_ref, sqx_ref):
    columns = [norms(x_ref[pl.ds(b, LANES), :]) for b in range(0, x_ref.shape[0], LANES)]
    sqx_ref[...] = to_dense(columns)


def first_kernel(y_ref, x_ref, lt_ref, tile_ref, lse_ref, sqy_ref):
    wide = 256
    y = y_ref[...]
    unit = scale(y.shape[1])
    sqy = norms(y)
    sqy_ref[...] = to_dense([sqy[b : b + LANES] for b in range(0, y.shape[0], LANES)])
    bias = to_column(lt_ref[...]) * LOG2E - sqy
    for b in range(x_ref.shape[0] // wide):
        at = pl.ds(b * wide, wide)
        x = x_ref[at, :]
        tile = lax.dot_general(y, x, NT_DIMS, preferred_element_type=jnp.float32) * (2.0 * unit)
        tile_ref[:, at] = tile
        row = over_targets(tile + bias)
        for c in range(wide // LANES):
            lse_ref[pl.ds(b * (wide // LANES) + c, 1), :] = row[:, c * LANES : (c + 1) * LANES]


def early_rows(rows):
    return rows // 2


def targets_kernel(n_parts, tile_ref, lt_ref, sqy_ref, *refs):
    parts, pieces, (lse_ref, pack_ref) = refs[:n_parts], refs[n_parts:-3], refs[-2:]
    rows = pieces[0].shape[0]
    cut = early_rows(rows)
    pack_ref[: rows - cut, :] = pieces[0][cut:, :]
    for k, piece in enumerate(pieces[1:], 1):
        pack_ref[pl.ds(rows * k - cut, rows), :] = piece[...]
    g_pot = sqy_ref[...] - merge_all([ref[...] for ref in parts])
    bias = to_column(lt_ref[...] * LOG2E + g_pot - sqy_ref[...])
    for b in range(tile_ref.shape[1] // LANES):
        lse_ref[pl.ds(b, 1), :] = over_targets(tile_ref[:, pl.ds(b * LANES, LANES)] + bias)


def merge_kernel(n_parts, *refs):
    parts, refs = refs[:n_parts], refs[n_parts:]
    n_pieces = len(refs) // 2
    pieces, (out_ref, pack_ref, *copies) = refs[:n_pieces], refs[n_pieces:]
    out_ref[...] = merge_all([ref[...] for ref in parts])
    rows = pieces[-1].shape[0]
    pack_ref[:rows, :] = pieces[-1][...]
    pack_ref[rows:, :] = pieces[0][: early_rows(rows), :]
    for piece, copy in zip(pieces[:-1], copies):
        copy[...] = piece[...]


def sources_kernel(n_parts, tile_ref, ls_ref, sqx_ref, *refs):
    bias = source_bias(ls_ref, sqx_ref, refs[:n_parts])
    columns = []
    for j in range(tile_ref.shape[0] // LANES):
        peak, total, _ = over_sources(tile_ref, pl.ds(j * LANES, LANES), bias)
        columns.append(peak + jnp.log2(total))
    refs[-1][...] = to_dense(columns)


def last_sources_kernel(tile_ref, x_ref, ls_ref, sqx_ref, *refs):
    parts, (lse_ref, sent_ref, mine_ref) = refs[:-4], refs[-3:]
    bias = source_bias(ls_ref, sqx_ref, parts)
    x = x_ref[...]
    n_rows = mine_ref.shape[0] // LANES
    core = lax.axis_index("row") % 2
    for out_ref, place in ((sent_ref, 1 - core), (mine_ref, core)):
        columns = []
        for j in range(n_rows):
            at = pl.ds(pl.multiple_of((place * n_rows + j) * LANES, LANES), LANES)
            peak, total, exps = over_sources(tile_ref, at, bias)
            columns.append(peak + jnp.log2(total))
            weights = jnp.concatenate([block.astype(jnp.bfloat16) for block in exps], axis=1)
            mean = jnp.dot(weights, x, preferred_element_type=jnp.float32)
            out_ref[pl.ds(j * LANES, LANES), :] = mean * (1.0 / total)
        lse_ref[pl.ds(place * n_rows, n_rows), :] = to_dense(columns)


def source_bias(ls_ref, sqx_ref, parts):
    f_pot = sqx_ref[...] - merge_all([ref[...] for ref in parts])
    return ls_ref[...] * LOG2E + f_pot - sqx_ref[...]


def over_sources(tile_ref, at, bias):
    scores = [tile_ref[at, pl.ds(b * LANES, LANES)] + bias[b : b + 1, :] for b in range(bias.shape[0])]
    top = scores[0]
    for block in scores[1:]:
        top = jnp.maximum(top, block)
    peak = jnp.max(top, axis=1, keepdims=True)
    exps = [jnp.exp2(block - peak) for block in scores]
    return peak, jnp.sum(sum(exps), axis=1, keepdims=True), exps


def share_kernel(mine_ref, came_ref, total_ref, lse_ref, came_lse_ref, *refs):
    pieces, (out_ref, pack_ref) = refs[:-2], refs[-2:]
    half = mine_ref.shape[0] // LANES
    at = pl.ds(lax.axis_index("row") % 2 * half, half)
    total = total_ref[at, :]
    share, came_share = to_column(jnp.exp2(lse_ref[at, :] - total)), to_column(jnp.exp2(came_lse_ref[at, :] - total))
    out_ref[...] = mine_ref[...] * share + came_ref[...] * came_share
    n_shards, n_y, rows, _ = pack_ref.shape
    y = lax.axis_index("row") // 2
    early, late = pieces[:n_y], pieces[n_y:]
    cut = early_rows(rows)
    for j in range(n_y):
        place = y ^ j
        pack_ref[0, place] = early[j][:rows, :]
        pack_ref[1, place, :cut, :] = early[j][rows:, :]
        pack_ref[1, place, cut:, :] = late[j][: rows - cut, :]
        for k in range(2, n_shards):
            pack_ref[k, place] = late[j][pl.ds((k - 1) * rows - cut, rows), :]


def add_kernel(one_ref, two_ref, *out_refs):
    rows = out_refs[0].shape[0]
    for k, ref in enumerate(out_refs):
        at = pl.ds(k * rows, rows)
        ref[...] = one_ref[at, :] + two_ref[at, :]


def join_kernel(n_pieces, *refs):
    out_ref = refs[-1]
    rows = out_ref.shape[0] // n_pieces
    for k in range(n_pieces):
        parts = refs[k:-1:n_pieces]
        lses = [ref[rows : rows + pl.cdiv(rows, LANES), :LANES] for ref in parts]
        whole = merge_all(lses)
        shares = [to_column(jnp.exp2(lse - whole))[:rows] for lse in lses]
        out_ref[pl.ds(k * rows, rows), :] = sum(ref[:rows, :] * share for ref, share in zip(parts, shares))


def place_kernel(*refs):
    n = (len(refs) - 2) // 2
    mine, others, out_hbm, sems = refs[:n], refs[n : 2 * n], refs[-2], refs[-1]
    rows = mine[0].shape[0]
    core = lax.axis_index("row") % 2
    copies = []
    for place, pieces in ((core, mine), (1 - core, others)):
        for k, piece in enumerate(pieces):
            at = pl.ds(pl.multiple_of((place * n + k) * rows, rows), rows)
            copies.append(pltpu.make_async_copy(piece, out_hbm.at[at, :], sems.at[len(copies)]))
            copies[-1].start()
    for copy in copies:
        copy.wait()


def scores_kernel(near, x_ref, own_ref, mine_ref, other_ref, y_ref, inner_ref):
    rows = inner_ref.shape[0] // 2
    n_tgt = own_ref.shape[0]
    n_came, n_y, part, _ = mine_ref.shape
    col, core = lax.axis_index("col"), lax.axis_index("row") % 2
    y_ref[:n_tgt, :] = own_ref[...]
    for k in range(n_came):
        for ref, place in ((mine_ref, core), (other_ref, 1 - core)):
            for y in range(n_y):
                start = (k + 1) * n_tgt + (2 * y + place) * part
                y_ref[pl.ds(pl.multiple_of(start, part), part), :] = ref[k, y].astype(jnp.bfloat16)
    blocks = [x_ref[pl.ds(pl.multiple_of((col ^ flip) * rows, rows), rows), :] for flip in (0, near)]
    x = jnp.concatenate(blocks, axis=0)
    unit = scale(x.shape[1])
    for b in range(y_ref.shape[0] // n_tgt):
        at = pl.ds(b * n_tgt, n_tgt)
        inner_ref[:, at] = lax.dot_general(x, y_ref[at, :], NT_DIMS, preferred_element_type=jnp.float32) * (2.0 * unit)


EXTRA = 8


def images(start, inner_ref, y_ref, bias_refs, scores_ref):
    rows = scores_ref.shape[0]
    n_shards = len(bias_refs)
    n_tgt = y_ref.shape[0] // n_shards
    block = pl.ds(start, rows)
    peak = jnp.full((rows, 1), -jnp.inf, jnp.float32)
    for k, bias_ref in enumerate(bias_refs[::-1]):
        at = pl.ds(k * n_tgt, n_tgt)
        scores = inner_ref[block, at] + to_row(bias_ref[...])
        scores_ref[:, at] = scores
        peak = jnp.maximum(peak, jnp.max(scores, axis=1, keepdims=True))
    total = jnp.zeros((rows, 1), jnp.float32)
    numer = jnp.zeros((rows, y_ref.shape[1]), jnp.float32)
    for k in range(n_shards):
        at = pl.ds(k * n_tgt, n_tgt)
        plan = jnp.exp2(scores_ref[:, at] - peak)
        total = total + jnp.sum(plan, axis=1, keepdims=True)
        numer = numer + jnp.dot(plan.astype(jnp.bfloat16), y_ref[at, :], preferred_element_type=jnp.float32)
    return numer, total, peak


def lanes_of(column):
    rows = column.shape[0]
    if rows % LANES:
        column = jnp.concatenate([column, jnp.zeros((-rows % LANES, 1), jnp.float32)], axis=0)
    return to_dense([column[b : b + LANES] for b in range(0, column.shape[0], LANES)])


EXTRA = 8


def image_kernel(start, inner_ref, y_ref, *refs):
    bias_refs, (image_ref, scores_ref) = refs[:-2], refs[-2:]
    numer, total, peak = images(start, inner_ref, y_ref, bias_refs, scores_ref)
    rows = numer.shape[0]
    lse = lanes_of(peak + jnp.log2(total))
    image_ref[:rows, :] = numer * (1.0 / total)
    image_ref[rows:, :] = jnp.zeros((EXTRA, image_ref.shape[1]), jnp.float32)
    image_ref[rows : rows + lse.shape[0], :LANES] = lse


def swap(value, axis, distance):
    n = lax.axis_size(axis)
    return lax.ppermute(value, axis, [(i, i ^ distance) for i in range(n)])


def bits_of(n):
    return [1 << b for b in range(n.bit_length() - 1)]


def on_device(source, target, log_source_mass, log_target_mass):
    n_src, width = source.shape
    n_tgt = target.shape[0]
    n_col, n_row = lax.axis_size("col"), lax.axis_size("row")
    count = n_src // n_col
    n_x = 1 << (len(bits_of(n_col)) // 2)
    n_z = n_col // n_x
    y_bits = bits_of(n_row)[1:]
    ls = log_source_mass.reshape(-1, LANES)
    lt = log_target_mass.reshape(-1, LANES)
    src_dense, tgt_dense = f32(*ls.shape), f32(*lt.shape)
    half = n_tgt // 2

    part = f32(n_tgt // n_row, width)
    pieces = {0: call(quarter_kernel, part, target)}
    for distance in [bit for bit in bits_of(n_col) if bit > n_x][::-1]:
        pieces |= {k ^ distance: swap(piece, "col", distance) for k, piece in pieces.items()}
    early = swap(pieces[0], "col", 1)

    def along_y(piece):
        held = [piece]
        for distance in y_bits:
            held += [swap(one, "row", distance) for one in held]
        return held

    tile, lse, sqy = call(first_kernel, (f32(n_tgt, n_src), src_dense, tgt_dense), target, source, lt)
    sqx = call(norms_kernel, src_dense, source)
    cut = early_rows(part.shape[0])
    for step in range(ITERS):
        if step > 0:
            apart = [0, 1] + [k for k in pieces if k > 1]
            lse, late = call(
                lambda *refs: targets_kernel(n_row, *refs),
                (src_dense, f32((len(apart) - 2) * part.shape[0] - cut, width)),
                tile, lt, sqy, *parts, *[pieces[k] for k in apart[2:]], early[-1],
            )
            late = along_y(late)
        last = n_x if step == 0 else n_col // 2
        group = [*bits_of(n_x), n_x + n_col // 2 - last]
        rest = [bit for bit in bits_of(n_col) if bit not in group and bit != last] + [last]
        ways = [0]
        for bit in group:
            ways += [way | bit for way in ways]
        near = [lse] + [swap(lse, "col", way) for way in ways[:0:-1]]
        if step > 0:
            lse = merge_all(near[:1] + near[:0:-1])
        else:
            far = [k for k in pieces if k > 0]
            lse, early, *copies = call(
                lambda *refs: merge_kernel(len(ways), *refs),
                (src_dense, f32(part.shape[0] + cut, width), *(part,) * len(far)),
                *near, *[pieces[k] for k in far], early,
            )
            early = along_y(early)
            pieces |= dict(zip(far, copies))
            for bit in bits_of(n_x)[::-1]:
                pieces |= {k ^ bit: swap(piece, "col", bit) for k, piece in pieces.items() if k ^ bit != 1}
        for distance in rest[:-1]:
            lse = merge_all([lse, swap(lse, "col", distance)])
        parts = [lse, swap(lse, "col", rest[-1])]
        if step < ITERS - 1:
            lse = call(lambda *refs: sources_kernel(2, *refs), tgt_dense, tile, ls, sqx, *parts)
        else:
            lse, sent, mine = call(
                last_sources_kernel,
                (tgt_dense, f32(half, width), f32(half, width)),
                tile, source, ls, sqx, *parts, late[-1],
            )
        parts = [lse] + [swap(lse, "row", k) for k in range(1, n_row)]
    total = merge_all(parts)

    bias = lt * LOG2E + (sqy - total) - sqy
    biases = [bias] + [swap(bias, "col", distance) for distance in apart[1:]]

    mine, came = call(
        share_kernel,
        (f32(half, width), f32(len(apart) - 1, n_row // 2, *part.shape)),
        mine, swap(sent, "row", 1), total, lse, parts[1], *early, *late,
    )
    rest = bits_of(n_row)[1:]
    for distance in rest[:-1]:
        mine, = call(add_kernel, (f32(half, width),), mine, swap(mine, "row", distance))
    mine_came = swap(mine, "row", rest[-1])

    n_all = len(apart) * n_tgt
    all_y, inner = call(
        lambda *refs: scores_kernel(n_x, *refs),
        (bf16(n_all, width), f32(2 * count, n_all)),
        source, target, came, swap(came, "row", 1),
        limit=32,
    )

    n_images = 2
    rows = count // n_images

    def image(start):
        return call(
            lambda *refs: image_kernel(start, *refs),
            f32(rows + EXTRA, width),
            inner, all_y, *biases[::-1],
            scratch=[pltpu.VMEM((rows, n_all), jnp.float32)],
        )

    came = [swap(image(count + k * rows), "col", n_x) for k in range(n_images)]
    own = [image(k * rows) for k in range(n_images)]
    n_last = 4
    mine = call(add_kernel, (f32(half // n_last, width),) * n_last, mine, mine_came)
    target_image = call(
        place_kernel, f32(n_tgt, width), *mine, *[swap(piece, "row", 1) for piece in mine],
        out_specs=HBM, scratch=[DMA((2 * n_last,))],
    )
    source_image = call(lambda *refs: join_kernel(n_images, *refs), f32(count, width), *own, *came)
    return source_image, target_image


def solution(mesh):
    in_specs = (P("row", None), P("col", None), P("row"), P("col"))
    out_specs = (P(("row", "col"), None), P("col", None))
    return jax.shard_map(
        on_device, mesh=mesh, in_specs=in_specs, out_specs=out_specs, check_vma=False
    )
```

```python
import math

import jax
import jax.numpy as jnp
from jax import lax
from jax.experimental import pallas as pl
from jax.experimental.pallas import tpu as pltpu
from jax.sharding import PartitionSpec as P

ITERS = 2
BLUR = 0.1
LOG2E = math.log2(math.e)
LANES = 128
NT_DIMS = (((1,), (1,)), ((), ()))
VMEM = pl.BlockSpec(memory_space=pltpu.VMEM)
HBM = pl.BlockSpec(memory_space=pltpu.HBM)
ANY = pl.BlockSpec(memory_space=pl.ANY)
DMA = pltpu.SemaphoreType.DMA


def call(kernel, out_shape, *args, in_specs=None, out_specs=None, scratch=(), limit=24):
    return pl.pallas_call(
        kernel,
        out_shape=out_shape,
        in_specs=in_specs or [VMEM] * len(args),
        out_specs=out_specs or jax.tree.map(lambda _: VMEM, out_shape),
        scratch_shapes=list(scratch),
        compiler_params=pltpu.CompilerParams(vmem_limit_bytes=limit << 20),
    )(*args)


def f32(*shape):
    return jax.ShapeDtypeStruct(shape, jnp.float32)


def bf16(*shape):
    return jax.ShapeDtypeStruct(shape, jnp.bfloat16)


def scale(width):
    return LOG2E / (width * BLUR)


def to_column(dense):
    n = dense.shape[0]
    square = jnp.concatenate([dense, jnp.zeros((LANES - n, LANES), jnp.float32)], axis=0).T
    return jnp.concatenate([square[:, b : b + 1] for b in range(n)], axis=0)


def to_dense(columns):
    lane = lax.broadcasted_iota(jnp.int32, (LANES, LANES), 1)
    square = jnp.zeros((LANES, LANES), jnp.float32)
    for b, column in enumerate(columns):
        square = jnp.where(lane == b, column, square)
    return square.T[: len(columns)]


def to_row(dense):
    return jnp.concatenate([dense[b : b + 1, :] for b in range(dense.shape[0])], axis=1)


def over_targets(scores):
    peak = jnp.max(scores, axis=0, keepdims=True)
    total = jnp.sum(jnp.exp2(scores - peak), axis=0, keepdims=True)
    return peak + jnp.log2(total)


def half_at(ref, place):
    half = ref.shape[0] // 2
    return ref[pl.ds(place * half, half), :]


def merge_all(parts):
    peak = parts[0]
    for part in parts[1:]:
        peak = jnp.maximum(peak, part)
    return peak + jnp.log2(sum(jnp.exp2(part - peak) for part in parts))


def norms(block):
    wide = block.astype(jnp.float32)
    return jnp.sum(wide * wide, axis=1, keepdims=True) * scale(block.shape[1])


def quarter_kernel(y_ref, out_ref):
    rows = out_ref.shape[0]
    out_ref[...] = y_ref[pl.ds(pl.multiple_of(lax.axis_index("row") * rows, rows), rows), :].astype(jnp.float32)


def norms_kernel(x_ref, sqx_ref):
    columns = [norms(x_ref[pl.ds(b, LANES), :]) for b in range(0, x_ref.shape[0], LANES)]
    sqx_ref[...] = to_dense(columns)


def first_kernel(y_ref, x_ref, lt_ref, tile_ref, lse_ref, sqy_ref):
    wide = 256
    y = y_ref[...]
    unit = scale(y.shape[1])
    sqy = norms(y)
    sqy_ref[...] = to_dense([sqy[b : b + LANES] for b in range(0, y.shape[0], LANES)])
    bias = to_column(lt_ref[...]) * LOG2E - sqy
    for b in range(x_ref.shape[0] // wide):
        at = pl.ds(b * wide, wide)
        x = x_ref[at, :]
        tile = lax.dot_general(y, x, NT_DIMS, preferred_element_type=jnp.float32) * (2.0 * unit)
        tile_ref[:, at] = tile
        row = over_targets(tile + bias)
        for c in range(wide // LANES):
            lse_ref[pl.ds(b * (wide // LANES) + c, 1), :] = row[:, c * LANES : (c + 1) * LANES]


def early_rows(rows):
    return rows // 2


def targets_kernel(n_parts, tile_ref, lt_ref, sqy_ref, *refs):
    parts, pieces, (lse_ref, pack_ref) = refs[:n_parts], refs[n_parts:-3], refs[-2:]
    rows = pieces[0].shape[0]
    cut = early_rows(rows)
    pack_ref[: rows - cut, :] = pieces[0][cut:, :]
    for k, piece in enumerate(pieces[1:], 1):
        pack_ref[pl.ds(rows * k - cut, rows), :] = piece[...]
    g_pot = sqy_ref[...] - merge_all([ref[...] for ref in parts])
    bias = to_column(lt_ref[...] * LOG2E + g_pot - sqy_ref[...])
    for b in range(tile_ref.shape[1] // LANES):
        lse_ref[pl.ds(b, 1), :] = over_targets(tile_ref[:, pl.ds(b * LANES, LANES)] + bias)


def merge_kernel(n_parts, *refs):
    parts, refs = refs[:n_parts], refs[n_parts:]
    n_pieces = len(refs) // 2
    pieces, (out_ref, pack_ref, *copies) = refs[:n_pieces], refs[n_pieces:]
    out_ref[...] = merge_all([ref[...] for ref in parts])
    rows = pieces[-1].shape[0]
    pack_ref[:rows, :] = pieces[-1][...]
    pack_ref[rows:, :] = pieces[0][: early_rows(rows), :]
    for piece, copy in zip(pieces[:-1], copies):
        copy[...] = piece[...]


ROWS = 64


def sources_kernel(n_parts, tile_ref, ls_ref, sqx_ref, *refs):
    bias = source_bias(ls_ref, sqx_ref, refs[:n_parts])
    columns = []
    for j in range(tile_ref.shape[0] // ROWS):
        peak, total, _ = over_sources(tile_ref, pl.ds(j * ROWS, ROWS), bias)
        columns.append(peak + jnp.log2(total))
    column = jnp.concatenate(columns, axis=0)
    refs[-1][...] = to_dense([column[b : b + LANES] for b in range(0, column.shape[0], LANES)])


def last_sources_kernel(tile_ref, x_ref, ls_ref, sqx_ref, *refs):
    parts, (lse_ref, sent_ref, mine_ref) = refs[:-4], refs[-3:]
    bias = source_bias(ls_ref, sqx_ref, parts)
    x = x_ref[...]
    n_rows = mine_ref.shape[0] // LANES
    core = lax.axis_index("row") % 2
    for out_ref, place in ((sent_ref, 1 - core), (mine_ref, core)):
        columns = []
        for j in range(n_rows):
            totals, weights = [], []
            for r in range(0, LANES, ROWS):
                at = pl.ds(pl.multiple_of((place * n_rows + j) * LANES + r, ROWS), ROWS)
                peak, total, exps = over_sources(tile_ref, at, bias)
                columns.append(peak + jnp.log2(total))
                totals.append(total)
                weights.append(jnp.concatenate([block.astype(jnp.bfloat16) for block in exps], axis=1))
            mean = jnp.dot(jnp.concatenate(weights, axis=0), x, preferred_element_type=jnp.float32)
            out_ref[pl.ds(j * LANES, LANES), :] = mean * (1.0 / jnp.concatenate(totals, axis=0))
        column = jnp.concatenate(columns, axis=0)
        columns = [column[b : b + LANES] for b in range(0, column.shape[0], LANES)]
        lse_ref[pl.ds(place * n_rows, n_rows), :] = to_dense(columns)


def source_bias(ls_ref, sqx_ref, parts):
    f_pot = sqx_ref[...] - merge_all([ref[...] for ref in parts])
    return ls_ref[...] * LOG2E + f_pot - sqx_ref[...]


def over_sources(tile_ref, at, bias):
    scores = [tile_ref[at, pl.ds(b * LANES, LANES)] + bias[b : b + 1, :] for b in range(bias.shape[0])]
    top = scores[0]
    for block in scores[1:]:
        top = jnp.maximum(top, block)
    peak = jnp.max(top, axis=1, keepdims=True)
    exps = [jnp.exp2(block - peak) for block in scores]
    return peak, jnp.sum(sum(exps), axis=1, keepdims=True), exps


def share_kernel(mine_ref, came_ref, total_ref, lse_ref, came_lse_ref, *refs):
    pieces, (out_ref, pack_ref) = refs[:-2], refs[-2:]
    half = mine_ref.shape[0] // LANES
    at = pl.ds(lax.axis_index("row") % 2 * half, half)
    total = total_ref[at, :]
    share, came_share = to_column(jnp.exp2(lse_ref[at, :] - total)), to_column(jnp.exp2(came_lse_ref[at, :] - total))
    out_ref[...] = mine_ref[...] * share + came_ref[...] * came_share
    n_shards, n_y, rows, _ = pack_ref.shape
    y = lax.axis_index("row") // 2
    early, late = pieces[:n_y], pieces[n_y:]
    cut = early_rows(rows)
    for j in range(n_y):
        place = y ^ j
        pack_ref[0, place] = early[j][:rows, :]
        pack_ref[1, place, :cut, :] = early[j][rows:, :]
        pack_ref[1, place, cut:, :] = late[j][: rows - cut, :]
        for k in range(2, n_shards):
            pack_ref[k, place] = late[j][pl.ds((k - 1) * rows - cut, rows), :]


def add_kernel(one_ref, two_ref, *out_refs):
    rows = out_refs[0].shape[0]
    for k, ref in enumerate(out_refs):
        at = pl.ds(k * rows, rows)
        ref[...] = one_ref[at, :] + two_ref[at, :]


def join_kernel(*refs):
    parts, (out_hbm, held_ref, sems) = refs[:-3], refs[-3:]
    rows = held_ref.shape[0]
    lses = [ref[rows : rows + pl.cdiv(rows, LANES), :LANES] for ref in parts]
    whole = merge_all(lses)
    shares = [to_column(jnp.exp2(lse - whole))[:rows] for lse in lses]
    n_pieces = sems.shape[0]
    copies = []
    for k in range(n_pieces):
        at = pl.ds(k * rows // n_pieces, rows // n_pieces)
        begin, end = k * rows // n_pieces, (k + 1) * rows // n_pieces
        held_ref[at, :] = sum(ref[at, :] * share[begin:end] for ref, share in zip(parts, shares))
        copies.append(pltpu.make_async_copy(held_ref.at[at, :], out_hbm.at[at, :], sems.at[k]))
        copies[-1].start()
    for copy in copies:
        copy.wait()


def place_kernel(*refs):
    n = (len(refs) - 2) // 2
    mine, others, out_hbm, sems = refs[:n], refs[n : 2 * n], refs[-2], refs[-1]
    rows = mine[0].shape[0]
    core = lax.axis_index("row") % 2
    copies = []
    for place, pieces in ((core, mine), (1 - core, others)):
        for k, piece in enumerate(pieces):
            at = pl.ds(pl.multiple_of((place * n + k) * rows, rows), rows)
            copies.append(pltpu.make_async_copy(piece, out_hbm.at[at, :], sems.at[len(copies)]))
            copies[-1].start()
    for copy in copies:
        copy.wait()


def scores_kernel(near, x_ref, own_ref, mine_ref, other_ref, y_ref, inner_ref):
    rows = inner_ref.shape[0] // 2
    n_tgt = own_ref.shape[0]
    n_came, n_y, part, _ = mine_ref.shape
    col, core = lax.axis_index("col"), lax.axis_index("row") % 2
    y_ref[:n_tgt, :] = own_ref[...]
    for k in range(n_came):
        for ref, place in ((mine_ref, core), (other_ref, 1 - core)):
            for y in range(n_y):
                start = (k + 1) * n_tgt + (2 * y + place) * part
                y_ref[pl.ds(pl.multiple_of(start, part), part), :] = ref[k, y].astype(jnp.bfloat16)
    blocks = [x_ref[pl.ds(pl.multiple_of((col ^ flip) * rows, rows), rows), :] for flip in (0, near)]
    x = jnp.concatenate(blocks, axis=0)
    unit = scale(x.shape[1])
    for b in range(y_ref.shape[0] // n_tgt):
        at = pl.ds(b * n_tgt, n_tgt)
        inner_ref[:, at] = lax.dot_general(x, y_ref[at, :], NT_DIMS, preferred_element_type=jnp.float32) * (2.0 * unit)


EXTRA = 8


def images(flip, inner_ref, y_ref, bias_refs, scores_ref):
    rows = scores_ref.shape[0]
    n_shards = len(bias_refs)
    n_tgt = y_ref.shape[0] // n_shards
    block = pl.ds(flip * rows, rows)
    peak = jnp.full((rows, 1), -jnp.inf, jnp.float32)
    for k, bias_ref in enumerate(bias_refs[::-1]):
        at = pl.ds(k * n_tgt, n_tgt)
        scores = inner_ref[block, at] + to_row(bias_ref[...])
        scores_ref[:, at] = scores
        peak = jnp.maximum(peak, jnp.max(scores, axis=1, keepdims=True))
    total = jnp.zeros((rows, 1), jnp.float32)
    numer = jnp.zeros((rows, y_ref.shape[1]), jnp.float32)
    for k in range(n_shards):
        at = pl.ds(k * n_tgt, n_tgt)
        plan = jnp.exp2(scores_ref[:, at] - peak)
        total = total + jnp.sum(plan, axis=1, keepdims=True)
        numer = numer + jnp.dot(plan.astype(jnp.bfloat16), y_ref[at, :], preferred_element_type=jnp.float32)
    return numer, total, peak


def lanes_of(column):
    rows = column.shape[0]
    if rows % LANES:
        column = jnp.concatenate([column, jnp.zeros((-rows % LANES, 1), jnp.float32)], axis=0)
    return to_dense([column[b : b + LANES] for b in range(0, column.shape[0], LANES)])


EXTRA = 8


def image_kernel(flip, inner_ref, y_ref, *refs):
    bias_refs, (image_ref, scores_ref) = refs[:-2], refs[-2:]
    numer, total, peak = images(flip, inner_ref, y_ref, bias_refs, scores_ref)
    rows = numer.shape[0]
    lse = lanes_of(peak + jnp.log2(total))
    image_ref[:rows, :] = numer * (1.0 / total)
    image_ref[rows:, :] = jnp.zeros((EXTRA, image_ref.shape[1]), jnp.float32)
    image_ref[rows : rows + lse.shape[0], :LANES] = lse


def swap(value, axis, distance):
    n = lax.axis_size(axis)
    return lax.ppermute(value, axis, [(i, i ^ distance) for i in range(n)])


def bits_of(n):
    return [1 << b for b in range(n.bit_length() - 1)]


def on_device(source, target, log_source_mass, log_target_mass):
    n_src, width = source.shape
    n_tgt = target.shape[0]
    n_col, n_row = lax.axis_size("col"), lax.axis_size("row")
    count = n_src // n_col
    n_x = 1 << (len(bits_of(n_col)) // 2)
    n_z = n_col // n_x
    y_bits = bits_of(n_row)[1:]
    ls = log_source_mass.reshape(-1, LANES)
    lt = log_target_mass.reshape(-1, LANES)
    src_dense, tgt_dense = f32(*ls.shape), f32(*lt.shape)
    half = n_tgt // 2

    part = f32(n_tgt // n_row, width)
    pieces = {0: call(quarter_kernel, part, target)}
    for distance in [bit for bit in bits_of(n_col) if bit > n_x][::-1]:
        pieces |= {k ^ distance: swap(piece, "col", distance) for k, piece in pieces.items()}
    early = swap(pieces[0], "col", 1)

    def along_y(piece):
        held = [piece]
        for distance in y_bits:
            held += [swap(one, "row", distance) for one in held]
        return held

    tile, lse, sqy = call(first_kernel, (f32(n_tgt, n_src), src_dense, tgt_dense), target, source, lt)
    sqx = call(norms_kernel, src_dense, source)
    cut = early_rows(part.shape[0])
    for step in range(ITERS):
        if step > 0:
            apart = [0, 1] + [k for k in pieces if k > 1]
            lse, late = call(
                lambda *refs: targets_kernel(n_row, *refs),
                (src_dense, f32((len(apart) - 2) * part.shape[0] - cut, width)),
                tile, lt, sqy, *parts, *[pieces[k] for k in apart[2:]], early[-1],
            )
            late = along_y(late)
        if step > 0:
            rest = bits_of(n_col)
        else:
            group, rest = [*bits_of(n_x), n_col // 2], [bit for bit in bits_of(n_col // 2) if bit >= n_x]
            ways = [0]
            for bit in group:
                ways += [way | bit for way in ways]
            near = [lse] + [swap(lse, "col", way) for way in ways[:0:-1]]
            far = [k for k in pieces if k > 0]
            lse, early, *copies = call(
                lambda *refs: merge_kernel(len(ways), *refs),
                (src_dense, f32(part.shape[0] + cut, width), *(part,) * len(far)),
                *near, *[pieces[k] for k in far], early,
            )
            early = along_y(early)
            pieces |= dict(zip(far, copies))
            for bit in bits_of(n_x)[::-1]:
                pieces |= {k ^ bit: swap(piece, "col", bit) for k, piece in pieces.items() if k ^ bit != 1}
        for distance in rest[:-1]:
            lse = merge_all([lse, swap(lse, "col", distance)])
        parts = [lse, swap(lse, "col", rest[-1])]
        if step < ITERS - 1:
            lse = call(lambda *refs: sources_kernel(2, *refs), tgt_dense, tile, ls, sqx, *parts)
        else:
            lse, sent, mine = call(
                last_sources_kernel,
                (tgt_dense, f32(half, width), f32(half, width)),
                tile, source, ls, sqx, *parts, late[-1],
            )
        parts = [lse] + [swap(lse, "row", k) for k in range(1, n_row)]
    total = merge_all(parts)

    bias = lt * LOG2E + (sqy - total) - sqy
    biases = [bias] + [swap(bias, "col", distance) for distance in apart[1:]]

    mine, came = call(
        share_kernel,
        (f32(half, width), f32(len(apart) - 1, n_row // 2, *part.shape)),
        mine, swap(sent, "row", 1), total, lse, parts[1], *early, *late,
    )
    rest = bits_of(n_row)[1:]
    for distance in rest[:-1]:
        mine, = call(add_kernel, (f32(half, width),), mine, swap(mine, "row", distance))
    mine_came = swap(mine, "row", rest[-1])

    n_all = len(apart) * n_tgt
    all_y, inner = call(
        lambda *refs: scores_kernel(n_x, *refs),
        (bf16(n_all, width), f32(2 * count, n_all)),
        source, target, came, swap(came, "row", 1),
        limit=32,
    )

    def image(flip):
        return call(
            lambda *refs: image_kernel(flip, *refs),
            f32(count + EXTRA, width),
            inner, all_y, *biases[::-1],
            scratch=[pltpu.VMEM((count, n_all), jnp.float32)],
        )

    came = swap(image(1), "col", n_x)
    own = image(0)
    n_last = 4
    mine = call(add_kernel, (f32(half // n_last, width),) * n_last, mine, mine_came)
    target_image = call(
        place_kernel, f32(n_tgt, width), *mine, *[swap(piece, "row", 1) for piece in mine],
        out_specs=HBM, scratch=[DMA((2 * n_last,))],
    )
    source_image = call(
        join_kernel, f32(count, width), own, came,
        out_specs=HBM, scratch=[pltpu.VMEM((count, width), jnp.float32), DMA((4,))],
    )
    return source_image, target_image


def solution(mesh):
    in_specs = (P("row", None), P("col", None), P("row"), P("col"))
    out_specs = (P(("row", "col"), None), P("col", None))
    return jax.shard_map(
        on_device, mesh=mesh, in_specs=in_specs, out_specs=out_specs, check_vma=False
    )
```

```python
import math

import jax
import jax.numpy as jnp
from jax import lax
from jax.experimental import pallas as pl
from jax.experimental.pallas import tpu as pltpu
from jax.sharding import PartitionSpec as P

ITERS = 2
BLUR = 0.1
LOG2E = math.log2(math.e)
LANES = 128
NT_DIMS = (((1,), (1,)), ((), ()))
VMEM = pl.BlockSpec(memory_space=pltpu.VMEM)
HBM = pl.BlockSpec(memory_space=pltpu.HBM)
ANY = pl.BlockSpec(memory_space=pl.ANY)
DMA = pltpu.SemaphoreType.DMA


def call(kernel, out_shape, *args, in_specs=None, out_specs=None, scratch=(), limit=24):
    return pl.pallas_call(
        kernel,
        out_shape=out_shape,
        in_specs=in_specs or [VMEM] * len(args),
        out_specs=out_specs or jax.tree.map(lambda _: VMEM, out_shape),
        scratch_shapes=list(scratch),
        compiler_params=pltpu.CompilerParams(vmem_limit_bytes=limit << 20),
    )(*args)


def f32(*shape):
    return jax.ShapeDtypeStruct(shape, jnp.float32)


def bf16(*shape):
    return jax.ShapeDtypeStruct(shape, jnp.bfloat16)


def scale(width):
    return LOG2E / (width * BLUR)


def to_column(dense):
    n = dense.shape[0]
    square = jnp.concatenate([dense, jnp.zeros((LANES - n, LANES), jnp.float32)], axis=0).T
    return jnp.concatenate([square[:, b : b + 1] for b in range(n)], axis=0)


def to_dense(columns):
    lane = lax.broadcasted_iota(jnp.int32, (LANES, LANES), 1)
    square = jnp.zeros((LANES, LANES), jnp.float32)
    for b, column in enumerate(columns):
        square = jnp.where(lane == b, column, square)
    return square.T[: len(columns)]


def to_row(dense):
    return jnp.concatenate([dense[b : b + 1, :] for b in range(dense.shape[0])], axis=1)


def over_targets(scores):
    peak = jnp.max(scores, axis=0, keepdims=True)
    total = jnp.sum(jnp.exp2(scores - peak), axis=0, keepdims=True)
    return peak + jnp.log2(total)


def half_at(ref, place):
    half = ref.shape[0] // 2
    return ref[pl.ds(place * half, half), :]


def merge_all(parts):
    peak = parts[0]
    for part in parts[1:]:
        peak = jnp.maximum(peak, part)
    return peak + jnp.log2(sum(jnp.exp2(part - peak) for part in parts))


def norms(block):
    wide = block.astype(jnp.float32)
    return jnp.sum(wide * wide, axis=1, keepdims=True) * scale(block.shape[1])


def quarter_kernel(y_ref, out_ref):
    rows = out_ref.shape[0]
    out_ref[...] = y_ref[pl.ds(pl.multiple_of(lax.axis_index("row") * rows, rows), rows), :].astype(jnp.float32)


def norms_kernel(x_ref, sqx_ref):
    columns = [norms(x_ref[pl.ds(b, LANES), :]) for b in range(0, x_ref.shape[0], LANES)]
    sqx_ref[...] = to_dense(columns)


def first_kernel(y_ref, x_ref, lt_ref, tile_ref, lse_ref, sqy_ref):
    wide = 256
    y = y_ref[...]
    unit = scale(y.shape[1])
    sqy = norms(y)
    sqy_ref[...] = to_dense([sqy[b : b + LANES] for b in range(0, y.shape[0], LANES)])
    bias = to_column(lt_ref[...]) * LOG2E - sqy
    for b in range(x_ref.shape[0] // wide):
        at = pl.ds(b * wide, wide)
        x = x_ref[at, :]
        tile = lax.dot_general(y, x, NT_DIMS, preferred_element_type=jnp.float32) * (2.0 * unit)
        tile_ref[:, at] = tile
        row = over_targets(tile + bias)
        for c in range(wide // LANES):
            lse_ref[pl.ds(b * (wide // LANES) + c, 1), :] = row[:, c * LANES : (c + 1) * LANES]


def early_rows(rows):
    return rows // 2


def targets_kernel(n_parts, tile_ref, lt_ref, sqy_ref, *refs):
    parts, pieces, (lse_ref, pack_ref) = refs[:n_parts], refs[n_parts:-3], refs[-2:]
    rows = pieces[0].shape[0]
    cut = early_rows(rows)
    pack_ref[: rows - cut, :] = pieces[0][cut:, :]
    for k, piece in enumerate(pieces[1:], 1):
        pack_ref[pl.ds(rows * k - cut, rows), :] = piece[...]
    g_pot = sqy_ref[...] - merge_all([ref[...] for ref in parts])
    bias = to_column(lt_ref[...] * LOG2E + g_pot - sqy_ref[...])
    for b in range(tile_ref.shape[1] // LANES):
        lse_ref[pl.ds(b, 1), :] = over_targets(tile_ref[:, pl.ds(b * LANES, LANES)] + bias)


def merge_kernel(n_parts, *refs):
    parts, refs = refs[:n_parts], refs[n_parts:]
    n_pieces = len(refs) // 2
    pieces, (out_ref, pack_ref, *copies) = refs[:n_pieces], refs[n_pieces:]
    out_ref[...] = merge_all([ref[...] for ref in parts])
    rows = pieces[-1].shape[0]
    pack_ref[:rows, :] = pieces[-1][...]
    pack_ref[rows:, :] = pieces[0][: early_rows(rows), :]
    for piece, copy in zip(pieces[:-1], copies):
        copy[...] = piece[...]


def sources_kernel(n_parts, tile_ref, ls_ref, sqx_ref, *refs):
    bias = source_bias(ls_ref, sqx_ref, refs[:n_parts])
    columns = []
    for j in range(tile_ref.shape[0] // LANES):
        peak, total, _ = over_sources(tile_ref, pl.ds(j * LANES, LANES), bias)
        columns.append(peak + jnp.log2(total))
    refs[-1][...] = to_dense(columns)


def last_sources_kernel(tile_ref, x_ref, ls_ref, sqx_ref, *refs):
    parts, (lse_ref, sent_ref, mine_ref) = refs[:-4], refs[-3:]
    bias = source_bias(ls_ref, sqx_ref, parts)
    x = x_ref[...]
    n_rows = mine_ref.shape[0] // LANES
    core = lax.axis_index("row") % 2
    for out_ref, place in ((sent_ref, 1 - core), (mine_ref, core)):
        columns = []
        for j in range(n_rows):
            at = pl.ds(pl.multiple_of((place * n_rows + j) * LANES, LANES), LANES)
            peak, total, exps = over_sources(tile_ref, at, bias)
            columns.append(peak + jnp.log2(total))
            weights = jnp.concatenate([block.astype(jnp.bfloat16) for block in exps], axis=1)
            mean = jnp.dot(weights, x, preferred_element_type=jnp.float32)
            out_ref[pl.ds(j * LANES, LANES), :] = mean * (1.0 / total)
        lse_ref[pl.ds(place * n_rows, n_rows), :] = to_dense(columns)


def source_bias(ls_ref, sqx_ref, parts):
    f_pot = sqx_ref[...] - merge_all([ref[...] for ref in parts])
    return ls_ref[...] * LOG2E + f_pot - sqx_ref[...]


def over_sources(tile_ref, at, bias):
    scores = [tile_ref[at, pl.ds(b * LANES, LANES)] + bias[b : b + 1, :] for b in range(bias.shape[0])]
    top = scores[0]
    for block in scores[1:]:
        top = jnp.maximum(top, block)
    peak = jnp.max(top, axis=1, keepdims=True)
    exps = [jnp.exp2(block - peak) for block in scores]
    return peak, jnp.sum(sum(exps), axis=1, keepdims=True), exps


def share_kernel(mine_ref, came_ref, total_ref, lse_ref, came_lse_ref, out_ref):
    half = mine_ref.shape[0] // LANES
    at = pl.ds(lax.axis_index("row") % 2 * half, half)
    total = total_ref[0, at, :]
    share = to_column(jnp.exp2(lse_ref[0, at, :] - total))
    came_share = to_column(jnp.exp2(came_lse_ref[0, at, :] - total))
    out_ref[...] = mine_ref[...] * share + came_ref[...] * came_share


def stack_kernel(*refs):
    for k, ref in enumerate(refs[-3::-1]):
        refs[-1][k] = ref[...]


def pack_kernel(*refs):
    pieces, pack_ref = refs[:-2], refs[-1]
    n_shards, n_y, rows, _ = pack_ref.shape
    y = lax.axis_index("row") // 2
    early, late = pieces[:n_y], pieces[n_y:]
    cut = early_rows(rows)
    for j in range(n_y):
        place = y ^ j
        pack_ref[0, place] = early[j][:rows, :]
        pack_ref[1, place, :cut, :] = early[j][rows:, :]
        pack_ref[1, place, cut:, :] = late[j][: rows - cut, :]
        for k in range(2, n_shards):
            pack_ref[k, place] = late[j][pl.ds((k - 1) * rows - cut, rows), :]


def add_kernel(one_ref, two_ref, *out_refs):
    rows = out_refs[0].shape[0]
    for k, ref in enumerate(out_refs):
        at = pl.ds(k * rows, rows)
        ref[...] = one_ref[at, :] + two_ref[at, :]


def join_kernel(*refs):
    parts, out_ref = refs[:-1], refs[-1]
    rows = out_ref.shape[0]
    lses = [ref[rows : rows + pl.cdiv(rows, LANES), :LANES] for ref in parts]
    whole = merge_all(lses)
    shares = [to_column(jnp.exp2(lse - whole))[:rows] for lse in lses]
    out_ref[...] = sum(ref[:rows, :] * share for ref, share in zip(parts, shares))


def place_kernel(*refs):
    n = (len(refs) - 2) // 2
    mine, others, out_hbm, sems = refs[:n], refs[n : 2 * n], refs[-2], refs[-1]
    rows = mine[0].shape[0]
    core = lax.axis_index("row") % 2
    copies = []
    for place, pieces in ((core, mine), (1 - core, others)):
        for k, piece in enumerate(pieces):
            at = pl.ds(pl.multiple_of((place * n + k) * rows, rows), rows)
            copies.append(pltpu.make_async_copy(piece, out_hbm.at[at, :], sems.at[len(copies)]))
            copies[-1].start()
    for copy in copies:
        copy.wait()


def scores_kernel(near, x_ref, own_ref, mine_ref, other_ref, y_ref, inner_ref):
    rows = inner_ref.shape[0] // 2
    n_tgt = own_ref.shape[0]
    n_came, n_y, part, _ = mine_ref.shape
    col, core = lax.axis_index("col"), lax.axis_index("row") % 2
    y_ref[:n_tgt, :] = own_ref[...]
    for k in range(n_came):
        for ref, place in ((mine_ref, core), (other_ref, 1 - core)):
            for y in range(n_y):
                start = (k + 1) * n_tgt + (2 * y + place) * part
                y_ref[pl.ds(pl.multiple_of(start, part), part), :] = ref[k, y].astype(jnp.bfloat16)
    blocks = [x_ref[pl.ds(pl.multiple_of((col ^ flip) * rows, rows), rows), :] for flip in (0, near)]
    x = jnp.concatenate(blocks, axis=0)
    unit = scale(x.shape[1])
    for b in range(y_ref.shape[0] // n_tgt):
        at = pl.ds(b * n_tgt, n_tgt)
        inner_ref[:, at] = lax.dot_general(x, y_ref[at, :], NT_DIMS, preferred_element_type=jnp.float32) * (2.0 * unit)


EXTRA = 8


def images(flip, inner_ref, y_ref, totals_ref, scores_ref):
    rows = scores_ref.shape[0]
    n_shards = totals_ref.shape[0]
    n_tgt = y_ref.shape[0] // n_shards
    block = pl.ds(flip * rows, rows)
    peak = jnp.full((rows, 1), -jnp.inf, jnp.float32)
    for k in range(n_shards):
        at = pl.ds(k * n_tgt, n_tgt)
        scores = inner_ref[block, at] - to_row(totals_ref[k])
        scores_ref[:, at] = scores
        peak = jnp.maximum(peak, jnp.max(scores, axis=1, keepdims=True))
    total = jnp.zeros((rows, 1), jnp.float32)
    numer = jnp.zeros((rows, y_ref.shape[1]), jnp.float32)
    for k in range(n_shards):
        at = pl.ds(k * n_tgt, n_tgt)
        plan = jnp.exp2(scores_ref[:, at] - peak)
        total = total + jnp.sum(plan, axis=1, keepdims=True)
        numer = numer + jnp.dot(plan.astype(jnp.bfloat16), y_ref[at, :], preferred_element_type=jnp.float32)
    return numer, total, peak


def lanes_of(column):
    rows = column.shape[0]
    if rows % LANES:
        column = jnp.concatenate([column, jnp.zeros((-rows % LANES, 1), jnp.float32)], axis=0)
    return to_dense([column[b : b + LANES] for b in range(0, column.shape[0], LANES)])


EXTRA = 8


def image_kernel(flip, inner_ref, y_ref, totals_ref, *refs):
    image_ref, scores_ref = refs[-2:]
    numer, total, peak = images(flip, inner_ref, y_ref, totals_ref, scores_ref)
    rows = numer.shape[0]
    lse = lanes_of(peak + jnp.log2(total))
    image_ref[:rows, :] = numer * (1.0 / total)
    image_ref[rows:, :] = jnp.zeros((EXTRA, image_ref.shape[1]), jnp.float32)
    image_ref[rows : rows + lse.shape[0], :LANES] = lse


def swap(value, axis, distance):
    n = lax.axis_size(axis)
    return lax.ppermute(value, axis, [(i, i ^ distance) for i in range(n)])


def bits_of(n):
    return [1 << b for b in range(n.bit_length() - 1)]


def on_device(source, target, log_source_mass, log_target_mass):
    n_src, width = source.shape
    n_tgt = target.shape[0]
    n_col, n_row = lax.axis_size("col"), lax.axis_size("row")
    count = n_src // n_col
    n_x = 1 << (len(bits_of(n_col)) // 2)
    n_z = n_col // n_x
    y_bits = bits_of(n_row)[1:]
    ls = log_source_mass.reshape(-1, LANES)
    lt = log_target_mass.reshape(-1, LANES)
    src_dense, tgt_dense = f32(*ls.shape), f32(*lt.shape)
    half = n_tgt // 2

    part = f32(n_tgt // n_row, width)
    pieces = {0: call(quarter_kernel, part, target)}
    for distance in [bit for bit in bits_of(n_col) if bit > n_x][::-1]:
        pieces |= {k ^ distance: swap(piece, "col", distance) for k, piece in pieces.items()}
    early = swap(pieces[0], "col", 1)

    def along_y(piece):
        held = [piece]
        for distance in y_bits:
            held += [swap(one, "row", distance) for one in held]
        return held

    tile, lse, sqy = call(first_kernel, (f32(n_tgt, n_src), src_dense, tgt_dense), target, source, lt)
    sqx = call(norms_kernel, src_dense, source)
    cut = early_rows(part.shape[0])
    for step in range(ITERS):
        if step > 0:
            apart = [0, 1] + [k for k in pieces if k > 1]
            lse, late = call(
                lambda *refs: targets_kernel(n_row, *refs),
                (src_dense, f32((len(apart) - 2) * part.shape[0] - cut, width)),
                tile, lt, sqy, *parts, *[pieces[k] for k in apart[2:]], early[-1],
            )
            late = along_y(late)
        if step > 0:
            rest = bits_of(n_col)
        else:
            group, rest = [*bits_of(n_x), n_col // 2], [bit for bit in bits_of(n_col // 2) if bit >= n_x]
            ways = [0]
            for bit in group:
                ways += [way | bit for way in ways]
            near = [lse] + [swap(lse, "col", way) for way in ways[:0:-1]]
            far = [k for k in pieces if k > 0]
            lse, early, *copies = call(
                lambda *refs: merge_kernel(len(ways), *refs),
                (src_dense, f32(part.shape[0] + cut, width), *(part,) * len(far)),
                *near, *[pieces[k] for k in far], early,
            )
            early = along_y(early)
            pieces |= dict(zip(far, copies))
            for bit in bits_of(n_x)[::-1]:
                pieces |= {k ^ bit: swap(piece, "col", bit) for k, piece in pieces.items() if k ^ bit != 1}
        for distance in rest[:-1]:
            lse = merge_all([lse, swap(lse, "col", distance)])
        parts = [lse, swap(lse, "col", rest[-1])]
        if step < ITERS - 1:
            lse = call(lambda *refs: sources_kernel(2, *refs), tgt_dense, tile, ls, sqx, *parts)
        else:
            lse, sent, mine = call(
                last_sources_kernel,
                (tgt_dense, f32(half, width), f32(half, width)),
                tile, source, ls, sqx, *parts, late[-1],
            )
        if step < ITERS - 1:
            parts = [lse] + [swap(lse, "row", k) for k in range(1, n_row)]

    came = call(pack_kernel, f32(len(apart) - 1, n_row // 2, *part.shape), *early, *late, lse)
    n_all = len(apart) * n_tgt
    all_y, inner = call(
        lambda *refs: scores_kernel(n_x, *refs),
        (bf16(n_all, width), f32(2 * count, n_all)),
        source, target, came, swap(came, "row", 1),
        limit=32,
    )

    part_total = (lse - sqy) - (lt * LOG2E - sqy)
    others = [swap(part_total, "col", distance) for distance in apart[:0:-1]]
    totals = call(stack_kernel, f32(len(apart), *lt.shape), *others, part_total, inner)
    parts = [totals] + [swap(totals, "row", k) for k in range(1, n_row)]
    totals = merge_all(parts)

    mine = call(share_kernel, f32(half, width), mine, swap(sent, "row", 1), totals, parts[0], parts[1])
    rest = bits_of(n_row)[1:]
    for distance in rest[:-1]:
        mine, = call(add_kernel, (f32(half, width),), mine, swap(mine, "row", distance))
    mine_came = swap(mine, "row", rest[-1])

    def image(flip, *after):
        return call(
            lambda *refs: image_kernel(flip, *refs),
            f32(count + EXTRA, width),
            inner, all_y, totals, *after,
            scratch=[pltpu.VMEM((count, n_all), jnp.float32)],
        )

    came = swap(image(1), "col", n_x)
    n_last = 4
    mine = call(add_kernel, (f32(half // n_last, width),) * n_last, mine, mine_came)
    other = [swap(piece, "row", 1) for piece in mine]
    target_image = call(
        place_kernel, f32(n_tgt, width), *mine, *other,
        out_specs=HBM, scratch=[DMA((2 * n_last,))],
    )
    own = image(0, *other)
    source_image = call(join_kernel, f32(count, width), own, came)
    return source_image, target_image


def solution(mesh):
    in_specs = (P("row", None), P("col", None), P("row"), P("col"))
    out_specs = (P(("row", "col"), None), P("col", None))
    return jax.shard_map(
        on_device, mesh=mesh, in_specs=in_specs, out_specs=out_specs, check_vma=False
    )
```

```python
import math

import jax
import jax.numpy as jnp
from jax import lax
from jax.experimental import pallas as pl
from jax.experimental.pallas import tpu as pltpu
from jax.sharding import PartitionSpec as P

ITERS = 2
BLUR = 0.1
LOG2E = math.log2(math.e)
LANES = 128
NT_DIMS = (((1,), (1,)), ((), ()))
VMEM = pl.BlockSpec(memory_space=pltpu.VMEM)
HBM = pl.BlockSpec(memory_space=pltpu.HBM)
ANY = pl.BlockSpec(memory_space=pl.ANY)
DMA = pltpu.SemaphoreType.DMA


def call(kernel, out_shape, *args, in_specs=None, out_specs=None, scratch=(), limit=24):
    return pl.pallas_call(
        kernel,
        out_shape=out_shape,
        in_specs=in_specs or [VMEM] * len(args),
        out_specs=out_specs or jax.tree.map(lambda _: VMEM, out_shape),
        scratch_shapes=list(scratch),
        compiler_params=pltpu.CompilerParams(vmem_limit_bytes=limit << 20),
    )(*args)


def f32(*shape):
    return jax.ShapeDtypeStruct(shape, jnp.float32)


def bf16(*shape):
    return jax.ShapeDtypeStruct(shape, jnp.bfloat16)


def scale(width):
    return LOG2E / (width * BLUR)


def to_column(dense):
    n = dense.shape[0]
    square = jnp.concatenate([dense, jnp.zeros((LANES - n, LANES), jnp.float32)], axis=0).T
    return jnp.concatenate([square[:, b : b + 1] for b in range(n)], axis=0)


def to_dense(columns):
    lane = lax.broadcasted_iota(jnp.int32, (LANES, LANES), 1)
    square = jnp.zeros((LANES, LANES), jnp.float32)
    for b, column in enumerate(columns):
        square = jnp.where(lane == b, column, square)
    return square.T[: len(columns)]


def to_row(dense):
    return jnp.concatenate([dense[b : b + 1, :] for b in range(dense.shape[0])], axis=1)


def over_targets(scores):
    peak = jnp.max(scores, axis=0, keepdims=True)
    total = jnp.sum(jnp.exp2(scores - peak), axis=0, keepdims=True)
    return peak + jnp.log2(total)


def half_at(ref, place):
    half = ref.shape[0] // 2
    return ref[pl.ds(place * half, half), :]


def merge_all(parts):
    peak = parts[0]
    for part in parts[1:]:
        peak = jnp.maximum(peak, part)
    return peak + jnp.log2(sum(jnp.exp2(part - peak) for part in parts))


def norms(block):
    wide = block.astype(jnp.float32)
    return jnp.sum(wide * wide, axis=1, keepdims=True) * scale(block.shape[1])


def quarter_kernel(y_ref, out_ref):
    rows = out_ref.shape[0]
    out_ref[...] = y_ref[pl.ds(pl.multiple_of(lax.axis_index("row") * rows, rows), rows), :].astype(jnp.float32)


def norms_kernel(x_ref, sqx_ref):
    columns = [norms(x_ref[pl.ds(b, LANES), :]) for b in range(0, x_ref.shape[0], LANES)]
    sqx_ref[...] = to_dense(columns)


def first_kernel(y_ref, x_ref, lt_ref, tile_ref, lse_ref, sqy_ref):
    wide = 256
    y = y_ref[...]
    unit = scale(y.shape[1])
    sqy = norms(y)
    sqy_ref[...] = to_dense([sqy[b : b + LANES] for b in range(0, y.shape[0], LANES)])
    bias = to_column(lt_ref[...]) * LOG2E - sqy
    for b in range(x_ref.shape[0] // wide):
        at = pl.ds(b * wide, wide)
        x = x_ref[at, :]
        tile = lax.dot_general(y, x, NT_DIMS, preferred_element_type=jnp.float32) * (2.0 * unit)
        tile_ref[:, at] = tile
        row = over_targets(tile + bias)
        for c in range(wide // LANES):
            lse_ref[pl.ds(b * (wide // LANES) + c, 1), :] = row[:, c * LANES : (c + 1) * LANES]


def early_rows(rows):
    return rows // 2


def targets_kernel(n_parts, tile_ref, lt_ref, sqy_ref, *refs):
    parts, pieces, (lse_ref, pack_ref) = refs[:n_parts], refs[n_parts:-3], refs[-2:]
    rows = pieces[0].shape[0]
    cut = early_rows(rows)
    pack_ref[: rows - cut, :] = pieces[0][cut:, :]
    for k, piece in enumerate(pieces[1:], 1):
        pack_ref[pl.ds(rows * k - cut, rows), :] = piece[...]
    g_pot = sqy_ref[...] - merge_all([ref[...] for ref in parts])
    bias = to_column(lt_ref[...] * LOG2E + g_pot - sqy_ref[...])
    for b in range(tile_ref.shape[1] // LANES):
        lse_ref[pl.ds(b, 1), :] = over_targets(tile_ref[:, pl.ds(b * LANES, LANES)] + bias)


def merge_kernel(n_parts, *refs):
    parts, refs = refs[:n_parts], refs[n_parts:]
    n_pieces = len(refs) // 2
    pieces, (out_ref, pack_ref, *copies) = refs[:n_pieces], refs[n_pieces:]
    out_ref[...] = merge_all([ref[...] for ref in parts])
    rows = pieces[-1].shape[0]
    pack_ref[:rows, :] = pieces[-1][...]
    pack_ref[rows:, :] = pieces[0][: early_rows(rows), :]
    for piece, copy in zip(pieces[:-1], copies):
        copy[...] = piece[...]


def sources_kernel(n_parts, tile_ref, ls_ref, sqx_ref, *refs):
    bias = source_bias(ls_ref, sqx_ref, refs[:n_parts])
    columns = []
    for j in range(tile_ref.shape[0] // LANES):
        peak, total, _ = over_sources(tile_ref, pl.ds(j * LANES, LANES), bias)
        columns.append(peak + jnp.log2(total))
    refs[-1][...] = to_dense(columns)


def last_sources_kernel(tile_ref, x_ref, ls_ref, sqx_ref, *refs):
    parts, (lse_ref, sent_ref, mine_ref, weights_ref) = refs[:-5], refs[-4:]
    bias = source_bias(ls_ref, sqx_ref, parts)
    half = mine_ref.shape[0]
    n_rows = half // LANES
    core = lax.axis_index("row") % 2
    inverse = []
    for k, place in enumerate((1 - core, core)):
        columns = []
        for j in range(n_rows):
            at = pl.ds(pl.multiple_of((place * n_rows + j) * LANES, LANES), LANES)
            peak, total, exps = over_sources(tile_ref, at, bias)
            columns.append(peak + jnp.log2(total))
            inverse.append(1.0 / total)
            for b, block in enumerate(exps):
                weights_ref[pl.ds((k * n_rows + j) * LANES, LANES), pl.ds(b * LANES, LANES)] = block.astype(jnp.bfloat16)
        lse_ref[pl.ds(place * n_rows, n_rows), :] = to_dense(columns)
    mean = jnp.dot(weights_ref[...], x_ref[...], preferred_element_type=jnp.float32)
    sent_ref[...] = mean[:half] * jnp.concatenate(inverse[:n_rows], axis=0)
    mine_ref[...] = mean[half:] * jnp.concatenate(inverse[n_rows:], axis=0)


def source_bias(ls_ref, sqx_ref, parts):
    f_pot = sqx_ref[...] - merge_all([ref[...] for ref in parts])
    return ls_ref[...] * LOG2E + f_pot - sqx_ref[...]


def over_sources(tile_ref, at, bias):
    scores = [tile_ref[at, pl.ds(b * LANES, LANES)] + bias[b : b + 1, :] for b in range(bias.shape[0])]
    top = scores[0]
    for block in scores[1:]:
        top = jnp.maximum(top, block)
    peak = jnp.max(top, axis=1, keepdims=True)
    exps = [jnp.exp2(block - peak) for block in scores]
    return peak, jnp.sum(sum(exps), axis=1, keepdims=True), exps


def share_kernel(mine_ref, came_ref, total_ref, lse_ref, came_lse_ref, *refs):
    pieces, (out_ref, pack_ref) = refs[:-2], refs[-2:]
    half = mine_ref.shape[0] // LANES
    at = pl.ds(lax.axis_index("row") % 2 * half, half)
    total = total_ref[at, :]
    share, came_share = to_column(jnp.exp2(lse_ref[at, :] - total)), to_column(jnp.exp2(came_lse_ref[at, :] - total))
    out_ref[...] = mine_ref[...] * share + came_ref[...] * came_share
    n_shards, n_y, rows, _ = pack_ref.shape
    y = lax.axis_index("row") // 2
    early, late = pieces[:n_y], pieces[n_y:]
    cut = early_rows(rows)
    for j in range(n_y):
        place = y ^ j
        pack_ref[0, place] = early[j][:rows, :]
        pack_ref[1, place, :cut, :] = early[j][rows:, :]
        pack_ref[1, place, cut:, :] = late[j][: rows - cut, :]
        for k in range(2, n_shards):
            pack_ref[k, place] = late[j][pl.ds((k - 1) * rows - cut, rows), :]


def add_kernel(one_ref, two_ref, *out_refs):
    rows = out_refs[0].shape[0]
    for k, ref in enumerate(out_refs):
        at = pl.ds(k * rows, rows)
        ref[...] = one_ref[at, :] + two_ref[at, :]


def join_kernel(*refs):
    parts, out_ref = refs[:-1], refs[-1]
    rows = out_ref.shape[0]
    lses = [ref[rows : rows + pl.cdiv(rows, LANES), :LANES] for ref in parts]
    whole = merge_all(lses)
    shares = [to_column(jnp.exp2(lse - whole))[:rows] for lse in lses]
    out_ref[...] = sum(ref[:rows, :] * share for ref, share in zip(parts, shares))


def place_kernel(*refs):
    n = (len(refs) - 2) // 2
    mine, others, out_hbm, sems = refs[:n], refs[n : 2 * n], refs[-2], refs[-1]
    rows = mine[0].shape[0]
    core = lax.axis_index("row") % 2
    copies = []
    for place, pieces in ((core, mine), (1 - core, others)):
        for k, piece in enumerate(pieces):
            at = pl.ds(pl.multiple_of((place * n + k) * rows, rows), rows)
            copies.append(pltpu.make_async_copy(piece, out_hbm.at[at, :], sems.at[len(copies)]))
            copies[-1].start()
    for copy in copies:
        copy.wait()


def scores_kernel(near, x_ref, own_ref, mine_ref, other_ref, y_ref, inner_ref):
    rows = inner_ref.shape[0] // 2
    n_tgt = own_ref.shape[0]
    n_came, n_y, part, _ = mine_ref.shape
    col, core = lax.axis_index("col"), lax.axis_index("row") % 2
    y_ref[:n_tgt, :] = own_ref[...]
    for k in range(n_came):
        for ref, place in ((mine_ref, core), (other_ref, 1 - core)):
            for y in range(n_y):
                start = (k + 1) * n_tgt + (2 * y + place) * part
                y_ref[pl.ds(pl.multiple_of(start, part), part), :] = ref[k, y].astype(jnp.bfloat16)
    blocks = [x_ref[pl.ds(pl.multiple_of((col ^ flip) * rows, rows), rows), :] for flip in (0, near)]
    x = jnp.concatenate(blocks, axis=0)
    unit = scale(x.shape[1])
    for b in range(y_ref.shape[0] // n_tgt):
        at = pl.ds(b * n_tgt, n_tgt)
        inner_ref[:, at] = lax.dot_general(x, y_ref[at, :], NT_DIMS, preferred_element_type=jnp.float32) * (2.0 * unit)


EXTRA = 8


def images(flip, inner_ref, y_ref, bias_refs, scores_ref):
    rows = scores_ref.shape[0]
    n_shards = len(bias_refs)
    n_tgt = y_ref.shape[0] // n_shards
    block = pl.ds(flip * rows, rows)
    peak = jnp.full((rows, 1), -jnp.inf, jnp.float32)
    for k, bias_ref in enumerate(bias_refs[::-1]):
        at = pl.ds(k * n_tgt, n_tgt)
        scores = inner_ref[block, at] + to_row(bias_ref[...])
        scores_ref[:, at] = scores
        peak = jnp.maximum(peak, jnp.max(scores, axis=1, keepdims=True))
    total = jnp.zeros((rows, 1), jnp.float32)
    numer = jnp.zeros((rows, y_ref.shape[1]), jnp.float32)
    for k in range(n_shards):
        at = pl.ds(k * n_tgt, n_tgt)
        plan = jnp.exp2(scores_ref[:, at] - peak)
        total = total + jnp.sum(plan, axis=1, keepdims=True)
        numer = numer + jnp.dot(plan.astype(jnp.bfloat16), y_ref[at, :], preferred_element_type=jnp.float32)
    return numer, total, peak


def lanes_of(column):
    rows = column.shape[0]
    if rows % LANES:
        column = jnp.concatenate([column, jnp.zeros((-rows % LANES, 1), jnp.float32)], axis=0)
    return to_dense([column[b : b + LANES] for b in range(0, column.shape[0], LANES)])


EXTRA = 8


def image_kernel(flip, inner_ref, y_ref, *refs):
    bias_refs, (image_ref, scores_ref) = refs[:-2], refs[-2:]
    numer, total, peak = images(flip, inner_ref, y_ref, bias_refs, scores_ref)
    rows = numer.shape[0]
    lse = lanes_of(peak + jnp.log2(total))
    image_ref[:rows, :] = numer * (1.0 / total)
    image_ref[rows:, :] = jnp.zeros((EXTRA, image_ref.shape[1]), jnp.float32)
    image_ref[rows : rows + lse.shape[0], :LANES] = lse


def swap(value, axis, distance):
    n = lax.axis_size(axis)
    return lax.ppermute(value, axis, [(i, i ^ distance) for i in range(n)])


def bits_of(n):
    return [1 << b for b in range(n.bit_length() - 1)]


def on_device(source, target, log_source_mass, log_target_mass):
    n_src, width = source.shape
    n_tgt = target.shape[0]
    n_col, n_row = lax.axis_size("col"), lax.axis_size("row")
    count = n_src // n_col
    n_x = 1 << (len(bits_of(n_col)) // 2)
    n_z = n_col // n_x
    y_bits = bits_of(n_row)[1:]
    ls = log_source_mass.reshape(-1, LANES)
    lt = log_target_mass.reshape(-1, LANES)
    src_dense, tgt_dense = f32(*ls.shape), f32(*lt.shape)
    half = n_tgt // 2

    part = f32(n_tgt // n_row, width)
    pieces = {0: call(quarter_kernel, part, target)}
    for distance in [bit for bit in bits_of(n_col) if bit > n_x][::-1]:
        pieces |= {k ^ distance: swap(piece, "col", distance) for k, piece in pieces.items()}
    early = swap(pieces[0], "col", 1)

    def along_y(piece):
        held = [piece]
        for distance in y_bits:
            held += [swap(one, "row", distance) for one in held]
        return held

    tile, lse, sqy = call(first_kernel, (f32(n_tgt, n_src), src_dense, tgt_dense), target, source, lt)
    sqx = call(norms_kernel, src_dense, source)
    cut = early_rows(part.shape[0])
    for step in range(ITERS):
        if step > 0:
            apart = [0, 1] + [k for k in pieces if k > 1]
            lse, late = call(
                lambda *refs: targets_kernel(n_row, *refs),
                (src_dense, f32((len(apart) - 2) * part.shape[0] - cut, width)),
                tile, lt, sqy, *parts, *[pieces[k] for k in apart[2:]], early[-1],
            )
            late = along_y(late)
        if step > 0:
            rest = bits_of(n_col)
        else:
            group, rest = [*bits_of(n_x), n_col // 2], [bit for bit in bits_of(n_col // 2) if bit >= n_x]
            ways = [0]
            for bit in group:
                ways += [way | bit for way in ways]
            near = [lse] + [swap(lse, "col", way) for way in ways[:0:-1]]
            far = [k for k in pieces if k > 0]
            lse, early, *copies = call(
                lambda *refs: merge_kernel(len(ways), *refs),
                (src_dense, f32(part.shape[0] + cut, width), *(part,) * len(far)),
                *near, *[pieces[k] for k in far], early,
            )
            early = along_y(early)
            pieces |= dict(zip(far, copies))
            for bit in bits_of(n_x)[::-1]:
                pieces |= {k ^ bit: swap(piece, "col", bit) for k, piece in pieces.items() if k ^ bit != 1}
        for distance in rest[:-1]:
            lse = merge_all([lse, swap(lse, "col", distance)])
        parts = [lse, swap(lse, "col", rest[-1])]
        if step < ITERS - 1:
            lse = call(lambda *refs: sources_kernel(2, *refs), tgt_dense, tile, ls, sqx, *parts)
        else:
            lse, sent, mine = call(
                last_sources_kernel,
                (tgt_dense, f32(half, width), f32(half, width)),
                tile, source, ls, sqx, *parts, late[-1],
                scratch=[pltpu.VMEM((n_tgt, n_src), jnp.bfloat16)],
            )
        parts = [lse] + [swap(lse, "row", k) for k in range(1, n_row)]
    total = merge_all(parts)

    bias = lt * LOG2E + (sqy - total) - sqy
    biases = [bias] + [swap(bias, "col", distance) for distance in apart[1:]]

    mine, came = call(
        share_kernel,
        (f32(half, width), f32(len(apart) - 1, n_row // 2, *part.shape)),
        mine, swap(sent, "row", 1), total, lse, parts[1], *early, *late,
    )
    rest = bits_of(n_row)[1:]
    for distance in rest[:-1]:
        mine, = call(add_kernel, (f32(half, width),), mine, swap(mine, "row", distance))
    mine_came = swap(mine, "row", rest[-1])

    n_all = len(apart) * n_tgt
    all_y, inner = call(
        lambda *refs: scores_kernel(n_x, *refs),
        (bf16(n_all, width), f32(2 * count, n_all)),
        source, target, came, swap(came, "row", 1),
        limit=32,
    )

    def image(flip):
        return call(
            lambda *refs: image_kernel(flip, *refs),
            f32(count + EXTRA, width),
            inner, all_y, *biases[::-1],
            scratch=[pltpu.VMEM((count, n_all), jnp.float32)],
        )

    came = swap(image(1), "col", n_x)
    own = image(0)
    n_last = 4
    mine = call(add_kernel, (f32(half // n_last, width),) * n_last, mine, mine_came)
    target_image = call(
        place_kernel, f32(n_tgt, width), *mine, *[swap(piece, "row", 1) for piece in mine],
        out_specs=HBM, scratch=[DMA((2 * n_last,))],
    )
    source_image = call(join_kernel, f32(count, width), own, came)
    return source_image, target_image


def solution(mesh):
    in_specs = (P("row", None), P("col", None), P("row"), P("col"))
    out_specs = (P(("row", "col"), None), P("col", None))
    return jax.shard_map(
        on_device, mesh=mesh, in_specs=in_specs, out_specs=out_specs, check_vma=False
    )
```

```python
import math

import jax
import jax.numpy as jnp
from jax import lax
from jax.experimental import pallas as pl
from jax.experimental.pallas import tpu as pltpu
from jax.sharding import PartitionSpec as P

ITERS = 2
BLUR = 0.1
LOG2E = math.log2(math.e)
LANES = 128
NT_DIMS = (((1,), (1,)), ((), ()))
VMEM = pl.BlockSpec(memory_space=pltpu.VMEM)
HBM = pl.BlockSpec(memory_space=pltpu.HBM)
ANY = pl.BlockSpec(memory_space=pl.ANY)
DMA = pltpu.SemaphoreType.DMA


def call(kernel, out_shape, *args, in_specs=None, out_specs=None, scratch=(), limit=24):
    return pl.pallas_call(
        kernel,
        out_shape=out_shape,
        in_specs=in_specs or [VMEM] * len(args),
        out_specs=out_specs or jax.tree.map(lambda _: VMEM, out_shape),
        scratch_shapes=list(scratch),
        compiler_params=pltpu.CompilerParams(vmem_limit_bytes=limit << 20),
    )(*args)


def f32(*shape):
    return jax.ShapeDtypeStruct(shape, jnp.float32)


def bf16(*shape):
    return jax.ShapeDtypeStruct(shape, jnp.bfloat16)


def scale(width):
    return LOG2E / (width * BLUR)


def to_column(dense):
    n = dense.shape[0]
    square = jnp.concatenate([dense, jnp.zeros((LANES - n, LANES), jnp.float32)], axis=0).T
    return jnp.concatenate([square[:, b : b + 1] for b in range(n)], axis=0)


def to_dense(columns):
    lane = lax.broadcasted_iota(jnp.int32, (LANES, LANES), 1)
    square = jnp.zeros((LANES, LANES), jnp.float32)
    for b, column in enumerate(columns):
        square = jnp.where(lane == b, column, square)
    return square.T[: len(columns)]


def to_row(dense):
    return jnp.concatenate([dense[b : b + 1, :] for b in range(dense.shape[0])], axis=1)


def over_targets(scores):
    peak = jnp.max(scores, axis=0, keepdims=True)
    total = jnp.sum(jnp.exp2(scores - peak), axis=0, keepdims=True)
    return peak + jnp.log2(total)


def half_at(ref, place):
    half = ref.shape[0] // 2
    return ref[pl.ds(place * half, half), :]


def merge_all(parts):
    peak = parts[0]
    for part in parts[1:]:
        peak = jnp.maximum(peak, part)
    return peak + jnp.log2(sum(jnp.exp2(part - peak) for part in parts))


def norms(block):
    wide = block.astype(jnp.float32)
    return jnp.sum(wide * wide, axis=1, keepdims=True) * scale(block.shape[1])


def quarter_kernel(y_ref, out_ref):
    rows = out_ref.shape[0]
    out_ref[...] = y_ref[pl.ds(pl.multiple_of(lax.axis_index("row") * rows, rows), rows), :].astype(jnp.float32)


def norms_kernel(x_ref, sqx_ref):
    columns = [norms(x_ref[pl.ds(b, LANES), :]) for b in range(0, x_ref.shape[0], LANES)]
    sqx_ref[...] = to_dense(columns)


def first_kernel(y_ref, x_ref, lt_ref, tile_ref, lse_ref, sqy_ref):
    wide = 256
    y = y_ref[...]
    unit = scale(y.shape[1])
    sqy = norms(y)
    sqy_ref[...] = to_dense([sqy[b : b + LANES] for b in range(0, y.shape[0], LANES)])
    bias = to_column(lt_ref[...]) * LOG2E - sqy
    for b in range(x_ref.shape[0] // wide):
        at = pl.ds(b * wide, wide)
        x = x_ref[at, :]
        tile = lax.dot_general(y, x, NT_DIMS, preferred_element_type=jnp.float32) * (2.0 * unit)
        tile_ref[:, at] = tile
        row = over_targets(tile + bias)
        for c in range(wide // LANES):
            lse_ref[pl.ds(b * (wide // LANES) + c, 1), :] = row[:, c * LANES : (c + 1) * LANES]


def early_rows(rows):
    return rows // 2


def targets_kernel(n_parts, tile_ref, lt_ref, sqy_ref, *refs):
    parts, pieces, (lse_ref, pack_ref) = refs[:n_parts], refs[n_parts:-3], refs[-2:]
    rows = pieces[0].shape[0]
    cut = early_rows(rows)
    pack_ref[: rows - cut, :] = pieces[0][cut:, :]
    for k, piece in enumerate(pieces[1:], 1):
        pack_ref[pl.ds(rows * k - cut, rows), :] = piece[...]
    g_pot = sqy_ref[...] - merge_all([ref[...] for ref in parts])
    bias = to_column(lt_ref[...] * LOG2E + g_pot - sqy_ref[...])
    for b in range(tile_ref.shape[1] // LANES):
        lse_ref[pl.ds(b, 1), :] = over_targets(tile_ref[:, pl.ds(b * LANES, LANES)] + bias)


def merge_kernel(n_parts, *refs):
    parts, refs = refs[:n_parts], refs[n_parts:]
    n_pieces = len(refs) // 2
    pieces, (out_ref, pack_ref, *copies) = refs[:n_pieces], refs[n_pieces:]
    out_ref[...] = merge_all([ref[...] for ref in parts])
    rows = pieces[-1].shape[0]
    pack_ref[:rows, :] = pieces[-1][...]
    pack_ref[rows:, :] = pieces[0][: early_rows(rows), :]
    for piece, copy in zip(pieces[:-1], copies):
        copy[...] = piece[...]


def sources_kernel(n_parts, tile_ref, ls_ref, sqx_ref, *refs):
    bias = source_bias(ls_ref, sqx_ref, refs[:n_parts])
    columns = []
    for j in range(tile_ref.shape[0] // LANES):
        peak, total, _ = over_sources(tile_ref, pl.ds(j * LANES, LANES), bias)
        columns.append(peak + jnp.log2(total))
    refs[-1][...] = to_dense(columns)


def last_sources_kernel(tile_ref, x_ref, ls_ref, sqx_ref, *refs):
    parts, (lse_ref, sent_ref, mine_ref) = refs[:-4], refs[-3:]
    bias = source_bias(ls_ref, sqx_ref, parts)
    x = x_ref[...]
    n_rows = mine_ref.shape[0] // LANES
    core = lax.axis_index("row") % 2
    for out_ref, place in ((sent_ref, 1 - core), (mine_ref, core)):
        columns = []
        for j in range(n_rows):
            at = pl.ds(pl.multiple_of((place * n_rows + j) * LANES, LANES), LANES)
            peak, total, exps = over_sources(tile_ref, at, bias)
            columns.append(peak + jnp.log2(total))
            weights = jnp.concatenate([block.astype(jnp.bfloat16) for block in exps], axis=1)
            mean = jnp.dot(weights, x, preferred_element_type=jnp.float32)
            out_ref[pl.ds(j * LANES, LANES), :] = mean * (1.0 / total)
        lse_ref[pl.ds(place * n_rows, n_rows), :] = to_dense(columns)


def source_bias(ls_ref, sqx_ref, parts):
    f_pot = sqx_ref[...] - merge_all([ref[...] for ref in parts])
    return ls_ref[...] * LOG2E + f_pot - sqx_ref[...]


def over_sources(tile_ref, at, bias):
    scores = [tile_ref[at, pl.ds(b * LANES, LANES)] + bias[b : b + 1, :] for b in range(bias.shape[0])]
    top = scores[0]
    for block in scores[1:]:
        top = jnp.maximum(top, block)
    peak = jnp.max(top, axis=1, keepdims=True)
    exps = [jnp.exp2(block - peak) for block in scores]
    return peak, jnp.sum(sum(exps), axis=1, keepdims=True), exps


def share_kernel(mine_ref, came_ref, total_ref, lse_ref, came_lse_ref, *refs):
    pieces, (out_ref, pack_ref) = refs[:-2], refs[-2:]
    half = mine_ref.shape[0] // LANES
    at = pl.ds(lax.axis_index("row") % 2 * half, half)
    total = total_ref[at, :]
    share, came_share = to_column(jnp.exp2(lse_ref[at, :] - total)), to_column(jnp.exp2(came_lse_ref[at, :] - total))
    out_ref[...] = mine_ref[...] * share + came_ref[...] * came_share
    n_shards, n_y, rows, _ = pack_ref.shape
    y = lax.axis_index("row") // 2
    early, late = pieces[:n_y], pieces[n_y:]
    cut = early_rows(rows)
    for j in range(n_y):
        place = y ^ j
        pack_ref[0, place] = early[j][:rows, :]
        pack_ref[1, place, :cut, :] = early[j][rows:, :]
        pack_ref[1, place, cut:, :] = late[j][: rows - cut, :]
        for k in range(2, n_shards):
            pack_ref[k, place] = late[j][pl.ds((k - 1) * rows - cut, rows), :]


def add_kernel(one_ref, two_ref, *out_refs):
    rows = out_refs[0].shape[0]
    for k, ref in enumerate(out_refs):
        at = pl.ds(k * rows, rows)
        ref[...] = one_ref[at, :] + two_ref[at, :]


def join_kernel(*refs):
    parts, out_ref = refs[:-1], refs[-1]
    rows = out_ref.shape[0]
    lses = [ref[rows : rows + pl.cdiv(rows, LANES), :LANES] for ref in parts]
    whole = merge_all(lses)
    shares = [to_column(jnp.exp2(lse - whole))[:rows] for lse in lses]
    out_ref[...] = sum(ref[:rows, :] * share for ref, share in zip(parts, shares))


def place_kernel(*refs):
    n = (len(refs) - 2) // 2
    mine, others, out_hbm, sems = refs[:n], refs[n : 2 * n], refs[-2], refs[-1]
    rows = mine[0].shape[0]
    core = lax.axis_index("row") % 2
    copies = []
    for place, pieces in ((core, mine), (1 - core, others)):
        for k, piece in enumerate(pieces):
            at = pl.ds(pl.multiple_of((place * n + k) * rows, rows), rows)
            copies.append(pltpu.make_async_copy(piece, out_hbm.at[at, :], sems.at[len(copies)]))
            copies[-1].start()
    for copy in copies:
        copy.wait()


def scores_kernel(near, x_ref, own_ref, mine_ref, other_ref, y_ref, inner_ref):
    rows = inner_ref.shape[0] // 2
    n_tgt = own_ref.shape[0]
    n_came, n_y, part, _ = mine_ref.shape
    col, core = lax.axis_index("col"), lax.axis_index("row") % 2
    y_ref[:n_tgt, :] = own_ref[...]
    for k in range(n_came):
        for ref, place in ((mine_ref, core), (other_ref, 1 - core)):
            for y in range(n_y):
                start = (k + 1) * n_tgt + (2 * y + place) * part
                y_ref[pl.ds(pl.multiple_of(start, part), part), :] = ref[k, y].astype(jnp.bfloat16)
    blocks = [x_ref[pl.ds(pl.multiple_of((col ^ flip) * rows, rows), rows), :] for flip in (0, near)]
    x = jnp.concatenate(blocks, axis=0)
    unit = scale(x.shape[1])
    for b in range(y_ref.shape[0] // n_tgt):
        at = pl.ds(b * n_tgt, n_tgt)
        inner_ref[:, at] = lax.dot_general(x, y_ref[at, :], NT_DIMS, preferred_element_type=jnp.float32) * (2.0 * unit)


EXTRA = 8


def images(flip, inner_ref, y_ref, bias_refs, scores_ref):
    rows = scores_ref.shape[0]
    n_shards = len(bias_refs)
    n_tgt = y_ref.shape[0] // n_shards
    block = pl.ds(flip * rows, rows)
    peak = jnp.full((rows, 1), -jnp.inf, jnp.float32)
    for k, bias_ref in enumerate(bias_refs[::-1]):
        at = pl.ds(k * n_tgt, n_tgt)
        scores = inner_ref[block, at] + to_row(bias_ref[...])
        scores_ref[:, at] = scores
        peak = jnp.maximum(peak, jnp.max(scores, axis=1, keepdims=True))
    total = jnp.zeros((rows, 1), jnp.float32)
    numer = jnp.zeros((rows, y_ref.shape[1]), jnp.float32)
    for k in range(n_shards):
        at = pl.ds(k * n_tgt, n_tgt)
        plan = jnp.exp2(scores_ref[:, at] - peak)
        total = total + jnp.sum(plan, axis=1, keepdims=True)
        numer = numer + jnp.dot(plan.astype(jnp.bfloat16), y_ref[at, :], preferred_element_type=jnp.float32)
    return numer, total, peak


def lanes_of(column):
    rows = column.shape[0]
    if rows % LANES:
        column = jnp.concatenate([column, jnp.zeros((-rows % LANES, 1), jnp.float32)], axis=0)
    return to_dense([column[b : b + LANES] for b in range(0, column.shape[0], LANES)])


EXTRA = 8


def image_kernel(flip, inner_ref, y_ref, *refs):
    bias_refs, (image_ref, scores_ref) = refs[:-2], refs[-2:]
    numer, total, peak = images(flip, inner_ref, y_ref, bias_refs, scores_ref)
    rows = numer.shape[0]
    lse = lanes_of(peak + jnp.log2(total))
    image_ref[:rows, :] = numer * (1.0 / total)
    image_ref[rows:, :] = jnp.zeros((EXTRA, image_ref.shape[1]), jnp.float32)
    image_ref[rows : rows + lse.shape[0], :LANES] = lse


def swap(value, axis, distance):
    n = lax.axis_size(axis)
    return lax.ppermute(value, axis, [(i, i ^ distance) for i in range(n)])


def bits_of(n):
    return [1 << b for b in range(n.bit_length() - 1)]


def on_device(source, target, log_source_mass, log_target_mass):
    n_src, width = source.shape
    n_tgt = target.shape[0]
    n_col, n_row = lax.axis_size("col"), lax.axis_size("row")
    count = n_src // n_col
    n_x = 1 << (len(bits_of(n_col)) // 2)
    n_z = n_col // n_x
    y_bits = bits_of(n_row)[1:]
    ls = log_source_mass.reshape(-1, LANES)
    lt = log_target_mass.reshape(-1, LANES)
    src_dense, tgt_dense = f32(*ls.shape), f32(*lt.shape)
    half = n_tgt // 2

    part = f32(n_tgt // n_row, width)
    pieces = {0: call(quarter_kernel, part, target)}
    for distance in [bit for bit in bits_of(n_col) if bit > n_x][::-1]:
        pieces |= {k ^ distance: swap(piece, "col", distance) for k, piece in pieces.items()}
    early = swap(pieces[0], "col", 1)

    def along_y(piece):
        held = [piece]
        for distance in y_bits:
            held += [swap(one, "row", distance) for one in held]
        return held

    tile, lse, sqy = call(first_kernel, (f32(n_tgt, n_src), src_dense, tgt_dense), target, source, lt)
    sqx = call(norms_kernel, src_dense, source)
    cut = early_rows(part.shape[0])
    for step in range(ITERS):
        if step > 0:
            apart = [0, 1] + [k for k in pieces if k > 1]
            lse, late = call(
                lambda *refs: targets_kernel(n_row, *refs),
                (src_dense, f32((len(apart) - 2) * part.shape[0] - cut, width)),
                tile, lt, sqy, *parts, *[pieces[k] for k in apart[2:]], early[-1],
            )
            late = along_y(late)
        if step > 0:
            rest = [*bits_of(n_x), *[bit for bit in bits_of(n_col) if bit > n_x], n_x]
        else:
            group, rest = [*bits_of(n_x), n_col // 2], [bit for bit in bits_of(n_col // 2) if bit >= n_x]
            ways = [0]
            for bit in group:
                ways += [way | bit for way in ways]
            near = [lse] + [swap(lse, "col", way) for way in ways[:0:-1]]
            far = [k for k in pieces if k > 0]
            lse, early, *copies = call(
                lambda *refs: merge_kernel(len(ways), *refs),
                (src_dense, f32(part.shape[0] + cut, width), *(part,) * len(far)),
                *near, *[pieces[k] for k in far], early,
            )
            early = along_y(early)
            pieces |= dict(zip(far, copies))
            for bit in bits_of(n_x)[::-1]:
                pieces |= {k ^ bit: swap(piece, "col", bit) for k, piece in pieces.items() if k ^ bit != 1}
        for distance in rest[:-1]:
            lse = merge_all([lse, swap(lse, "col", distance)])
        parts = [lse, swap(lse, "col", rest[-1])]
        if step < ITERS - 1:
            lse = call(lambda *refs: sources_kernel(2, *refs), tgt_dense, tile, ls, sqx, *parts)
        else:
            lse, sent, mine = call(
                last_sources_kernel,
                (tgt_dense, f32(half, width), f32(half, width)),
                tile, source, ls, sqx, *parts, late[-1],
            )
        parts = [lse] + [swap(lse, "row", k) for k in range(1, n_row)]
    total = merge_all(parts)

    bias = lt * LOG2E + (sqy - total) - sqy
    biases = [bias] + [swap(bias, "col", distance) for distance in apart[1:]]

    mine, came = call(
        share_kernel,
        (f32(half, width), f32(len(apart) - 1, n_row // 2, *part.shape)),
        mine, swap(sent, "row", 1), total, lse, parts[1], *early, *late,
    )
    rest = bits_of(n_row)[1:]
    for distance in rest[:-1]:
        mine, = call(add_kernel, (f32(half, width),), mine, swap(mine, "row", distance))
    mine_came = swap(mine, "row", rest[-1])

    n_all = len(apart) * n_tgt
    all_y, inner = call(
        lambda *refs: scores_kernel(n_x, *refs),
        (bf16(n_all, width), f32(2 * count, n_all)),
        source, target, came, swap(came, "row", 1),
        limit=32,
    )

    def image(flip):
        return call(
            lambda *refs: image_kernel(flip, *refs),
            f32(count + EXTRA, width),
            inner, all_y, *biases[::-1],
            scratch=[pltpu.VMEM((count, n_all), jnp.float32)],
        )

    came = swap(image(1), "col", n_x)
    own = image(0)
    n_last = 4
    mine = call(add_kernel, (f32(half // n_last, width),) * n_last, mine, mine_came)
    target_image = call(
        place_kernel, f32(n_tgt, width), *mine, *[swap(piece, "row", 1) for piece in mine],
        out_specs=HBM, scratch=[DMA((2 * n_last,))],
    )
    source_image = call(join_kernel, f32(count, width), own, came)
    return source_image, target_image


def solution(mesh):
    in_specs = (P("row", None), P("col", None), P("row"), P("col"))
    out_specs = (P(("row", "col"), None), P("col", None))
    return jax.shard_map(
        on_device, mesh=mesh, in_specs=in_specs, out_specs=out_specs, check_vma=False
    )
```

```python
import math

import jax
import jax.numpy as jnp
from jax import lax
from jax.experimental import pallas as pl
from jax.experimental.pallas import tpu as pltpu
from jax.sharding import PartitionSpec as P

ITERS = 2
BLUR = 0.1
LOG2E = math.log2(math.e)
LANES = 128
NT_DIMS = (((1,), (1,)), ((), ()))
VMEM = pl.BlockSpec(memory_space=pltpu.VMEM)
HBM = pl.BlockSpec(memory_space=pltpu.HBM)
ANY = pl.BlockSpec(memory_space=pl.ANY)
DMA = pltpu.SemaphoreType.DMA


def call(kernel, out_shape, *args, in_specs=None, out_specs=None, scratch=(), limit=24):
    return pl.pallas_call(
        kernel,
        out_shape=out_shape,
        in_specs=in_specs or [VMEM] * len(args),
        out_specs=out_specs or jax.tree.map(lambda _: VMEM, out_shape),
        scratch_shapes=list(scratch),
        compiler_params=pltpu.CompilerParams(vmem_limit_bytes=limit << 20),
    )(*args)


def f32(*shape):
    return jax.ShapeDtypeStruct(shape, jnp.float32)


def bf16(*shape):
    return jax.ShapeDtypeStruct(shape, jnp.bfloat16)


def scale(width):
    return LOG2E / (width * BLUR)


def to_column(dense):
    n = dense.shape[0]
    square = jnp.concatenate([dense, jnp.zeros((LANES - n, LANES), jnp.float32)], axis=0).T
    return jnp.concatenate([square[:, b : b + 1] for b in range(n)], axis=0)


def to_dense(columns):
    lane = lax.broadcasted_iota(jnp.int32, (LANES, LANES), 1)
    square = jnp.zeros((LANES, LANES), jnp.float32)
    for b, column in enumerate(columns):
        square = jnp.where(lane == b, column, square)
    return square.T[: len(columns)]


def to_row(dense):
    return jnp.concatenate([dense[b : b + 1, :] for b in range(dense.shape[0])], axis=1)


def over_targets(scores):
    peak = jnp.max(scores, axis=0, keepdims=True)
    total = jnp.sum(jnp.exp2(scores - peak), axis=0, keepdims=True)
    return peak + jnp.log2(total)


def half_at(ref, place):
    half = ref.shape[0] // 2
    return ref[pl.ds(place * half, half), :]


def merge_all(parts):
    peak = parts[0]
    for part in parts[1:]:
        peak = jnp.maximum(peak, part)
    return peak + jnp.log2(sum(jnp.exp2(part - peak) for part in parts))


def norms(block):
    wide = block.astype(jnp.float32)
    return jnp.sum(wide * wide, axis=1, keepdims=True) * scale(block.shape[1])


def quarter_kernel(y_ref, out_ref):
    rows = out_ref.shape[0]
    out_ref[...] = y_ref[pl.ds(pl.multiple_of(lax.axis_index("row") * rows, rows), rows), :].astype(jnp.float32)


def norms_kernel(x_ref, sqx_ref):
    columns = [norms(x_ref[pl.ds(b, LANES), :]) for b in range(0, x_ref.shape[0], LANES)]
    sqx_ref[...] = to_dense(columns)


def first_kernel(y_ref, x_ref, lt_ref, tile_ref, lse_ref, sqy_ref):
    wide = 256
    y = y_ref[...]
    unit = scale(y.shape[1])
    sqy = norms(y)
    sqy_ref[...] = to_dense([sqy[b : b + LANES] for b in range(0, y.shape[0], LANES)])
    bias = to_column(lt_ref[...]) * LOG2E - sqy
    for b in range(x_ref.shape[0] // wide):
        at = pl.ds(b * wide, wide)
        x = x_ref[at, :]
        tile = lax.dot_general(y, x, NT_DIMS, preferred_element_type=jnp.float32) * (2.0 * unit)
        tile_ref[:, at] = tile
        row = over_targets(tile + bias)
        for c in range(wide // LANES):
            lse_ref[pl.ds(b * (wide // LANES) + c, 1), :] = row[:, c * LANES : (c + 1) * LANES]


def early_rows(rows):
    return rows // 2


def targets_kernel(n_parts, tile_ref, lt_ref, sqy_ref, *refs):
    parts, pieces, (lse_ref, pack_ref) = refs[:n_parts], refs[n_parts:-3], refs[-2:]
    rows = pieces[0].shape[0]
    cut = early_rows(rows)
    pack_ref[: rows - cut, :] = pieces[0][cut:, :]
    for k, piece in enumerate(pieces[1:], 1):
        pack_ref[pl.ds(rows * k - cut, rows), :] = piece[...]
    g_pot = sqy_ref[...] - merge_all([ref[...] for ref in parts])
    bias = to_column(lt_ref[...] * LOG2E + g_pot - sqy_ref[...])
    for b in range(tile_ref.shape[1] // LANES):
        lse_ref[pl.ds(b, 1), :] = over_targets(tile_ref[:, pl.ds(b * LANES, LANES)] + bias)


def merge_kernel(n_parts, *refs):
    parts, refs = refs[:n_parts], refs[n_parts:]
    n_pieces = len(refs) // 2
    pieces, (out_ref, pack_ref, *copies) = refs[:n_pieces], refs[n_pieces:]
    out_ref[...] = merge_all([ref[...] for ref in parts])
    rows = pieces[-1].shape[0]
    pack_ref[:rows, :] = pieces[-1][...]
    pack_ref[rows:, :] = pieces[0][: early_rows(rows), :]
    for piece, copy in zip(pieces[:-1], copies):
        copy[...] = piece[...]


def sources_kernel(n_parts, tile_ref, ls_ref, sqx_ref, *refs):
    bias = source_bias(ls_ref, sqx_ref, refs[:n_parts])
    columns = []
    for j in range(tile_ref.shape[0] // LANES):
        peak, total, _ = over_sources(tile_ref, pl.ds(j * LANES, LANES), bias)
        columns.append(peak + jnp.log2(total))
    refs[-1][...] = to_dense(columns)


def last_sources_kernel(n_parts, tile_ref, x_ref, ls_ref, sqx_ref, *refs):
    pieces, (lse_ref, sent_ref, mine_ref, pack_ref) = refs[n_parts:-4], refs[-4:]
    n_shards, n_y, rows, _ = pack_ref.shape
    y = lax.axis_index("row") // 2
    early, late = pieces[:n_y], pieces[n_y:]
    cut = early_rows(rows)
    for j in range(n_y):
        place = y ^ j
        pack_ref[0, place] = early[j][:rows, :]
        pack_ref[1, place, :cut, :] = early[j][rows:, :]
        pack_ref[1, place, cut:, :] = late[j][: rows - cut, :]
        for k in range(2, n_shards):
            pack_ref[k, place] = late[j][pl.ds((k - 1) * rows - cut, rows), :]
    bias = source_bias(ls_ref, sqx_ref, refs[:n_parts])
    x = x_ref[...]
    n_rows = mine_ref.shape[0] // LANES
    core = lax.axis_index("row") % 2
    for out_ref, place in ((sent_ref, 1 - core), (mine_ref, core)):
        columns = []
        for j in range(n_rows):
            at = pl.ds(pl.multiple_of((place * n_rows + j) * LANES, LANES), LANES)
            peak, total, exps = over_sources(tile_ref, at, bias)
            columns.append(peak + jnp.log2(total))
            weights = jnp.concatenate([block.astype(jnp.bfloat16) for block in exps], axis=1)
            mean = jnp.dot(weights, x, preferred_element_type=jnp.float32)
            out_ref[pl.ds(j * LANES, LANES), :] = mean * (1.0 / total)
        lse_ref[pl.ds(place * n_rows, n_rows), :] = to_dense(columns)


def source_bias(ls_ref, sqx_ref, parts):
    f_pot = sqx_ref[...] - merge_all([ref[...] for ref in parts])
    return ls_ref[...] * LOG2E + f_pot - sqx_ref[...]


def over_sources(tile_ref, at, bias):
    scores = [tile_ref[at, pl.ds(b * LANES, LANES)] + bias[b : b + 1, :] for b in range(bias.shape[0])]
    top = scores[0]
    for block in scores[1:]:
        top = jnp.maximum(top, block)
    peak = jnp.max(top, axis=1, keepdims=True)
    exps = [jnp.exp2(block - peak) for block in scores]
    return peak, jnp.sum(sum(exps), axis=1, keepdims=True), exps


def share_kernel(mine_ref, came_ref, total_ref, lse_ref, came_lse_ref, out_ref):
    half = mine_ref.shape[0] // LANES
    at = pl.ds(lax.axis_index("row") % 2 * half, half)
    total = total_ref[at, :]
    share, came_share = to_column(jnp.exp2(lse_ref[at, :] - total)), to_column(jnp.exp2(came_lse_ref[at, :] - total))
    out_ref[...] = mine_ref[...] * share + came_ref[...] * came_share


def add_kernel(one_ref, two_ref, *out_refs):
    rows = out_refs[0].shape[0]
    for k, ref in enumerate(out_refs):
        at = pl.ds(k * rows, rows)
        ref[...] = one_ref[at, :] + two_ref[at, :]


def join_kernel(*refs):
    parts, out_ref = refs[:-1], refs[-1]
    rows = out_ref.shape[0]
    lses = [ref[rows : rows + pl.cdiv(rows, LANES), :LANES] for ref in parts]
    whole = merge_all(lses)
    shares = [to_column(jnp.exp2(lse - whole))[:rows] for lse in lses]
    out_ref[...] = sum(ref[:rows, :] * share for ref, share in zip(parts, shares))


def place_kernel(*refs):
    n = (len(refs) - 2) // 2
    mine, others, out_hbm, sems = refs[:n], refs[n : 2 * n], refs[-2], refs[-1]
    rows = mine[0].shape[0]
    core = lax.axis_index("row") % 2
    copies = []
    for place, pieces in ((core, mine), (1 - core, others)):
        for k, piece in enumerate(pieces):
            at = pl.ds(pl.multiple_of((place * n + k) * rows, rows), rows)
            copies.append(pltpu.make_async_copy(piece, out_hbm.at[at, :], sems.at[len(copies)]))
            copies[-1].start()
    for copy in copies:
        copy.wait()


def scores_kernel(near, x_ref, own_ref, mine_ref, other_ref, y_ref, inner_ref):
    rows = inner_ref.shape[0] // 2
    n_tgt = own_ref.shape[0]
    n_came, n_y, part, _ = mine_ref.shape
    col, core = lax.axis_index("col"), lax.axis_index("row") % 2
    y_ref[:n_tgt, :] = own_ref[...]
    for k in range(n_came):
        for ref, place in ((mine_ref, core), (other_ref, 1 - core)):
            for y in range(n_y):
                start = (k + 1) * n_tgt + (2 * y + place) * part
                y_ref[pl.ds(pl.multiple_of(start, part), part), :] = ref[k, y].astype(jnp.bfloat16)
    blocks = [x_ref[pl.ds(pl.multiple_of((col ^ flip) * rows, rows), rows), :] for flip in (0, near)]
    x = jnp.concatenate(blocks, axis=0)
    unit = scale(x.shape[1])
    for b in range(y_ref.shape[0] // n_tgt):
        at = pl.ds(b * n_tgt, n_tgt)
        inner_ref[:, at] = lax.dot_general(x, y_ref[at, :], NT_DIMS, preferred_element_type=jnp.float32) * (2.0 * unit)


EXTRA = 8


def images(flip, inner_ref, y_ref, bias_refs, scores_ref):
    rows = scores_ref.shape[0]
    n_shards = len(bias_refs)
    n_tgt = y_ref.shape[0] // n_shards
    block = pl.ds(flip * rows, rows)
    peak = jnp.full((rows, 1), -jnp.inf, jnp.float32)
    for k, bias_ref in enumerate(bias_refs[::-1]):
        at = pl.ds(k * n_tgt, n_tgt)
        scores = inner_ref[block, at] + to_row(bias_ref[...])
        scores_ref[:, at] = scores
        peak = jnp.maximum(peak, jnp.max(scores, axis=1, keepdims=True))
    total = jnp.zeros((rows, 1), jnp.float32)
    numer = jnp.zeros((rows, y_ref.shape[1]), jnp.float32)
    for k in range(n_shards):
        at = pl.ds(k * n_tgt, n_tgt)
        plan = jnp.exp2(scores_ref[:, at] - peak)
        total = total + jnp.sum(plan, axis=1, keepdims=True)
        numer = numer + jnp.dot(plan.astype(jnp.bfloat16), y_ref[at, :], preferred_element_type=jnp.float32)
    return numer, total, peak


def lanes_of(column):
    rows = column.shape[0]
    if rows % LANES:
        column = jnp.concatenate([column, jnp.zeros((-rows % LANES, 1), jnp.float32)], axis=0)
    return to_dense([column[b : b + LANES] for b in range(0, column.shape[0], LANES)])


EXTRA = 8


def image_kernel(flip, inner_ref, y_ref, *refs):
    bias_refs, (image_ref, scores_ref) = refs[:-2], refs[-2:]
    numer, total, peak = images(flip, inner_ref, y_ref, bias_refs, scores_ref)
    rows = numer.shape[0]
    lse = lanes_of(peak + jnp.log2(total))
    image_ref[:rows, :] = numer * (1.0 / total)
    image_ref[rows:, :] = jnp.zeros((EXTRA, image_ref.shape[1]), jnp.float32)
    image_ref[rows : rows + lse.shape[0], :LANES] = lse


def swap(value, axis, distance):
    n = lax.axis_size(axis)
    return lax.ppermute(value, axis, [(i, i ^ distance) for i in range(n)])


def bits_of(n):
    return [1 << b for b in range(n.bit_length() - 1)]


def on_device(source, target, log_source_mass, log_target_mass):
    n_src, width = source.shape
    n_tgt = target.shape[0]
    n_col, n_row = lax.axis_size("col"), lax.axis_size("row")
    count = n_src // n_col
    n_x = 1 << (len(bits_of(n_col)) // 2)
    n_z = n_col // n_x
    y_bits = bits_of(n_row)[1:]
    ls = log_source_mass.reshape(-1, LANES)
    lt = log_target_mass.reshape(-1, LANES)
    src_dense, tgt_dense = f32(*ls.shape), f32(*lt.shape)
    half = n_tgt // 2

    part = f32(n_tgt // n_row, width)
    pieces = {0: call(quarter_kernel, part, target)}
    for distance in [bit for bit in bits_of(n_col) if bit > n_x][::-1]:
        pieces |= {k ^ distance: swap(piece, "col", distance) for k, piece in pieces.items()}
    early = swap(pieces[0], "col", 1)

    def along_y(piece):
        held = [piece]
        for distance in y_bits:
            held += [swap(one, "row", distance) for one in held]
        return held

    tile, lse, sqy = call(first_kernel, (f32(n_tgt, n_src), src_dense, tgt_dense), target, source, lt)
    sqx = call(norms_kernel, src_dense, source)
    cut = early_rows(part.shape[0])
    for step in range(ITERS):
        if step > 0:
            apart = [0, 1] + [k for k in pieces if k > 1]
            lse, late = call(
                lambda *refs: targets_kernel(n_row, *refs),
                (src_dense, f32((len(apart) - 2) * part.shape[0] - cut, width)),
                tile, lt, sqy, *parts, *[pieces[k] for k in apart[2:]], early[-1],
            )
            late = along_y(late)
        if step > 0:
            rest = bits_of(n_col)
        else:
            group, rest = [*bits_of(n_x), n_col // 2], [bit for bit in bits_of(n_col // 2) if bit >= n_x]
            ways = [0]
            for bit in group:
                ways += [way | bit for way in ways]
            near = [lse] + [swap(lse, "col", way) for way in ways[:0:-1]]
            far = [k for k in pieces if k > 0]
            lse, early, *copies = call(
                lambda *refs: merge_kernel(len(ways), *refs),
                (src_dense, f32(part.shape[0] + cut, width), *(part,) * len(far)),
                *near, *[pieces[k] for k in far], early,
            )
            early = along_y(early)
            pieces |= dict(zip(far, copies))
            for bit in bits_of(n_x)[::-1]:
                pieces |= {k ^ bit: swap(piece, "col", bit) for k, piece in pieces.items() if k ^ bit != 1}
        for distance in rest[:-1]:
            lse = merge_all([lse, swap(lse, "col", distance)])
        parts = [lse, swap(lse, "col", rest[-1])]
        if step < ITERS - 1:
            lse = call(lambda *refs: sources_kernel(2, *refs), tgt_dense, tile, ls, sqx, *parts)
        else:
            lse, sent, mine, came = call(
                lambda *refs: last_sources_kernel(2, *refs),
                (tgt_dense, f32(half, width), f32(half, width), f32(len(apart) - 1, n_row // 2, *part.shape)),
                tile, source, ls, sqx, *parts, *early, *late,
            )
        parts = [lse] + [swap(lse, "row", k) for k in range(1, n_row)]
    total = merge_all(parts)

    bias = lt * LOG2E + (sqy - total) - sqy
    biases = [bias] + [swap(bias, "col", distance) for distance in apart[1:]]

    mine = call(share_kernel, f32(half, width), mine, swap(sent, "row", 1), total, lse, parts[1])
    rest = bits_of(n_row)[1:]
    for distance in rest[:-1]:
        mine, = call(add_kernel, (f32(half, width),), mine, swap(mine, "row", distance))
    mine_came = swap(mine, "row", rest[-1])

    n_all = len(apart) * n_tgt
    all_y, inner = call(
        lambda *refs: scores_kernel(n_x, *refs),
        (bf16(n_all, width), f32(2 * count, n_all)),
        source, target, came, swap(came, "row", 1),
        limit=32,
    )

    def image(flip):
        return call(
            lambda *refs: image_kernel(flip, *refs),
            f32(count + EXTRA, width),
            inner, all_y, *biases[::-1],
            scratch=[pltpu.VMEM((count, n_all), jnp.float32)],
        )

    came = swap(image(1), "col", n_x)
    own = image(0)
    n_last = 4
    mine = call(add_kernel, (f32(half // n_last, width),) * n_last, mine, mine_came)
    target_image = call(
        place_kernel, f32(n_tgt, width), *mine, *[swap(piece, "row", 1) for piece in mine],
        out_specs=HBM, scratch=[DMA((2 * n_last,))],
    )
    source_image = call(join_kernel, f32(count, width), own, came)
    return source_image, target_image


def solution(mesh):
    in_specs = (P("row", None), P("col", None), P("row"), P("col"))
    out_specs = (P(("row", "col"), None), P("col", None))
    return jax.shard_map(
        on_device, mesh=mesh, in_specs=in_specs, out_specs=out_specs, check_vma=False
    )
```

```python
import math

import jax
import jax.numpy as jnp
from jax import lax
from jax.experimental import pallas as pl
from jax.experimental.pallas import tpu as pltpu
from jax.sharding import PartitionSpec as P

ITERS = 2
BLUR = 0.1
LOG2E = math.log2(math.e)
LANES = 128
NT_DIMS = (((1,), (1,)), ((), ()))
VMEM = pl.BlockSpec(memory_space=pltpu.VMEM)
HBM = pl.BlockSpec(memory_space=pltpu.HBM)
ANY = pl.BlockSpec(memory_space=pl.ANY)
DMA = pltpu.SemaphoreType.DMA


def call(kernel, out_shape, *args, in_specs=None, out_specs=None, scratch=(), limit=24):
    return pl.pallas_call(
        kernel,
        out_shape=out_shape,
        in_specs=in_specs or [VMEM] * len(args),
        out_specs=out_specs or jax.tree.map(lambda _: VMEM, out_shape),
        scratch_shapes=list(scratch),
        compiler_params=pltpu.CompilerParams(vmem_limit_bytes=limit << 20),
    )(*args)


def f32(*shape):
    return jax.ShapeDtypeStruct(shape, jnp.float32)


def bf16(*shape):
    return jax.ShapeDtypeStruct(shape, jnp.bfloat16)


def scale(width):
    return LOG2E / (width * BLUR)


def to_column(dense):
    n = dense.shape[0]
    square = jnp.concatenate([dense, jnp.zeros((LANES - n, LANES), jnp.float32)], axis=0).T
    return jnp.concatenate([square[:, b : b + 1] for b in range(n)], axis=0)


def to_dense(columns):
    lane = lax.broadcasted_iota(jnp.int32, (LANES, LANES), 1)
    square = jnp.zeros((LANES, LANES), jnp.float32)
    for b, column in enumerate(columns):
        square = jnp.where(lane == b, column, square)
    return square.T[: len(columns)]


def to_row(dense):
    return jnp.concatenate([dense[b : b + 1, :] for b in range(dense.shape[0])], axis=1)


def over_targets(scores):
    peak = jnp.max(scores, axis=0, keepdims=True)
    total = jnp.sum(jnp.exp2(scores - peak), axis=0, keepdims=True)
    return peak + jnp.log2(total)


def half_at(ref, place):
    half = ref.shape[0] // 2
    return ref[pl.ds(place * half, half), :]


def merge_all(parts):
    peak = parts[0]
    for part in parts[1:]:
        peak = jnp.maximum(peak, part)
    return peak + jnp.log2(sum(jnp.exp2(part - peak) for part in parts))


def norms(block):
    wide = block.astype(jnp.float32)
    return jnp.sum(wide * wide, axis=1, keepdims=True) * scale(block.shape[1])


def quarter_kernel(y_ref, out_ref):
    rows = out_ref.shape[0]
    out_ref[...] = y_ref[pl.ds(pl.multiple_of(lax.axis_index("row") * rows, rows), rows), :].astype(jnp.float32)


def norms_kernel(x_ref, sqx_ref):
    columns = [norms(x_ref[pl.ds(b, LANES), :]) for b in range(0, x_ref.shape[0], LANES)]
    sqx_ref[...] = to_dense(columns)


def first_kernel(y_ref, x_ref, lt_ref, tile_ref, lse_ref, sqy_ref):
    wide = 256
    y = y_ref[...]
    unit = scale(y.shape[1])
    sqy = norms(y)
    sqy_ref[...] = to_dense([sqy[b : b + LANES] for b in range(0, y.shape[0], LANES)])
    bias = to_column(lt_ref[...]) * LOG2E - sqy
    for b in range(x_ref.shape[0] // wide):
        at = pl.ds(b * wide, wide)
        x = x_ref[at, :]
        tile = lax.dot_general(y, x, NT_DIMS, preferred_element_type=jnp.float32) * (2.0 * unit)
        tile_ref[:, at] = tile
        row = over_targets(tile + bias)
        for c in range(wide // LANES):
            lse_ref[pl.ds(b * (wide // LANES) + c, 1), :] = row[:, c * LANES : (c + 1) * LANES]


def early_rows(rows):
    return rows // 2


def targets_kernel(n_parts, tile_ref, lt_ref, sqy_ref, *refs):
    parts, pieces, (lse_ref, pack_ref) = refs[:n_parts], refs[n_parts:-3], refs[-2:]
    rows = pieces[0].shape[0]
    cut = early_rows(rows)
    pack_ref[: rows - cut, :] = pieces[0][cut:, :]
    for k, piece in enumerate(pieces[1:], 1):
        pack_ref[pl.ds(rows * k - cut, rows), :] = piece[...]
    g_pot = sqy_ref[...] - merge_all([ref[...] for ref in parts])
    bias = to_column(lt_ref[...] * LOG2E + g_pot - sqy_ref[...])
    for b in range(tile_ref.shape[1] // LANES):
        lse_ref[pl.ds(b, 1), :] = over_targets(tile_ref[:, pl.ds(b * LANES, LANES)] + bias)


def merge_kernel(n_parts, *refs):
    parts, refs = refs[:n_parts], refs[n_parts:]
    n_pieces = len(refs) // 2
    pieces, (out_ref, pack_ref, *copies) = refs[:n_pieces], refs[n_pieces:]
    out_ref[...] = merge_all([ref[...] for ref in parts])
    rows = pieces[-1].shape[0]
    pack_ref[:rows, :] = pieces[-1][...]
    pack_ref[rows:, :] = pieces[0][: early_rows(rows), :]
    for piece, copy in zip(pieces[:-1], copies):
        copy[...] = piece[...]


def sources_kernel(n_parts, tile_ref, ls_ref, sqx_ref, *refs):
    bias = source_bias(ls_ref, sqx_ref, refs[:n_parts])
    columns = []
    for j in range(tile_ref.shape[0] // LANES):
        peak, total, _ = over_sources(tile_ref, pl.ds(j * LANES, LANES), bias)
        columns.append(peak + jnp.log2(total))
    refs[-1][...] = to_dense(columns)


def last_sources_kernel(n_parts, tile_ref, x_ref, ls_ref, sqx_ref, *refs):
    pieces, (lse_ref, sent_ref, mine_ref, pack_ref) = refs[n_parts:-4], refs[-4:]
    n_shards, n_y, rows, _ = pack_ref.shape
    y = lax.axis_index("row") // 2
    early, late = pieces[:n_y], pieces[n_y:]
    cut = early_rows(rows)
    for j in range(n_y):
        place = y ^ j
        pack_ref[0, place] = early[j][:rows, :]
        pack_ref[1, place, :cut, :] = early[j][rows:, :]
        pack_ref[1, place, cut:, :] = late[j][: rows - cut, :]
        for k in range(2, n_shards):
            pack_ref[k, place] = late[j][pl.ds((k - 1) * rows - cut, rows), :]
    bias = source_bias(ls_ref, sqx_ref, refs[:n_parts])
    x = x_ref[...]
    n_rows = mine_ref.shape[0] // LANES
    core = lax.axis_index("row") % 2
    for out_ref, place in ((sent_ref, 1 - core), (mine_ref, core)):
        columns, totals, weights = [], [], []
        for j in range(n_rows):
            at = pl.ds(pl.multiple_of((place * n_rows + j) * LANES, LANES), LANES)
            peak, total, exps = over_sources(tile_ref, at, bias)
            columns.append(peak + jnp.log2(total))
            totals.append(total)
            weights.append(jnp.concatenate([block.astype(jnp.bfloat16) for block in exps], axis=1))
        mean = jnp.dot(jnp.concatenate(weights, axis=0), x, preferred_element_type=jnp.float32)
        out_ref[...] = mean * (1.0 / jnp.concatenate(totals, axis=0))
        lse_ref[pl.ds(place * n_rows, n_rows), :] = to_dense(columns)


def source_bias(ls_ref, sqx_ref, parts):
    f_pot = sqx_ref[...] - merge_all([ref[...] for ref in parts])
    return ls_ref[...] * LOG2E + f_pot - sqx_ref[...]


def over_sources(tile_ref, at, bias):
    scores = [tile_ref[at, pl.ds(b * LANES, LANES)] + bias[b : b + 1, :] for b in range(bias.shape[0])]
    top = scores[0]
    for block in scores[1:]:
        top = jnp.maximum(top, block)
    peak = jnp.max(top, axis=1, keepdims=True)
    exps = [jnp.exp2(block - peak) for block in scores]
    return peak, jnp.sum(sum(exps), axis=1, keepdims=True), exps


def share_kernel(mine_ref, came_ref, total_ref, lse_ref, came_lse_ref, after_ref, out_ref):
    half = mine_ref.shape[0] // LANES
    at = pl.ds(lax.axis_index("row") % 2 * half, half)
    total = total_ref[at, :]
    share, came_share = to_column(jnp.exp2(lse_ref[at, :] - total)), to_column(jnp.exp2(came_lse_ref[at, :] - total))
    out_ref[...] = mine_ref[...] * share + came_ref[...] * came_share


def add_kernel(one_ref, two_ref, *out_refs):
    rows = out_refs[0].shape[0]
    for k, ref in enumerate(out_refs):
        at = pl.ds(k * rows, rows)
        ref[...] = one_ref[at, :] + two_ref[at, :]


def join_kernel(*refs):
    parts, out_ref = refs[:-1], refs[-1]
    rows = out_ref.shape[0]
    lses = [ref[rows : rows + pl.cdiv(rows, LANES), :LANES] for ref in parts]
    whole = merge_all(lses)
    shares = [to_column(jnp.exp2(lse - whole))[:rows] for lse in lses]
    out_ref[...] = sum(ref[:rows, :] * share for ref, share in zip(parts, shares))


def place_kernel(*refs):
    n = (len(refs) - 2) // 2
    mine, others, out_hbm, sems = refs[:n], refs[n : 2 * n], refs[-2], refs[-1]
    rows = mine[0].shape[0]
    core = lax.axis_index("row") % 2
    copies = []
    for place, pieces in ((core, mine), (1 - core, others)):
        for k, piece in enumerate(pieces):
            at = pl.ds(pl.multiple_of((place * n + k) * rows, rows), rows)
            copies.append(pltpu.make_async_copy(piece, out_hbm.at[at, :], sems.at[len(copies)]))
            copies[-1].start()
    for copy in copies:
        copy.wait()


def scores_kernel(near, x_ref, own_ref, mine_ref, other_ref, y_ref, inner_ref):
    rows = inner_ref.shape[0] // 2
    n_tgt = own_ref.shape[0]
    n_came, n_y, part, _ = mine_ref.shape
    col, core = lax.axis_index("col"), lax.axis_index("row") % 2
    y_ref[:n_tgt, :] = own_ref[...]
    for k in range(n_came):
        for ref, place in ((mine_ref, core), (other_ref, 1 - core)):
            for y in range(n_y):
                start = (k + 1) * n_tgt + (2 * y + place) * part
                y_ref[pl.ds(pl.multiple_of(start, part), part), :] = ref[k, y].astype(jnp.bfloat16)
    blocks = [x_ref[pl.ds(pl.multiple_of((col ^ flip) * rows, rows), rows), :] for flip in (0, near)]
    x = jnp.concatenate(blocks, axis=0)
    unit = scale(x.shape[1])
    for b in range(y_ref.shape[0] // n_tgt):
        at = pl.ds(b * n_tgt, n_tgt)
        inner_ref[:, at] = lax.dot_general(x, y_ref[at, :], NT_DIMS, preferred_element_type=jnp.float32) * (2.0 * unit)


EXTRA = 8


def images(flip, order, inner_ref, y_ref, biases_ref, scores_ref):
    rows = scores_ref.shape[0]
    n_shards = len(order)
    n_tgt = y_ref.shape[0] // n_shards
    block = pl.ds(flip * rows, rows)
    peak = jnp.full((rows, 1), -jnp.inf, jnp.float32)
    for k, place in enumerate(order):
        at = pl.ds(k * n_tgt, n_tgt)
        scores = inner_ref[block, at] + to_row(biases_ref[place])
        scores_ref[:, at] = scores
        peak = jnp.maximum(peak, jnp.max(scores, axis=1, keepdims=True))
    total = jnp.zeros((rows, 1), jnp.float32)
    numer = jnp.zeros((rows, y_ref.shape[1]), jnp.float32)
    for k in range(n_shards):
        at = pl.ds(k * n_tgt, n_tgt)
        plan = jnp.exp2(scores_ref[:, at] - peak)
        total = total + jnp.sum(plan, axis=1, keepdims=True)
        numer = numer + jnp.dot(plan.astype(jnp.bfloat16), y_ref[at, :], preferred_element_type=jnp.float32)
    return numer, total, peak


def lanes_of(column):
    rows = column.shape[0]
    if rows % LANES:
        column = jnp.concatenate([column, jnp.zeros((-rows % LANES, 1), jnp.float32)], axis=0)
    return to_dense([column[b : b + LANES] for b in range(0, column.shape[0], LANES)])


EXTRA = 8


def image_kernel(flip, order, inner_ref, y_ref, biases_ref, *refs):
    image_ref, scores_ref = refs[-2:]
    numer, total, peak = images(flip, order, inner_ref, y_ref, biases_ref, scores_ref)
    rows = numer.shape[0]
    lse = lanes_of(peak + jnp.log2(total))
    image_ref[:rows, :] = numer * (1.0 / total)
    image_ref[rows:, :] = jnp.zeros((EXTRA, image_ref.shape[1]), jnp.float32)
    image_ref[rows : rows + lse.shape[0], :LANES] = lse


def swap(value, axis, distance):
    n = lax.axis_size(axis)
    return lax.ppermute(value, axis, [(i, i ^ distance) for i in range(n)])


def bits_of(n):
    return [1 << b for b in range(n.bit_length() - 1)]


def on_device(source, target, log_source_mass, log_target_mass):
    n_src, width = source.shape
    n_tgt = target.shape[0]
    n_col, n_row = lax.axis_size("col"), lax.axis_size("row")
    count = n_src // n_col
    n_x = 1 << (len(bits_of(n_col)) // 2)
    n_z = n_col // n_x
    y_bits = bits_of(n_row)[1:]
    ls = log_source_mass.reshape(-1, LANES)
    lt = log_target_mass.reshape(-1, LANES)
    src_dense, tgt_dense = f32(*ls.shape), f32(*lt.shape)
    half = n_tgt // 2

    part = f32(n_tgt // n_row, width)
    pieces = {0: call(quarter_kernel, part, target)}
    for distance in [bit for bit in bits_of(n_col) if bit > n_x][::-1]:
        pieces |= {k ^ distance: swap(piece, "col", distance) for k, piece in pieces.items()}
    early = swap(pieces[0], "col", 1)

    def along_y(piece):
        held = [piece]
        for distance in y_bits:
            held += [swap(one, "row", distance) for one in held]
        return held

    tile, lse, sqy = call(first_kernel, (f32(n_tgt, n_src), src_dense, tgt_dense), target, source, lt)
    sqx = call(norms_kernel, src_dense, source)
    cut = early_rows(part.shape[0])
    for step in range(ITERS):
        if step > 0:
            apart = [0, 1] + [k for k in pieces if k > 1]
            lse, late = call(
                lambda *refs: targets_kernel(n_row, *refs),
                (src_dense, f32((len(apart) - 2) * part.shape[0] - cut, width)),
                tile, lt, sqy, *parts, *[pieces[k] for k in apart[2:]], early[-1],
            )
            late = along_y(late)
        if step > 0:
            for distance in bits_of(2 * n_x):
                lse = merge_all([lse, swap(lse, "col", distance)])
        else:
            near = [lse] + [swap(lse, "col", distance) for distance in range(2 * n_x - 1, 0, -1)]
            far = [k for k in pieces if k > 0]
            lse, early, *copies = call(
                lambda *refs: merge_kernel(2 * n_x, *refs),
                (src_dense, f32(part.shape[0] + cut, width), *(part,) * len(far)),
                *near, *[pieces[k] for k in far], early,
            )
            early = along_y(early)
            pieces |= dict(zip(far, copies))
            for bit in bits_of(n_x)[::-1]:
                pieces |= {k ^ bit: swap(piece, "col", bit) for k, piece in pieces.items() if k ^ bit != 1}
        for distance in [bit for bit in bits_of(n_col) if bit > n_x][:-1]:
            lse = merge_all([lse, swap(lse, "col", distance)])
        parts = [lse, swap(lse, "col", n_col // 2)]
        if step < ITERS - 1:
            lse = call(lambda *refs: sources_kernel(2, *refs), tgt_dense, tile, ls, sqx, *parts)
        else:
            lse, sent, mine, came = call(
                lambda *refs: last_sources_kernel(2, *refs),
                (tgt_dense, f32(half, width), f32(half, width), f32(len(apart) - 1, n_row // 2, *part.shape)),
                tile, source, ls, sqx, *parts, *early, *late,
            )
        parts = [lse] + [swap(lse, "row", k) for k in range(1, n_row)]
    total = merge_all(parts)

    bias = lt * LOG2E + (sqy - total) - sqy
    biases, held = bias[None], [0]
    for bit in [bit for bit in bits_of(n_col) if bit != n_x]:
        biases = jnp.concatenate([biases, swap(biases, "col", bit)], axis=0)
        held += [way ^ bit for way in held]
    order = [held.index(way) for way in apart]

    n_all = len(apart) * n_tgt
    all_y, inner = call(
        lambda *refs: scores_kernel(n_x, *refs),
        (bf16(n_all, width), f32(2 * count, n_all)),
        source, target, came, swap(came, "row", 1),
        limit=32,
    )

    mine = call(share_kernel, f32(half, width), mine, swap(sent, "row", 1), total, lse, parts[1], inner)
    rest = bits_of(n_row)[1:]
    for distance in rest[:-1]:
        mine, = call(add_kernel, (f32(half, width),), mine, swap(mine, "row", distance))
    mine_came = swap(mine, "row", rest[-1])

    def image(flip, *after):
        return call(
            lambda *refs: image_kernel(flip, order, *refs),
            f32(count + EXTRA, width),
            inner, all_y, biases, *after,
            scratch=[pltpu.VMEM((count, n_all), jnp.float32)],
        )

    came = swap(image(1), "col", n_x)
    n_last = 4
    mine = call(add_kernel, (f32(half // n_last, width),) * n_last, mine, mine_came)
    other = [swap(piece, "row", 1) for piece in mine]
    target_image = call(
        place_kernel, f32(n_tgt, width), *mine, *other,
        out_specs=HBM, scratch=[DMA((2 * n_last,))],
    )
    own = image(0, *other)
    source_image = call(join_kernel, f32(count, width), own, came)
    return source_image, target_image


def solution(mesh):
    in_specs = (P("row", None), P("col", None), P("row"), P("col"))
    out_specs = (P(("row", "col"), None), P("col", None))
    return jax.shard_map(
        on_device, mesh=mesh, in_specs=in_specs, out_specs=out_specs, check_vma=False
    )
```

```python
import math

import jax
import jax.numpy as jnp
from jax import lax
from jax.experimental import pallas as pl
from jax.experimental.pallas import tpu as pltpu
from jax.sharding import PartitionSpec as P

ITERS = 2
BLUR = 0.1
LOG2E = math.log2(math.e)
LANES = 128
NT_DIMS = (((1,), (1,)), ((), ()))
VMEM = pl.BlockSpec(memory_space=pltpu.VMEM)
HBM = pl.BlockSpec(memory_space=pltpu.HBM)
ANY = pl.BlockSpec(memory_space=pl.ANY)
DMA = pltpu.SemaphoreType.DMA


def call(kernel, out_shape, *args, in_specs=None, out_specs=None, scratch=(), limit=24):
    return pl.pallas_call(
        kernel,
        out_shape=out_shape,
        in_specs=in_specs or [VMEM] * len(args),
        out_specs=out_specs or jax.tree.map(lambda _: VMEM, out_shape),
        scratch_shapes=list(scratch),
        compiler_params=pltpu.CompilerParams(vmem_limit_bytes=limit << 20),
    )(*args)


def f32(*shape):
    return jax.ShapeDtypeStruct(shape, jnp.float32)


def bf16(*shape):
    return jax.ShapeDtypeStruct(shape, jnp.bfloat16)


def scale(width):
    return LOG2E / (width * BLUR)


def to_column(dense):
    n = dense.shape[0]
    square = jnp.concatenate([dense, jnp.zeros((LANES - n, LANES), jnp.float32)], axis=0).T
    return jnp.concatenate([square[:, b : b + 1] for b in range(n)], axis=0)


def to_dense(columns):
    lane = lax.broadcasted_iota(jnp.int32, (LANES, LANES), 1)
    square = jnp.zeros((LANES, LANES), jnp.float32)
    for b, column in enumerate(columns):
        square = jnp.where(lane == b, column, square)
    return square.T[: len(columns)]


def to_row(dense):
    return jnp.concatenate([dense[b : b + 1, :] for b in range(dense.shape[0])], axis=1)


def over_targets(scores):
    peak = jnp.max(scores, axis=0, keepdims=True)
    total = jnp.sum(jnp.exp2(scores - peak), axis=0, keepdims=True)
    return peak + jnp.log2(total)


def half_at(ref, place):
    half = ref.shape[0] // 2
    return ref[pl.ds(place * half, half), :]


def merge_all(parts):
    peak = parts[0]
    for part in parts[1:]:
        peak = jnp.maximum(peak, part)
    return peak + jnp.log2(sum(jnp.exp2(part - peak) for part in parts))


def norms(block):
    wide = block.astype(jnp.float32)
    return jnp.sum(wide * wide, axis=1, keepdims=True) * scale(block.shape[1])


def quarter_kernel(y_ref, out_ref):
    rows = out_ref.shape[0]
    out_ref[...] = y_ref[pl.ds(pl.multiple_of(lax.axis_index("row") * rows, rows), rows), :].astype(jnp.float32)


def norms_kernel(x_ref, sqx_ref):
    columns = [norms(x_ref[pl.ds(b, LANES), :]) for b in range(0, x_ref.shape[0], LANES)]
    sqx_ref[...] = to_dense(columns)


def first_kernel(y_ref, x_ref, lt_ref, tile_ref, lse_ref, sqy_ref):
    wide = 256
    y = y_ref[...]
    unit = scale(y.shape[1])
    sqy = norms(y)
    sqy_ref[...] = to_dense([sqy[b : b + LANES] for b in range(0, y.shape[0], LANES)])
    bias = to_column(lt_ref[...]) * LOG2E - sqy
    for b in range(x_ref.shape[0] // wide):
        at = pl.ds(b * wide, wide)
        x = x_ref[at, :]
        tile = lax.dot_general(y, x, NT_DIMS, preferred_element_type=jnp.float32) * (2.0 * unit)
        tile_ref[:, at] = tile
        row = over_targets(tile + bias)
        for c in range(wide // LANES):
            lse_ref[pl.ds(b * (wide // LANES) + c, 1), :] = row[:, c * LANES : (c + 1) * LANES]


def early_rows(rows):
    return rows // 2


def targets_kernel(n_parts, tile_ref, lt_ref, sqy_ref, *refs):
    parts, pieces, (lse_ref, pack_ref) = refs[:n_parts], refs[n_parts:-3], refs[-2:]
    rows = pieces[0].shape[0]
    cut = early_rows(rows)
    pack_ref[: rows - cut, :] = pieces[0][cut:, :]
    for k, piece in enumerate(pieces[1:], 1):
        pack_ref[pl.ds(rows * k - cut, rows), :] = piece[...]
    g_pot = sqy_ref[...] - merge_all([ref[...] for ref in parts])
    bias = to_column(lt_ref[...] * LOG2E + g_pot - sqy_ref[...])
    for b in range(tile_ref.shape[1] // LANES):
        lse_ref[pl.ds(b, 1), :] = over_targets(tile_ref[:, pl.ds(b * LANES, LANES)] + bias)


def merge_kernel(n_parts, *refs):
    parts, refs = refs[:n_parts], refs[n_parts:]
    n_pieces = len(refs) // 2
    pieces, (out_ref, pack_ref, *copies) = refs[:n_pieces], refs[n_pieces:]
    out_ref[...] = merge_all([ref[...] for ref in parts])
    rows = pieces[-1].shape[0]
    pack_ref[:rows, :] = pieces[-1][...]
    pack_ref[rows:, :] = pieces[0][: early_rows(rows), :]
    for piece, copy in zip(pieces[:-1], copies):
        copy[...] = piece[...]


def sources_kernel(n_parts, tile_ref, ls_ref, sqx_ref, *refs):
    bias = source_bias(ls_ref, sqx_ref, refs[:n_parts])
    columns = []
    for j in range(tile_ref.shape[0] // LANES):
        peak, total, _ = over_sources(tile_ref, pl.ds(j * LANES, LANES), bias)
        columns.append(peak + jnp.log2(total))
    refs[-1][...] = to_dense(columns)


def last_sources_kernel(n_parts, tile_ref, x_ref, ls_ref, sqx_ref, *refs):
    pieces, (lse_ref, sent_ref, mine_ref, pack_ref) = refs[n_parts:-4], refs[-4:]
    n_shards, n_y, rows, _ = pack_ref.shape
    y = lax.axis_index("row") // 2
    early, late = pieces[:n_y], pieces[n_y:]
    cut = early_rows(rows)
    for j in range(n_y):
        place = y ^ j
        pack_ref[0, place] = early[j][:rows, :]
        pack_ref[1, place, :cut, :] = early[j][rows:, :]
        pack_ref[1, place, cut:, :] = late[j][: rows - cut, :]
        for k in range(2, n_shards):
            pack_ref[k, place] = late[j][pl.ds((k - 1) * rows - cut, rows), :]
    bias = source_bias(ls_ref, sqx_ref, refs[:n_parts])
    x = x_ref[...]
    n_rows = mine_ref.shape[0] // LANES
    core = lax.axis_index("row") % 2
    for out_ref, place in ((sent_ref, 1 - core), (mine_ref, core)):
        columns, totals, weights = [], [], []
        for j in range(n_rows):
            at = pl.ds(pl.multiple_of((place * n_rows + j) * LANES, LANES), LANES)
            peak, total, exps = over_sources(tile_ref, at, bias)
            columns.append(peak + jnp.log2(total))
            totals.append(total)
            weights.append(jnp.concatenate([block.astype(jnp.bfloat16) for block in exps], axis=1))
        mean = jnp.dot(jnp.concatenate(weights, axis=0), x, preferred_element_type=jnp.float32)
        out_ref[...] = mean * (1.0 / jnp.concatenate(totals, axis=0))
        lse_ref[pl.ds(place * n_rows, n_rows), :] = to_dense(columns)


def source_bias(ls_ref, sqx_ref, parts):
    f_pot = sqx_ref[...] - merge_all([ref[...] for ref in parts])
    return ls_ref[...] * LOG2E + f_pot - sqx_ref[...]


def over_sources(tile_ref, at, bias):
    scores = [tile_ref[at, pl.ds(b * LANES, LANES)] + bias[b : b + 1, :] for b in range(bias.shape[0])]
    top = scores[0]
    for block in scores[1:]:
        top = jnp.maximum(top, block)
    peak = jnp.max(top, axis=1, keepdims=True)
    exps = [jnp.exp2(block - peak) for block in scores]
    return peak, jnp.sum(sum(exps), axis=1, keepdims=True), exps


def share_kernel(mine_ref, came_ref, total_ref, lse_ref, came_lse_ref, out_ref):
    half = mine_ref.shape[0] // LANES
    at = pl.ds(lax.axis_index("row") % 2 * half, half)
    total = total_ref[at, :]
    share, came_share = to_column(jnp.exp2(lse_ref[at, :] - total)), to_column(jnp.exp2(came_lse_ref[at, :] - total))
    out_ref[...] = mine_ref[...] * share + came_ref[...] * came_share


def add_kernel(one_ref, two_ref, *out_refs):
    rows = out_refs[0].shape[0]
    for k, ref in enumerate(out_refs):
        at = pl.ds(k * rows, rows)
        ref[...] = one_ref[at, :] + two_ref[at, :]


def join_kernel(*refs):
    parts, out_ref = refs[:-1], refs[-1]
    rows = out_ref.shape[0]
    lses = [ref[rows : rows + pl.cdiv(rows, LANES), :LANES] for ref in parts]
    whole = merge_all(lses)
    shares = [to_column(jnp.exp2(lse - whole))[:rows] for lse in lses]
    out_ref[...] = sum(ref[:rows, :] * share for ref, share in zip(parts, shares))


def place_kernel(*refs):
    n = (len(refs) - 2) // 2
    mine, others, out_hbm, sems = refs[:n], refs[n : 2 * n], refs[-2], refs[-1]
    rows = mine[0].shape[0]
    core = lax.axis_index("row") % 2
    copies = []
    for place, pieces in ((core, mine), (1 - core, others)):
        for k, piece in enumerate(pieces):
            at = pl.ds(pl.multiple_of((place * n + k) * rows, rows), rows)
            copies.append(pltpu.make_async_copy(piece, out_hbm.at[at, :], sems.at[len(copies)]))
            copies[-1].start()
    for copy in copies:
        copy.wait()


def scores_kernel(near, x_ref, own_ref, mine_ref, other_ref, y_ref, inner_ref):
    rows = inner_ref.shape[0] // 2
    n_tgt = own_ref.shape[0]
    n_came, n_y, part, _ = mine_ref.shape
    col, core = lax.axis_index("col"), lax.axis_index("row") % 2
    y_ref[:n_tgt, :] = own_ref[...]
    for k in range(n_came):
        for ref, place in ((mine_ref, core), (other_ref, 1 - core)):
            for y in range(n_y):
                start = (k + 1) * n_tgt + (2 * y + place) * part
                y_ref[pl.ds(pl.multiple_of(start, part), part), :] = ref[k, y].astype(jnp.bfloat16)
    blocks = [x_ref[pl.ds(pl.multiple_of((col ^ flip) * rows, rows), rows), :] for flip in (0, near)]
    x = jnp.concatenate(blocks, axis=0)
    unit = scale(x.shape[1])
    for b in range(y_ref.shape[0] // n_tgt):
        at = pl.ds(b * n_tgt, n_tgt)
        inner_ref[:, at] = lax.dot_general(x, y_ref[at, :], NT_DIMS, preferred_element_type=jnp.float32) * (2.0 * unit)


EXTRA = 8


def images(flip, inner_ref, y_ref, bias_refs, scores_ref):
    rows = scores_ref.shape[0]
    n_shards = len(bias_refs)
    n_tgt = y_ref.shape[0] // n_shards
    block = pl.ds(flip * rows, rows)
    peak = jnp.full((rows, 1), -jnp.inf, jnp.float32)
    for k, bias_ref in enumerate(bias_refs[::-1]):
        at = pl.ds(k * n_tgt, n_tgt)
        scores = inner_ref[block, at] + to_row(bias_ref[...])
        peak = jnp.maximum(peak, jnp.max(scores, axis=1, keepdims=True))
    total = jnp.zeros((rows, 1), jnp.float32)
    numer = jnp.zeros((rows, y_ref.shape[1]), jnp.float32)
    for k, bias_ref in enumerate(bias_refs[::-1]):
        at = pl.ds(k * n_tgt, n_tgt)
        plan = jnp.exp2(inner_ref[block, at] + to_row(bias_ref[...]) - peak)
        total = total + jnp.sum(plan, axis=1, keepdims=True)
        numer = numer + jnp.dot(plan.astype(jnp.bfloat16), y_ref[at, :], preferred_element_type=jnp.float32)
    return numer, total, peak


def lanes_of(column):
    rows = column.shape[0]
    if rows % LANES:
        column = jnp.concatenate([column, jnp.zeros((-rows % LANES, 1), jnp.float32)], axis=0)
    return to_dense([column[b : b + LANES] for b in range(0, column.shape[0], LANES)])


EXTRA = 8


def image_kernel(flip, inner_ref, y_ref, *refs):
    bias_refs, (image_ref, scores_ref) = refs[:-2], refs[-2:]
    numer, total, peak = images(flip, inner_ref, y_ref, bias_refs, scores_ref)
    rows = numer.shape[0]
    lse = lanes_of(peak + jnp.log2(total))
    image_ref[:rows, :] = numer * (1.0 / total)
    image_ref[rows:, :] = jnp.zeros((EXTRA, image_ref.shape[1]), jnp.float32)
    image_ref[rows : rows + lse.shape[0], :LANES] = lse


def swap(value, axis, distance):
    n = lax.axis_size(axis)
    return lax.ppermute(value, axis, [(i, i ^ distance) for i in range(n)])


def bits_of(n):
    return [1 << b for b in range(n.bit_length() - 1)]


def on_device(source, target, log_source_mass, log_target_mass):
    n_src, width = source.shape
    n_tgt = target.shape[0]
    n_col, n_row = lax.axis_size("col"), lax.axis_size("row")
    count = n_src // n_col
    n_x = 1 << (len(bits_of(n_col)) // 2)
    n_z = n_col // n_x
    y_bits = bits_of(n_row)[1:]
    ls = log_source_mass.reshape(-1, LANES)
    lt = log_target_mass.reshape(-1, LANES)
    src_dense, tgt_dense = f32(*ls.shape), f32(*lt.shape)
    half = n_tgt // 2

    part = f32(n_tgt // n_row, width)
    pieces = {0: call(quarter_kernel, part, target)}
    for distance in [bit for bit in bits_of(n_col) if bit > n_x][::-1]:
        pieces |= {k ^ distance: swap(piece, "col", distance) for k, piece in pieces.items()}
    early = swap(pieces[0], "col", 1)

    def along_y(piece):
        held = [piece]
        for distance in y_bits:
            held += [swap(one, "row", distance) for one in held]
        return held

    tile, lse, sqy = call(first_kernel, (f32(n_tgt, n_src), src_dense, tgt_dense), target, source, lt)
    sqx = call(norms_kernel, src_dense, source)
    cut = early_rows(part.shape[0])
    for step in range(ITERS):
        if step > 0:
            apart = [0, 1] + [k for k in pieces if k > 1]
            lse, late = call(
                lambda *refs: targets_kernel(n_row, *refs),
                (src_dense, f32((len(apart) - 2) * part.shape[0] - cut, width)),
                tile, lt, sqy, *parts, *[pieces[k] for k in apart[2:]], early[-1],
            )
            late = along_y(late)
        if step > 0:
            for distance in bits_of(2 * n_x):
                lse = merge_all([lse, swap(lse, "col", distance)])
        else:
            near = [lse] + [swap(lse, "col", distance) for distance in range(2 * n_x - 1, 0, -1)]
            far = [k for k in pieces if k > 0]
            lse, early, *copies = call(
                lambda *refs: merge_kernel(2 * n_x, *refs),
                (src_dense, f32(part.shape[0] + cut, width), *(part,) * len(far)),
                *near, *[pieces[k] for k in far], early,
            )
            early = along_y(early)
            pieces |= dict(zip(far, copies))
            for bit in bits_of(n_x)[::-1]:
                pieces |= {k ^ bit: swap(piece, "col", bit) for k, piece in pieces.items() if k ^ bit != 1}
        for distance in [bit for bit in bits_of(n_col) if bit > n_x][:-1]:
            lse = merge_all([lse, swap(lse, "col", distance)])
        parts = [lse, swap(lse, "col", n_col // 2)]
        if step < ITERS - 1:
            lse = call(lambda *refs: sources_kernel(2, *refs), tgt_dense, tile, ls, sqx, *parts)
        else:
            lse, sent, mine, came = call(
                lambda *refs: last_sources_kernel(2, *refs),
                (tgt_dense, f32(half, width), f32(half, width), f32(len(apart) - 1, n_row // 2, *part.shape)),
                tile, source, ls, sqx, *parts, *early, *late,
            )
        parts = [lse] + [swap(lse, "row", k) for k in range(1, n_row)]
    total = merge_all(parts)

    bias = lt * LOG2E + (sqy - total) - sqy
    biases = [bias] + [swap(bias, "col", distance) for distance in apart[1:]]

    mine = call(share_kernel, f32(half, width), mine, swap(sent, "row", 1), total, lse, parts[1])
    rest = bits_of(n_row)[1:]
    for distance in rest[:-1]:
        mine, = call(add_kernel, (f32(half, width),), mine, swap(mine, "row", distance))
    mine_came = swap(mine, "row", rest[-1])

    n_all = len(apart) * n_tgt
    all_y, inner = call(
        lambda *refs: scores_kernel(n_x, *refs),
        (bf16(n_all, width), f32(2 * count, n_all)),
        source, target, came, swap(came, "row", 1),
        limit=32,
    )

    def image(flip):
        return call(
            lambda *refs: image_kernel(flip, *refs),
            f32(count + EXTRA, width),
            inner, all_y, *biases[::-1],
            scratch=[pltpu.VMEM((count, n_all), jnp.float32)],
        )

    came = swap(image(1), "col", n_x)
    own = image(0)
    n_last = 4
    mine = call(add_kernel, (f32(half // n_last, width),) * n_last, mine, mine_came)
    target_image = call(
        place_kernel, f32(n_tgt, width), *mine, *[swap(piece, "row", 1) for piece in mine],
        out_specs=HBM, scratch=[DMA((2 * n_last,))],
    )
    source_image = call(join_kernel, f32(count, width), own, came)
    return source_image, target_image


def solution(mesh):
    in_specs = (P("row", None), P("col", None), P("row"), P("col"))
    out_specs = (P(("row", "col"), None), P("col", None))
    return jax.shard_map(
        on_device, mesh=mesh, in_specs=in_specs, out_specs=out_specs, check_vma=False
    )
```

```python
import math

import jax
import jax.numpy as jnp
from jax import lax
from jax.experimental import pallas as pl
from jax.experimental.pallas import tpu as pltpu
from jax.sharding import PartitionSpec as P

ITERS = 2
BLUR = 0.1
LOG2E = math.log2(math.e)
LANES = 128
NT_DIMS = (((1,), (1,)), ((), ()))
VMEM = pl.BlockSpec(memory_space=pltpu.VMEM)
HBM = pl.BlockSpec(memory_space=pltpu.HBM)
ANY = pl.BlockSpec(memory_space=pl.ANY)
DMA = pltpu.SemaphoreType.DMA


def call(kernel, out_shape, *args, in_specs=None, out_specs=None, scratch=(), limit=24):
    return pl.pallas_call(
        kernel,
        out_shape=out_shape,
        in_specs=in_specs or [VMEM] * len(args),
        out_specs=out_specs or jax.tree.map(lambda _: VMEM, out_shape),
        scratch_shapes=list(scratch),
        compiler_params=pltpu.CompilerParams(vmem_limit_bytes=limit << 20),
    )(*args)


def f32(*shape):
    return jax.ShapeDtypeStruct(shape, jnp.float32)


def bf16(*shape):
    return jax.ShapeDtypeStruct(shape, jnp.bfloat16)


def scale(width):
    return LOG2E / (width * BLUR)


def to_column(dense):
    n = dense.shape[0]
    square = jnp.concatenate([dense, jnp.zeros((LANES - n, LANES), jnp.float32)], axis=0).T
    return jnp.concatenate([square[:, b : b + 1] for b in range(n)], axis=0)


def to_dense(columns):
    lane = lax.broadcasted_iota(jnp.int32, (LANES, LANES), 1)
    square = jnp.zeros((LANES, LANES), jnp.float32)
    for b, column in enumerate(columns):
        square = jnp.where(lane == b, column, square)
    return square.T[: len(columns)]


def to_row(dense):
    return jnp.concatenate([dense[b : b + 1, :] for b in range(dense.shape[0])], axis=1)


def over_targets(scores):
    peak = jnp.max(scores, axis=0, keepdims=True)
    total = jnp.sum(jnp.exp2(scores - peak), axis=0, keepdims=True)
    return peak + jnp.log2(total)


def half_at(ref, place):
    half = ref.shape[0] // 2
    return ref[pl.ds(place * half, half), :]


def merge_all(parts):
    peak = parts[0]
    for part in parts[1:]:
        peak = jnp.maximum(peak, part)
    return peak + jnp.log2(sum(jnp.exp2(part - peak) for part in parts))


def norms(block):
    wide = block.astype(jnp.float32)
    return jnp.sum(wide * wide, axis=1, keepdims=True) * scale(block.shape[1])


def quarter_kernel(y_ref, out_ref):
    rows = out_ref.shape[0]
    out_ref[...] = y_ref[pl.ds(pl.multiple_of(lax.axis_index("row") * rows, rows), rows), :].astype(jnp.float32)


def norms_kernel(x_ref, sqx_ref):
    columns = [norms(x_ref[pl.ds(b, LANES), :]) for b in range(0, x_ref.shape[0], LANES)]
    sqx_ref[...] = to_dense(columns)


def first_kernel(y_ref, x_ref, lt_ref, tile_ref, lse_ref, sqy_ref):
    wide = 256
    y = y_ref[...]
    unit = scale(y.shape[1])
    sqy = norms(y)
    sqy_ref[...] = to_dense([sqy[b : b + LANES] for b in range(0, y.shape[0], LANES)])
    bias = to_column(lt_ref[...]) * LOG2E - sqy
    for b in range(x_ref.shape[0] // wide):
        at = pl.ds(b * wide, wide)
        x = x_ref[at, :]
        tile = lax.dot_general(y, x, NT_DIMS, preferred_element_type=jnp.float32) * (2.0 * unit)
        tile_ref[:, at] = tile
        row = over_targets(tile + bias)
        for c in range(wide // LANES):
            lse_ref[pl.ds(b * (wide // LANES) + c, 1), :] = row[:, c * LANES : (c + 1) * LANES]


def early_rows(rows):
    return rows // 2


def targets_kernel(n_parts, tile_ref, lt_ref, sqy_ref, *refs):
    parts, pieces, (lse_ref, pack_ref) = refs[:n_parts], refs[n_parts:-3], refs[-2:]
    rows = pieces[0].shape[0]
    cut = early_rows(rows)
    pack_ref[: rows - cut, :] = pieces[0][cut:, :]
    for k, piece in enumerate(pieces[1:], 1):
        pack_ref[pl.ds(rows * k - cut, rows), :] = piece[...]
    g_pot = sqy_ref[...] - merge_all([ref[...] for ref in parts])
    bias = to_column(lt_ref[...] * LOG2E + g_pot - sqy_ref[...])
    for b in range(tile_ref.shape[1] // LANES):
        lse_ref[pl.ds(b, 1), :] = over_targets(tile_ref[:, pl.ds(b * LANES, LANES)] + bias)


def merge_kernel(n_parts, *refs):
    parts, refs = refs[:n_parts], refs[n_parts:]
    n_pieces = len(refs) // 2
    pieces, (out_ref, pack_ref, *copies) = refs[:n_pieces], refs[n_pieces:]
    out_ref[...] = merge_all([ref[...] for ref in parts])
    rows = pieces[-1].shape[0]
    pack_ref[:rows, :] = pieces[-1][...]
    pack_ref[rows:, :] = pieces[0][: early_rows(rows), :]
    for piece, copy in zip(pieces[:-1], copies):
        copy[...] = piece[...]


def sources_kernel(n_parts, tile_ref, ls_ref, sqx_ref, *refs):
    bias = source_bias(ls_ref, sqx_ref, refs[:n_parts])
    columns = []
    for j in range(tile_ref.shape[0] // LANES):
        peak, total, _ = over_sources(tile_ref, pl.ds(j * LANES, LANES), bias)
        columns.append(peak + jnp.log2(total))
    refs[-1][...] = to_dense(columns)


def last_sources_kernel(n_parts, tile_ref, x_ref, ls_ref, sqx_ref, *refs):
    pieces, (lse_ref, sent_ref, mine_ref, pack_ref) = refs[n_parts:-4], refs[-4:]
    n_shards, n_y, rows, _ = pack_ref.shape
    y = lax.axis_index("row") // 2
    early, late = pieces[:n_y], pieces[n_y:]
    cut = early_rows(rows)
    for j in range(n_y):
        place = y ^ j
        pack_ref[0, place] = early[j][:rows, :]
        pack_ref[1, place, :cut, :] = early[j][rows:, :]
        pack_ref[1, place, cut:, :] = late[j][: rows - cut, :]
        for k in range(2, n_shards):
            pack_ref[k, place] = late[j][pl.ds((k - 1) * rows - cut, rows), :]
    bias = source_bias(ls_ref, sqx_ref, refs[:n_parts])
    x = x_ref[...]
    n_rows = mine_ref.shape[0] // LANES
    core = lax.axis_index("row") % 2
    for out_ref, place in ((sent_ref, 1 - core), (mine_ref, core)):
        columns = []
        for j in range(n_rows):
            at = pl.ds(pl.multiple_of((place * n_rows + j) * LANES, LANES), LANES)
            peak, total, exps = over_sources(tile_ref, at, bias)
            columns.append(peak + jnp.log2(total))
            weights = jnp.concatenate([block.astype(jnp.bfloat16) for block in exps], axis=1)
            mean = jnp.dot(weights, x, preferred_element_type=jnp.float32)
            out_ref[pl.ds(j * LANES, LANES), :] = mean * (1.0 / total)
        lse_ref[pl.ds(place * n_rows, n_rows), :] = to_dense(columns)


def source_bias(ls_ref, sqx_ref, parts):
    f_pot = sqx_ref[...] - merge_all([ref[...] for ref in parts])
    return ls_ref[...] * LOG2E + f_pot - sqx_ref[...]


def over_sources(tile_ref, at, bias):
    scores = [tile_ref[at, pl.ds(b * LANES, LANES)] + bias[b : b + 1, :] for b in range(bias.shape[0])]
    top = scores[0]
    for block in scores[1:]:
        top = jnp.maximum(top, block)
    peak = jnp.max(top, axis=1, keepdims=True)
    exps = [jnp.exp2(block - peak) for block in scores]
    return peak, jnp.sum(sum(exps), axis=1, keepdims=True), exps


def share_kernel(mine_ref, came_ref, total_ref, lse_ref, came_lse_ref, out_ref):
    half = mine_ref.shape[0] // LANES
    at = pl.ds(lax.axis_index("row") % 2 * half, half)
    total = total_ref[at, :]
    share, came_share = to_column(jnp.exp2(lse_ref[at, :] - total)), to_column(jnp.exp2(came_lse_ref[at, :] - total))
    out_ref[...] = mine_ref[...] * share + came_ref[...] * came_share


def add_kernel(one_ref, two_ref, *out_refs):
    rows = out_refs[0].shape[0]
    for k, ref in enumerate(out_refs):
        at = pl.ds(k * rows, rows)
        ref[...] = one_ref[at, :] + two_ref[at, :]


def join_kernel(*refs):
    parts, out_ref = refs[:-1], refs[-1]
    rows = out_ref.shape[0]
    lses = [ref[rows : rows + pl.cdiv(rows, LANES), :LANES] for ref in parts]
    whole = merge_all(lses)
    shares = [to_column(jnp.exp2(lse - whole))[:rows] for lse in lses]
    out_ref[...] = sum(ref[:rows, :] * share for ref, share in zip(parts, shares))


def place_kernel(*refs):
    n = (len(refs) - 2) // 2
    mine, others, out_hbm, sems = refs[:n], refs[n : 2 * n], refs[-2], refs[-1]
    rows = mine[0].shape[0]
    core = lax.axis_index("row") % 2
    copies = []
    for place, pieces in ((core, mine), (1 - core, others)):
        for k, piece in enumerate(pieces):
            at = pl.ds(pl.multiple_of((place * n + k) * rows, rows), rows)
            copies.append(pltpu.make_async_copy(piece, out_hbm.at[at, :], sems.at[len(copies)]))
            copies[-1].start()
    for copy in copies:
        copy.wait()


def scores_kernel(near, x_ref, own_ref, mine_ref, other_ref, y_ref, inner_ref):
    rows = inner_ref.shape[0] // 2
    n_tgt = own_ref.shape[0]
    n_came, n_y, part, _ = mine_ref.shape
    col, core = lax.axis_index("col"), lax.axis_index("row") % 2
    y_ref[:n_tgt, :] = own_ref[...]
    for k in range(n_came):
        for ref, place in ((mine_ref, core), (other_ref, 1 - core)):
            for y in range(n_y):
                start = (k + 1) * n_tgt + (2 * y + place) * part
                y_ref[pl.ds(pl.multiple_of(start, part), part), :] = ref[k, y].astype(jnp.bfloat16)
    blocks = [x_ref[pl.ds(pl.multiple_of((col ^ flip) * rows, rows), rows), :] for flip in (0, near)]
    x = jnp.concatenate(blocks, axis=0)
    unit = scale(x.shape[1])
    for b in range(y_ref.shape[0] // n_tgt):
        at = pl.ds(b * n_tgt, n_tgt)
        inner_ref[:, at] = lax.dot_general(x, y_ref[at, :], NT_DIMS, preferred_element_type=jnp.float32) * (2.0 * unit)


EXTRA = 8


def images(flip, inner_ref, y_ref, bias_refs, scores_ref):
    rows = scores_ref.shape[0]
    n_shards = len(bias_refs)
    n_tgt = y_ref.shape[0] // n_shards
    block = pl.ds(flip * rows, rows)
    peak = jnp.full((rows, 1), -jnp.inf, jnp.float32)
    for k, bias_ref in enumerate(bias_refs[::-1]):
        at = pl.ds(k * n_tgt, n_tgt)
        scores = inner_ref[block, at] + to_row(bias_ref[...])
        scores_ref[:, at] = scores
        peak = jnp.maximum(peak, jnp.max(scores, axis=1, keepdims=True))
    total = jnp.zeros((rows, 1), jnp.float32)
    numer = jnp.zeros((rows, y_ref.shape[1]), jnp.float32)
    for k in range(n_shards):
        at = pl.ds(k * n_tgt, n_tgt)
        plan = jnp.exp2(scores_ref[:, at] - peak)
        total = total + jnp.sum(plan, axis=1, keepdims=True)
        numer = numer + jnp.dot(plan.astype(jnp.bfloat16), y_ref[at, :], preferred_element_type=jnp.float32)
    return numer, total, peak


def lanes_of(column):
    rows = column.shape[0]
    if rows % LANES:
        column = jnp.concatenate([column, jnp.zeros((-rows % LANES, 1), jnp.float32)], axis=0)
    return to_dense([column[b : b + LANES] for b in range(0, column.shape[0], LANES)])


EXTRA = 8


def image_kernel(flip, inner_ref, y_ref, *refs):
    bias_refs, (image_ref, scores_ref) = refs[:-2], refs[-2:]
    numer, total, peak = images(flip, inner_ref, y_ref, bias_refs, scores_ref)
    rows = numer.shape[0]
    lse = lanes_of(peak + jnp.log2(total))
    image_ref[:rows, :] = numer * (1.0 / total)
    image_ref[rows:, :] = jnp.zeros((EXTRA, image_ref.shape[1]), jnp.float32)
    image_ref[rows : rows + lse.shape[0], :LANES] = lse


def swap(value, axis, distance):
    n = lax.axis_size(axis)
    return lax.ppermute(value, axis, [(i, i ^ distance) for i in range(n)])


def bits_of(n):
    return [1 << b for b in range(n.bit_length() - 1)]


def on_device(source, target, log_source_mass, log_target_mass):
    n_src, width = source.shape
    n_tgt = target.shape[0]
    n_col, n_row = lax.axis_size("col"), lax.axis_size("row")
    count = n_src // n_col
    n_x = 1 << (len(bits_of(n_col)) // 2)
    n_z = n_col // n_x
    y_bits = bits_of(n_row)[1:]
    ls = log_source_mass.reshape(-1, LANES)
    lt = log_target_mass.reshape(-1, LANES)
    src_dense, tgt_dense = f32(*ls.shape), f32(*lt.shape)
    half = n_tgt // 2

    part = f32(n_tgt // n_row, width)
    pieces = {0: call(quarter_kernel, part, target)}
    for distance in [bit for bit in bits_of(n_col) if bit > n_x][::-1]:
        pieces |= {k ^ distance: swap(piece, "col", distance) for k, piece in pieces.items()}
    early = swap(pieces[0], "col", 1)

    def along_y(piece):
        held = [piece]
        for distance in y_bits:
            held += [swap(one, "row", distance) for one in held]
        return held

    tile, lse, sqy = call(first_kernel, (f32(n_tgt, n_src), src_dense, tgt_dense), target, source, lt)
    sqx = call(norms_kernel, src_dense, source)
    cut = early_rows(part.shape[0])
    for step in range(ITERS):
        if step > 0:
            apart = [0, 1] + [k for k in pieces if k > 1]
            lse, late = call(
                lambda *refs: targets_kernel(n_row, *refs),
                (src_dense, f32((len(apart) - 2) * part.shape[0] - cut, width)),
                tile, lt, sqy, *parts, *[pieces[k] for k in apart[2:]], early[-1],
            )
            late = along_y(late)
        if step > 0:
            for distance in bits_of(2 * n_x):
                lse = merge_all([lse, swap(lse, "col", distance)])
        else:
            near = [lse] + [swap(lse, "col", distance) for distance in range(2 * n_x - 1, 0, -1)]
            far = [k for k in pieces if k > 0]
            lse, early, *copies = call(
                lambda *refs: merge_kernel(2 * n_x, *refs),
                (src_dense, f32(part.shape[0] + cut, width), *(part,) * len(far)),
                *near, *[pieces[k] for k in far], early,
            )
            early = along_y(early)
            pieces |= dict(zip(far, copies))
            for bit in bits_of(n_x)[::-1]:
                pieces |= {k ^ bit: swap(piece, "col", bit) for k, piece in pieces.items() if k ^ bit != 1}
        for distance in [bit for bit in bits_of(n_col) if bit > n_x][:-1]:
            lse = merge_all([lse, swap(lse, "col", distance)])
        parts = [lse, swap(lse, "col", n_col // 2)]
        if step < ITERS - 1:
            lse = call(lambda *refs: sources_kernel(2, *refs), tgt_dense, tile, ls, sqx, *parts)
        else:
            lse, sent, mine, came = call(
                lambda *refs: last_sources_kernel(2, *refs),
                (tgt_dense, f32(half, width), f32(half, width), f32(len(apart) - 1, n_row // 2, *part.shape)),
                tile, source, ls, sqx, *parts, *early, *late,
            )
        parts = [lse] + [swap(lse, "row", k) for k in range(1, n_row)]
    total = merge_all(parts)

    bias = lt * LOG2E + (sqy - total) - sqy
    biases = [bias] + [swap(bias, "col", distance) for distance in apart[1:]]

    mine = call(share_kernel, f32(half, width), mine, swap(sent, "row", 1), total, lse, parts[1])
    rest = bits_of(n_row)[1:]
    for distance in rest[:-1]:
        mine, = call(add_kernel, (f32(half, width),), mine, swap(mine, "row", distance))
    mine_came = swap(mine, "row", rest[-1])

    n_all = len(apart) * n_tgt
    all_y, inner = call(
        lambda *refs: scores_kernel(n_x, *refs),
        (bf16(n_all, width), f32(2 * count, n_all)),
        source, target, came, swap(came, "row", 1),
        limit=32,
    )

    def image(flip):
        return call(
            lambda *refs: image_kernel(flip, *refs),
            f32(count + EXTRA, width),
            inner, all_y, *biases[::-1],
            scratch=[pltpu.VMEM((count, n_all), jnp.float32)],
        )

    came = swap(image(1), "col", n_x)
    own = image(0)
    n_last = 4
    mine = call(add_kernel, (f32(half // n_last, width),) * n_last, mine, mine_came)
    target_image = call(
        place_kernel, f32(n_tgt, width), *mine, *[swap(piece, "row", 1) for piece in mine],
        out_specs=HBM, scratch=[DMA((2 * n_last,))],
    )
    source_image = call(join_kernel, f32(count, width), own, came)
    return source_image, target_image


def solution(mesh):
    in_specs = (P("row", None), P("col", None), P("row"), P("col"))
    out_specs = (P(("row", "col"), None), P("col", None))
    return jax.shard_map(
        on_device, mesh=mesh, in_specs=in_specs, out_specs=out_specs, check_vma=False
    )
```
